32 devices in a mesh: dp: 4 (over x, core), ctx: 8 (over z, y).
Axes of the slice: x: 2, y: 2, z: 4, core: 2. Of those that a mesh axis runs over, the one named last changes fastest.
Arguments:
- query: bfloat16 [4, 2048, 1024], P('dp', 'ctx'), may hold values from -150 to 150
- key: bfloat16 [4, 2048, 1024], P('dp', 'ctx'), may hold values from -3 to 3
- value: bfloat16 [4, 2048, 1024], P('dp', 'ctx'), may hold values from -6 to 6
- grad_out: bfloat16 [4, 2048, 1024], P('dp', 'ctx'), may hold values from -30 to 30
- clause: int32 [4, 2048], P('dp', 'ctx'), may hold values from 0 to 127, never falling along the last dimension, each value on 1 to 48 neighbouring positions
- bias_table: float32 [32, 2], replicated, may hold values from -1.5 to 1.5
Outputs:
- attended: bfloat16 [4, 2048, 1024], P('dp', 'ctx')
- query_gradient: bfloat16 [4, 2048, 1024], P('dp', 'ctx')
- key_gradient: bfloat16 [4, 2048, 1024], P('dp', 'ctx')
- value_gradient: bfloat16 [4, 2048, 1024], P('dp', 'ctx')
- bias_grad: float32 [32, 2], replicated
The draws below stay inside these ranges and needn't reach their ends.
Inputs may be any that keep to these rules, and one draw needn't show every extreme that they name: Clause ids never fall along a document; a clause holds 1 to 48 tokens, and some clause holds exactly 48.
All inputs are finite; a program needn't handle non-finite values.
Results may differ from the reference program's by a relative error of at most 0.009.
Values may be sent and summed in bfloat16 or wider, within the bound.
A program may use at most 128 MiB of HBM per device.

```python
import math
import jax
import jax.numpy as jnp
import numpy as np
from jax import lax

ROWS = 256
HEADS = 8
HEAD_DIM = 128
WINDOW = 512
BUCKETS = 32
DILATION_FIRST = 1
DILATION_SECOND = 8
DILATION_THIRD = 32
DOCS = 4
LENGTH = 2048
SEGMENT_FIRST = 2
SEGMENT_SECOND = 2
SEGMENT_THIRD = 8
CLAUSES = 128


def draw_key(key, part):
    shape = (DOCS, LENGTH, HEADS * HEAD_DIM)
    field = jnp.clip(jax.random.normal(jax.random.fold_in(key, 202), shape), -3.0, 3.0)
    return field.astype(jnp.bfloat16)


def draw_query(key, part):
    shape = (DOCS, LENGTH, HEADS * HEAD_DIM)
    values = jnp.clip(jax.random.normal(jax.random.fold_in(key, 404), shape), -4.0, 4.0)
    return values.astype(jnp.bfloat16)


def draw_grad_out(key, part):
    shape = (DOCS, LENGTH, HEADS * HEAD_DIM)
    base = jax.random.fold_in(key, 505)
    position = jnp.arange(LENGTH).astype(jnp.float32) / LENGTH
    rise = 3.0 ** position
    field = jnp.clip(jax.random.normal(jax.random.fold_in(base, 3), shape), -4.0, 4.0)
    return (field * rise[None, :, None]).astype(jnp.bfloat16)


def block_scale(key, shape, split, smallest, largest):
    def one(dim, blocks):
        draws = jax.random.uniform(jax.random.fold_in(jax.random.fold_in(key, 6), dim), (blocks,), jnp.float32, smallest / len(split), largest / len(split))
        return jnp.repeat(jnp.exp(draws), shape[dim] // blocks).reshape((-1,) + (1,) * (len(shape) - dim - 1))

    level = one(*split[0])
    for cut in split[1:]:
        level = level * one(*cut)
    return level


def profile(count, total, reach, slope):
    weights = [(1 << 20) // math.isqrt(grade ** slope) + 1 for grade in range(2, count + 1)]
    surplus, counts = total - reach - (count - 1), [1] * (count - 1)
    while surplus > 0:
        free = [i for i in range(count - 1) if counts[i] < reach]
        whole, left = sum([weights[i] for i in free]), surplus
        for i in free:
            addition = min(reach - counts[i], max(1, left * weights[i] // whole), surplus)
            counts[i] = counts[i] + addition
            surplus = surplus - addition
    return np.array([reach] + counts)


def ragged(key, number_of, total, limit, skew):
    if number_of == 2:
        one = jax.random.randint(key, (), max(1, total - limit), min(limit, total - 1) + 1)
        return jnp.stack([one, total - one])
    tallies = jnp.asarray(profile(number_of, total, limit, skew), jnp.int32)
    pairs = (number_of - 1) // 2
    donor, taker = tallies[1:1 + 2 * pairs:2], tallies[2:2 + 2 * pairs:2]
    margin = jnp.minimum(donor - 1, limit - taker)
    moved = jax.random.randint(jax.random.fold_in(key, 1), (pairs,), 0, 1 << 20) % (margin + 1)
    tallies = tallies.at[1:1 + 2 * pairs:2].set(donor - moved).at[2:2 + 2 * pairs:2].set(taker + moved)
    return tallies[jax.random.permutation(jax.random.fold_in(key, 2), number_of)]


def noise(rng, shape, spread, most, split=(), kind=jnp.bfloat16):
    entries = jax.random.normal(rng, shape, jnp.float32) * spread
    if len(split) > 0:
        entries = block_scale(rng, shape, split, -0.22, 0.18) * entries
    return jnp.clip(entries, min=-most, max=most).astype(kind)


def setup_inputs(seed: int = 0) -> dict:
    keys = jax.random.split(jax.random.key(seed), 7)
    query = draw_query(jax.random.fold_in(keys[6], 71), 0)
    key = draw_key(jax.random.fold_in(keys[6], 71), 0)
    value = noise(keys[2], (DOCS, LENGTH, HEADS * HEAD_DIM), 1.0, 6.0, ((0, 4), (1, 8)))
    grad_out = draw_grad_out(jax.random.fold_in(keys[6], 71), 0)
    clause = jax.vmap(lambda own: jnp.searchsorted(jnp.cumsum(ragged(own, CLAUSES, LENGTH, 48, 2)), jnp.arange(LENGTH), side="right"))(jax.random.split(keys[4], DOCS)).reshape((DOCS, LENGTH)).astype(jnp.int32)
    bias_table = jnp.clip(jax.random.uniform(keys[5], (BUCKETS, 2), jnp.float32, -1.5, 1.5), -1.5, 1.5)
    return {"query": query, "key": key, "value": value, "grad_out": grad_out, "clause": clause, "bias_table": bias_table}


def sample_rows(matrix, initial_flag, dilation_rate):
    count = matrix.shape[0] // dilation_rate
    head_dim = matrix.shape[1] // HEADS
    grid = matrix.reshape(count, dilation_rate, HEADS, head_dim)
    return jnp.stack([grid[:, 0, initial_flag], grid[:, dilation_rate // 2, initial_flag + 1]], axis=1)


def spread_rows(sampled, dilation_rate):
    count = sampled.shape[0]
    grid = jnp.zeros((count, dilation_rate) + sampled.shape[1:], sampled.dtype)
    grid = grid.at[:, 0, 0].set(sampled[:, 0]).at[:, dilation_rate // 2, 1].set(sampled[:, 1])
    return grid.reshape((count * dilation_rate,) + sampled.shape[1:])


def attend(score_matrix, query_matrix, incoming_keys, incoming_values, gradient_list, score_scale):
    top = jnp.max(score_matrix, axis=-1, keepdims=True)
    raised = jnp.exp(score_matrix - top)
    shares = raised / jnp.sum(raised, axis=-1, keepdims=True)
    softmax_weights = lax.optimization_barrier(shares.astype(jnp.bfloat16)).astype(jnp.float32)
    attended = jnp.einsum("ezb,beo->zeo", softmax_weights, incoming_values.astype(jnp.float32))
    weight_gradient = jnp.einsum("wvx,yvx->vwy", gradient_list.astype(jnp.float32), incoming_values.astype(jnp.float32))
    delta = jnp.sum(shares * weight_gradient, axis=-1, keepdims=True)
    logit_grads = shares * (weight_gradient - delta)
    score_gradient = lax.optimization_barrier(logit_grads.astype(jnp.bfloat16)).astype(jnp.float32)
    query_gradient = jnp.einsum("ezb,beo->zeo", score_gradient, incoming_keys.astype(jnp.float32)) * score_scale
    key_gradient = jnp.einsum("vjb,jvw->bvw", score_gradient, query_matrix.astype(jnp.float32)) * score_scale
    value_gradient = jnp.einsum("vjb,jvw->bvw", softmax_weights, gradient_list.astype(jnp.float32))
    return attended, query_gradient, key_gradient, value_gradient, logit_grads


def band_doc(query, key, value, grad_out, clause, table, score_scale):
    half = WINDOW // 2
    length = query.shape[0]
    head_dim = query.shape[1] // HEADS

    def heads(matrix):
        return matrix[:, :2 * head_dim].reshape(length, 2, head_dim)

    query_matrix, incoming_keys, incoming_values, gradient_list = heads(query), heads(key), heads(value), heads(grad_out)
    padded_keys = jnp.pad(incoming_keys, ((half, half), (0, 0), (0, 0)))
    padded_values = jnp.pad(incoming_values, ((half, half), (0, 0), (0, 0)))
    padded_clause = jnp.pad(clause, (half, half))

    def step(carry, block):
        key_running, value_running, bias_running = carry
        start = block * half
        query_block_rows = lax.dynamic_slice_in_dim(query_matrix, start, half, 0)
        block_grad = lax.dynamic_slice_in_dim(gradient_list, start, half, 0)
        block_clause = lax.dynamic_slice_in_dim(clause, start, half, 0)
        adjacent_keys = lax.dynamic_slice_in_dim(padded_keys, start, 3 * half, 0)
        near_values = lax.dynamic_slice_in_dim(padded_values, start, 3 * half, 0)
        near_clause = lax.dynamic_slice_in_dim(padded_clause, start, 3 * half, 0)
        query_pos = start + jnp.arange(half, dtype=jnp.int32)
        key_pos = start - half + jnp.arange(3 * half, dtype=jnp.int32)
        allowed = (jnp.abs(query_pos[:, None] - key_pos[None, :]) < half) & (key_pos[None, :] >= 0) & (key_pos[None, :] < length)
        bucket = jnp.minimum(jnp.abs(block_clause[:, None] - near_clause[None, :]), BUCKETS - 1)
        score_matrix = jnp.einsum("wvx,yvx->vwy", query_block_rows.astype(jnp.float32), adjacent_keys.astype(jnp.float32)) * score_scale
        score_matrix = score_matrix + jnp.moveaxis(table[bucket], -1, 0)
        score_matrix = jnp.where(allowed[None], score_matrix, -jnp.inf)
        attended, query_gradient, key_gradient, value_gradient, logit_grads = attend(score_matrix, query_block_rows, adjacent_keys, near_values, block_grad, score_scale)
        key_running = lax.dynamic_update_slice_in_dim(key_running, lax.dynamic_slice_in_dim(key_running, start, 3 * half, 0) + key_gradient, start, 0)
        value_running = lax.dynamic_update_slice_in_dim(value_running, lax.dynamic_slice_in_dim(value_running, start, 3 * half, 0) + value_gradient, start, 0)
        bias_running = bias_running + jax.ops.segment_sum(jnp.moveaxis(logit_grads, 0, -1).reshape(-1, 2), bucket.reshape(-1), num_segments=BUCKETS)
        return (key_running, value_running, bias_running), (attended, query_gradient)

    start_state = (jnp.zeros((length + 2 * half, 2, head_dim), jnp.float32), jnp.zeros((length + 2 * half, 2, head_dim), jnp.float32), jnp.zeros((BUCKETS, 2), jnp.float32))
    final, stacked = lax.scan(step, start_state, jnp.arange(length // half, dtype=jnp.int32))
    attended = stacked[0].reshape(length, 2, head_dim)
    query_gradient = stacked[1].reshape(length, 2, head_dim)
    return attended, query_gradient, final[0][half:half + length], final[1][half:half + length], final[2]


def dilated_doc(query, key, value, grad_out, initial_flag, dilation_rate, segment_width, score_scale):
    picked = [sample_rows(matrix, initial_flag, dilation_rate) for matrix in (query, key, value, grad_out)]
    count = picked[0].shape[0]
    per_segment = segment_width * ROWS // dilation_rate
    segments = count // per_segment
    grouped = tuple(matrix.reshape((segments, per_segment) + matrix.shape[1:]) for matrix in picked)

    def one(arrays):
        query_matrix, incoming_keys, incoming_values, gradient_list = arrays
        score_matrix = jnp.einsum("wvx,yvx->vwy", query_matrix.astype(jnp.float32), incoming_keys.astype(jnp.float32)) * score_scale
        result = attend(score_matrix, query_matrix, incoming_keys, incoming_values, gradient_list, score_scale)
        return result[0], result[1], result[2], result[3]

    results = lax.map(one, grouped)
    return [spread_rows(matrix.reshape((count,) + matrix.shape[2:]), dilation_rate) for matrix in results]


def reference(query, key, value, grad_out, clause, bias_table):
    score_scale = HEAD_DIM ** -0.5

    def document(arrays):
        doc_query, doc_key, doc_value, doc_grad, doc_clause = arrays
        band = band_doc(doc_query, doc_key, doc_value, doc_grad, doc_clause, bias_table, score_scale)
        pieces = [band[:4]]
        for initial_flag, dilation_rate, segment_width in ((2, DILATION_FIRST, SEGMENT_FIRST), (4, DILATION_SECOND, SEGMENT_SECOND), (6, DILATION_THIRD, SEGMENT_THIRD)):
            pieces.append(dilated_doc(doc_query, doc_key, doc_value, doc_grad, initial_flag, dilation_rate, segment_width, score_scale))
        length = doc_query.shape[0]
        joined = [jnp.concatenate([piece[slot] for piece in pieces], axis=1).reshape(length, -1).astype(jnp.bfloat16) for slot in range(4)]
        return joined[0], joined[1], joined[2], joined[3], band[4]

    outs = lax.map(document, (query, key, value, grad_out, clause))
    return outs[0], outs[1], outs[2], outs[3], jnp.sum(outs[4], axis=0)
```

```python
import jax
import jax.numpy as jnp
from jax import lax
from jax.experimental import pallas as pl
from jax.experimental.pallas import tpu as pltpu
from jax.sharding import PartitionSpec as P

HEADS = 8
WINDOW = 512
BUCKETS = 32
DILATION_FIRST = 1
DILATION_SECOND = 8
DILATION_THIRD = 32


def swapped(block, axis, bit):
    count = lax.axis_size(axis)
    route = []
    for low in range(count):
        high = low | 1 << bit
        if high != low and high < count:
            route += [(low, high), (high, low)]
    return lax.ppermute(block, axis, route)


def shifted(value, axis, steps):
    count = lax.axis_size(axis)
    leading, last = (max(0, -steps), min(count, count - steps))
    return lax.ppermute(value, axis, [(source, source + steps) for source in range(leading, last)])


def with_halo(shard, sides, width):
    for axis, dim in sides:
        size, length = (lax.axis_size(axis), shard.shape[dim])
        up = [(i, (i + 1) % size) for i in range(size - 1)]
        down = [(j, i) for i, j in up]
        last = lax.slice_in_dim(shard, length - width, length, axis=dim)
        leading = lax.slice_in_dim(shard, 0, width, axis=dim)
        before = lax.ppermute(last, axis, up)
        after = lax.ppermute(leading, axis, down)
        shard = jnp.concatenate([before, shard, after], axis=dim)
    return shard


def sample_rows(matrix, initial_flag, dilation_rate):
    count = matrix.shape[0] // dilation_rate
    head_dim = matrix.shape[1] // HEADS
    grid = matrix.reshape(count, dilation_rate, HEADS, head_dim)
    return jnp.concatenate(
        [grid[:, 0, initial_flag], grid[:, dilation_rate // 2, initial_flag + 1]], axis=1
    )


def spread_rows(sampled, dilation_rate):
    count = sampled.shape[0]
    grid = jnp.zeros((count, dilation_rate) + sampled.shape[1:], sampled.dtype)
    grid = grid.at[:, 0, 0].set(sampled[:, 0]).at[:, dilation_rate // 2, 1].set(sampled[:, 1])
    return grid.reshape((count * dilation_rate,) + sampled.shape[1:])


def upper_half(bit):
    index = lax.axis_index("ctx")
    return index // 2**bit % 2 == 1


def double_rows(block, bits):
    for bit in range(bits):
        other = swapped(block, "ctx", bit)
        block = jnp.where(
            upper_half(bit),
            jnp.concatenate([other, block], axis=0),
            jnp.concatenate([block, other], axis=0),
        )
    return block


def halve_sums(block, bits):
    for bit in reversed(range(bits)):
        half = block.shape[0] // 2
        lower, higher = (block[:half], block[half:])
        upper = upper_half(bit)
        outgoing = jnp.where(upper, lower, higher)
        staying = jnp.where(upper, higher, lower)
        block = staying + swapped(outgoing.astype(jnp.bfloat16), "ctx", bit).astype(outgoing.dtype)
    return block


def span_rows(block, bits):
    return double_rows(block, bits)


def span_sums(block, bits):
    return halve_sums(block, bits)


def rows_side(score_matrix, every_key_rows, every_value_rows, gradient_list, score_scale):
    top = jnp.max(score_matrix, axis=-1, keepdims=True)
    raised = jnp.exp(score_matrix - top)
    totals = jnp.sum(raised, axis=-1, keepdims=True)
    shares = raised / totals
    softmax_weights = shares.astype(jnp.bfloat16)
    attended = jnp.einsum(
        "ezb,beo->zeo", softmax_weights, every_value_rows, preferred_element_type=jnp.float32
    )
    weight_gradient = jnp.einsum(
        "wvx,yvx->vwy", gradient_list, every_value_rows, preferred_element_type=jnp.float32
    )
    delta = jnp.sum(shares * weight_gradient, axis=-1, keepdims=True)
    logit_grads = shares * (weight_gradient - delta)
    score_gradient = logit_grads.astype(jnp.bfloat16)
    query_gradient = (
        jnp.einsum(
            "ezb,beo->zeo", score_gradient, every_key_rows, preferred_element_type=jnp.float32
        )
        * score_scale
    )
    return (
        attended,
        query_gradient,
        softmax_weights,
        score_gradient,
        logit_grads,
        top,
        totals,
        delta,
    )


def keys_side(softmax_weights, score_gradient, query_matrix, gradient_list, score_scale):
    key_gradient = (
        jnp.einsum("vjb,jvw->bvw", score_gradient, query_matrix, preferred_element_type=jnp.float32)
        * score_scale
    )
    value_gradient = jnp.einsum(
        "vjb,jvw->bvw", softmax_weights, gradient_list, preferred_element_type=jnp.float32
    )
    return (key_gradient, value_gradient)


def bucket_lookup(bucket, table):
    running = jnp.zeros((table.shape[1],) + bucket.shape, jnp.float32)
    for level in range(BUCKETS):
        running = jnp.where(bucket[None] == level, table[level][:, None, None], running)
    return running


def bucket_sums(bucket, logit_grads):
    totals = [
        jnp.sum(jnp.where(bucket[None] == level, logit_grads, 0.0), axis=(1, 2))
        for level in range(BUCKETS)
    ]
    return jnp.stack(totals, axis=0)


def pass_rim(rim, offset):
    return shifted(rim.astype(jnp.bfloat16), "ctx", offset).astype(rim.dtype)


def band_part(query_rows, key_rows, value_rows, grad_rows, clause_rows, table, score_scale):
    rows, width = query_rows.shape
    head_dim = width // HEADS
    wide = 2 * head_dim
    half = WINDOW // 2
    pair_rows = jnp.concatenate([key_rows[:, :wide], value_rows[:, :wide]], axis=1)
    extended, extended_clause = (
        with_halo(pair_rows, (("ctx", 0),), half),
        with_halo(clause_rows, (("ctx", 0),), half),
    )
    reach = rows + 2 * half
    nearby_key_rows = extended[:, :wide].reshape(reach, 2, head_dim)
    values_near = extended[:, wide:].reshape(reach, 2, head_dim)
    query_matrix = query_rows[:, :wide].reshape(rows, 2, head_dim)
    gradient_list = grad_rows[:, :wide].reshape(rows, 2, head_dim)
    start = lax.axis_index("ctx") * rows
    length = rows * lax.axis_size("ctx")
    local_query = jnp.arange(rows)[:, None]
    local_key = jnp.arange(reach)[None, :] - half
    global_key = start + local_key
    allowed = (jnp.abs(local_query - local_key) < half) & (global_key >= 0) & (global_key < length)
    bucket = jnp.minimum(jnp.abs(clause_rows[:, None] - extended_clause[None, :]), BUCKETS - 1)
    score_matrix = (
        jnp.einsum(
            "wvx,yvx->vwy", query_matrix, nearby_key_rows, preferred_element_type=jnp.float32
        )
        * score_scale
    )
    score_matrix = jnp.where(allowed[None], score_matrix + bucket_lookup(bucket, table), -jnp.inf)
    attended, query_gradient, softmax_weights, score_gradient, logit_grads, top, totals, delta = (
        rows_side(score_matrix, nearby_key_rows, values_near, gradient_list, score_scale)
    )
    key_gradient, value_gradient = keys_side(
        softmax_weights, score_gradient, query_matrix, gradient_list, score_scale
    )
    sums = jnp.concatenate(
        [key_gradient.reshape(reach, wide), value_gradient.reshape(reach, wide)], axis=1
    )
    own = sums[half : half + rows]
    from_next = pass_rim(sums[:half], -1)
    from_prev = pass_rim(sums[half + rows :], 1)
    own = own.at[rows - half :].add(from_next).at[:half].add(from_prev)
    own_key = own[:, :wide].reshape(rows, 2, head_dim)
    own_value = own[:, wide:].reshape(rows, 2, head_dim)
    return (attended, query_gradient, own_key, own_value, bucket_sums(bucket, logit_grads))


def dilated(
    query_rows, key_rows, value_rows, grad_rows, initial_flag, dilation_rate, bits, score_scale
):
    head_dim = query_rows.shape[1] // HEADS
    wide = 2 * head_dim
    picked_query = sample_rows(query_rows, initial_flag, dilation_rate)
    picked_key = sample_rows(key_rows, initial_flag, dilation_rate)
    picked_value = sample_rows(value_rows, initial_flag, dilation_rate)
    picked_grad = sample_rows(grad_rows, initial_flag, dilation_rate)
    count = picked_query.shape[0]
    gathered = span_rows(jnp.concatenate([picked_key, picked_value], axis=1), bits)
    gathered_rows = gathered.shape[0]
    every_key_rows = gathered[:, :wide].reshape(gathered_rows, 2, head_dim)
    every_value_rows = gathered[:, wide:].reshape(gathered_rows, 2, head_dim)
    query_matrix = picked_query.reshape(count, 2, head_dim)
    gradient_list = picked_grad.reshape(count, 2, head_dim)
    score_matrix = (
        jnp.einsum("wvx,yvx->vwy", query_matrix, every_key_rows, preferred_element_type=jnp.float32)
        * score_scale
    )
    attended, query_gradient, softmax_weights, score_gradient, logit_grads, top, totals, delta = (
        rows_side(score_matrix, every_key_rows, every_value_rows, gradient_list, score_scale)
    )
    key_gradient, value_gradient = keys_side(
        softmax_weights, score_gradient, query_matrix, gradient_list, score_scale
    )
    partial_sums = jnp.concatenate(
        [key_gradient.reshape(gathered_rows, wide), value_gradient.reshape(gathered_rows, wide)],
        axis=1,
    )
    own = span_sums(partial_sums, bits)
    own_key = own[:, :wide].reshape(count, 2, head_dim)
    own_value = own[:, wide:].reshape(count, 2, head_dim)
    return (
        spread_rows(attended, dilation_rate),
        spread_rows(query_gradient, dilation_rate),
        spread_rows(own_key, dilation_rate),
        spread_rows(own_value, dilation_rate),
    )


def shards(query, key, value, grad_out, clause, bias_table):
    query_rows = query[0]
    key_rows = key[0]
    value_rows = value[0]
    grad_rows = grad_out[0]
    clause_rows = clause[0]
    rows, width = query_rows.shape
    head_dim = width // HEADS
    score_scale = head_dim ** (-0.5)
    bucket_bit_count = lax.axis_size("ctx").bit_length() - 1
    band = band_part(
        query_rows, key_rows, value_rows, grad_rows, clause_rows, bias_table, score_scale
    )
    pieces = [band[:4]]
    for initial_flag, dilation_rate, bits in (
        (2, DILATION_FIRST, max(bucket_bit_count - 5, 1)),
        (4, DILATION_SECOND, bucket_bit_count - 2),
        (6, DILATION_THIRD, bucket_bit_count),
    ):
        pieces.append(
            dilated(
                query_rows,
                key_rows,
                value_rows,
                grad_rows,
                initial_flag,
                dilation_rate,
                bits,
                score_scale,
            )
        )
    bias_grad = lax.psum(band[4], ("dp", "ctx"))
    joined = [
        jnp.concatenate([piece[slot] for piece in pieces], axis=1)
        .reshape(1, rows, width)
        .astype(jnp.bfloat16)
        for slot in range(4)
    ]
    return (joined[0], joined[1], joined[2], joined[3], bias_grad)


def general(mesh):
    in_specs = (
        P("dp", "ctx", None),
        P("dp", "ctx", None),
        P("dp", "ctx", None),
        P("dp", "ctx", None),
        P("dp", "ctx"),
        P(),
    )
    out_specs = (
        P("dp", "ctx", None),
        P("dp", "ctx", None),
        P("dp", "ctx", None),
        P("dp", "ctx", None),
        P(),
    )
    return jax.shard_map(shards, mesh=mesh, in_specs=in_specs, out_specs=out_specs, check_vma=False)


ROWS = 256
D = 128
BF = jnp.bfloat16
F32 = jnp.float32


def mm(a, b, dims):
    return lax.dot_general(a, b, (dims, ((), ())), preferred_element_type=F32)


def nt(a, b):
    return mm(a, b, ((1,), (1,)))


def nn(a, b):
    return mm(a, b, ((1,), (0,)))


def tn(a, b):
    return mm(a, b, ((0,), (0,)))


def halves(x):
    high = x.astype(BF)
    return high, (x - high.astype(F32)).astype(BF)


def softmax_grads(scores, q, k, v, g, scale):
    top = jnp.max(scores, axis=-1, keepdims=True)
    raised = jnp.exp(scores - top)
    shares = raised * (1.0 / jnp.sum(raised, axis=-1, keepdims=True))
    weights = shares.astype(BF)
    attended = nn(weights, v)
    weight_grads = nt(g, v)
    delta = jnp.sum(shares * weight_grads, axis=-1, keepdims=True)
    logit_grads = shares * (weight_grads - delta)
    score_grads = logit_grads.astype(BF)
    grad_q = nn(score_grads, k) * scale
    grad_k = tn(score_grads, q) * scale
    grad_v = tn(weights, g)
    return attended, grad_q, grad_k, grad_v, logit_grads


def selector(count, step, offset):
    row = lax.broadcasted_iota(jnp.int32, (count, ROWS), 0)
    col = lax.broadcasted_iota(jnp.int32, (count, ROWS), 1)
    return (col == row * step + offset).astype(BF)


def clause_column(row_form):
    whole = row_form[...].astype(jnp.int32)
    index = lax.broadcasted_iota(jnp.int32, whole.shape, 0)
    parts = jnp.where(index == 0, whole >> 6, jnp.where(index == 1, whole & 63, 0))
    line = lax.broadcasted_iota(jnp.int32, (8, D), 0)
    factor = jnp.where(line == 0, 64.0, jnp.where(line == 1, 1.0, 0.0))
    column = tn(parts.astype(F32).astype(BF), factor.astype(BF))
    return column.astype(jnp.int32)


def one_hot(column):
    lane = lax.broadcasted_iota(jnp.int32, (ROWS, D), 1)
    return (lane == (column & 127)).astype(F32).astype(BF)


def main_kernel(
    ctx_count, dp_count,
    table_ref, clause_ref, q_ref, k_ref, v_ref, g_ref,
    out_ref, second_ref, third_ref, bias_ref,
    pair_buf, halo_buf, halo_clause, pair_clause, grad_buf, grad_send, ret_send, ret_buf,
    s2, s3, bias_ctx, bias_dp,
    send_sem, recv_sem, s3_send, s3_recv, bc_send, bc_recv, bd_send, bd_recv,
):
    me = lax.axis_index("ctx")
    row = lax.axis_index("dp")
    c = lax.rem(me, 2)
    partner = me + 1 - 2 * c
    outward = me - 2 + 4 * c
    beyond = me + 2 - 4 * c
    has_out = (outward >= 0) & (outward < ctx_count)
    has_beyond = (beyond >= 0) & (beyond < ctx_count)
    scale = D**-0.5
    mesh_id = pl.DeviceIdType.MESH

    barrier = pltpu.get_barrier_semaphore()
    for step in range(1, ctx_count):
        pl.semaphore_signal(
            barrier, inc=1, device_id=(row, lax.rem(me + step, ctx_count)), device_id_type=mesh_id
        )
    for step in range(1, dp_count):
        pl.semaphore_signal(
            barrier, inc=1, device_id=(lax.rem(row + step, dp_count), me), device_id_type=mesh_id
        )
    pl.semaphore_wait(barrier, ctx_count + dp_count - 2)

    def remote(src, dst, index, target):
        return pltpu.make_async_remote_copy(
            src_ref=src,
            dst_ref=dst,
            send_sem=send_sem.at[index],
            recv_sem=recv_sem.at[index],
            device_id=(row, target),
            device_id_type=mesh_id,
        )

    def columns(head):
        return pl.ds(pl.multiple_of(head * D, D), D)

    inputs = (k_ref, v_ref, q_ref, g_ref)
    band_out = [
        remote(inputs[i].at[:, columns(1 - c)], pair_buf.at[i], i, partner) for i in range(4)
    ]
    first_out = [
        remote(inputs[i].at[:, columns(3 - c)], pair_buf.at[4 + i], 4 + i, partner)
        for i in range(4)
    ]
    clause_out = remote(clause_ref, pair_clause, 8, partner)
    own_halo = [
        remote(k_ref.at[:, columns(c)], halo_buf.at[1, 0], 9, outward),
        remote(v_ref.at[:, columns(c)], halo_buf.at[1, 1], 10, outward),
        remote(clause_ref, halo_clause.at[1], 11, outward),
    ]
    far_halo = [
        remote(pair_buf.at[0], halo_buf.at[0, 0], 12, beyond),
        remote(pair_buf.at[1], halo_buf.at[0, 1], 13, beyond),
        remote(pair_clause, halo_clause.at[0], 14, beyond),
    ]

    clause_out.start()
    for copy in band_out[:2]:
        copy.start()

    @pl.when(has_out)
    def _():
        for copy in own_halo:
            copy.start()

    for copy in band_out[2:]:
        copy.start()
    for copy in first_out:
        copy.start()

    for i, ref in enumerate((q_ref, k_ref, v_ref, g_ref)):
        for h in range(2):
            part = nn(selector(32, DILATION_SECOND, h * DILATION_SECOND // 2), ref[:, (4 + h) * D : (5 + h) * D])
            s2[0, :, (2 * i + h) * D : (2 * i + h + 1) * D] = part.astype(BF)

    def thirds(refs):
        return jnp.concatenate(
            [
                nn(selector(8, DILATION_THIRD, h * DILATION_THIRD // 2), ref[:, (6 + h) * D : (7 + h) * D])
                for ref in refs
                for h in range(2)
            ],
            axis=1,
        )

    s3[0] = jnp.concatenate([thirds((q_ref, k_ref)), thirds((v_ref, g_ref))], axis=0).astype(BF)
    second_out = remote(s2.at[0], s2.at[1], 15, partner)
    second_out.start()
    third_out = []
    for step in range(1, ctx_count):
        copy = pltpu.make_async_remote_copy(
            src_ref=s3.at[0],
            dst_ref=s3.at[ctx_count - step],
            send_sem=s3_send.at[step],
            recv_sem=s3_recv.at[ctx_count - step],
            device_id=(row, lax.rem(me + step, ctx_count)),
            device_id_type=mesh_id,
        )
        copy.start()
        third_out.append(copy)

    line = lax.broadcasted_iota(jnp.int32, (D, D), 0)
    lane = lax.broadcasted_iota(jnp.int32, (D, D), 1)
    apart = jnp.abs(((lane - line + 64) & 127) - 64)
    table = jnp.zeros((D, D), F32)
    for level in range(BUCKETS):
        table = jnp.where(apart == level, table_ref[level, c], table)
    far_bias = table_ref[BUCKETS - 1, c]
    table_high, table_low = halves(table)

    clause_out.wait_recv()
    band_out[0].wait_recv()
    band_out[1].wait_recv()

    @pl.when(has_beyond)
    def _():
        for copy in far_halo:
            copy.start()

    @pl.when(jnp.logical_not(has_out))
    def _():
        halo_buf[0] = jnp.zeros((2, ROWS, D), BF)
        halo_clause[0] = jnp.zeros((8, ROWS), jnp.int32)

    @pl.when(jnp.logical_not(has_beyond))
    def _():
        halo_buf[1] = jnp.zeros((2, ROWS, D), BF)
        halo_clause[1] = jnp.zeros((8, ROWS), jnp.int32)

    band_out[2].wait_recv()
    band_out[3].wait_recv()

    own = [ref[:, columns(c)] for ref in inputs]
    other = [pair_buf[i] for i in range(4)]
    clauses = {"own": clause_ref, "other": pair_clause}
    cols = {name: clause_column(ref) for name, ref in clauses.items()}
    hots = {name: one_hot(col) for name, col in cols.items()}
    line = lax.broadcasted_iota(jnp.int32, (ROWS, ROWS), 0)
    lane = lax.broadcasted_iota(jnp.int32, (ROWS, ROWS), 1)
    diff = (line - lane) * (1 - 2 * c)

    def band_block(slot, mine, near, mine_name, near_name, sign, halo_valid):
        k = jnp.concatenate([mine[0], near[0], halo_buf[slot, 0]], axis=0)
        v = jnp.concatenate([mine[1], near[1], halo_buf[slot, 1]], axis=0)
        q, g = mine[2], mine[3]
        halo_hot = one_hot(clause_column(halo_clause.at[slot]))
        key_hot = jnp.concatenate([hots[mine_name], hots[near_name], halo_hot], axis=0)
        key_row = jnp.concatenate(
            [clauses[mine_name][0:1, :], clauses[near_name][0:1, :], halo_clause[slot, 0:1, :]],
            axis=1,
        )
        query_hot = hots[mine_name]
        close = jnp.abs(cols[mine_name][:, 0:1] - key_row) < BUCKETS - 1
        spread = jnp.concatenate(
            [nn(query_hot, table_high).astype(BF), nn(query_hot, table_low).astype(BF)], axis=1
        )
        bias = nt(spread, jnp.concatenate([key_hot, key_hot], axis=1))
        signed = diff * sign
        reach = jnp.where(halo_valid, 0, ROWS)
        allowed = jnp.concatenate(
            [jnp.ones((ROWS, ROWS), jnp.int32), jnp.where(signed > 0, 1, 0), jnp.where(-signed > reach, 1, 0)],
            axis=1,
        )
        scores = nt(q, k) * scale + jnp.where(close, bias, far_bias)
        scores = jnp.where(allowed > 0, scores, -jnp.inf)
        attended, grad_q, grad_k, grad_v, logit_grads = softmax_grads(scores, q, k, v, g, scale)
        kept = jnp.where(close, logit_grads, 0.0)
        rest = jnp.sum(jnp.where(close, 0.0, logit_grads), axis=0, keepdims=True)
        high, low = halves(kept)
        by_clause = nn(high, key_hot) + nn(low, key_hot)
        high, low = halves(by_clause)
        pairs = tn(query_hot, high) + tn(query_hot, low) + tn(high, query_hot) + tn(low, query_hot)
        return attended, grad_q, grad_k, grad_v, pairs, rest

    @pl.when(has_out)
    def _():
        for copy in far_halo:
            copy.wait_recv()

    attended, grad_q, gk_a, gv_a, pairs_a, rest_a = band_block(
        0, own, other, "own", "other", 1, has_out
    )
    out_ref[0, c] = attended.astype(BF)
    out_ref[1, c] = grad_q.astype(BF)
    grad_send[0, 0] = gk_a[2 * ROWS :].astype(BF)
    grad_send[0, 1] = gv_a[2 * ROWS :].astype(BF)
    back_out = remote(grad_send.at[0], grad_buf.at[0], 16, outward)
    back_far = remote(grad_send.at[1], grad_buf.at[1], 17, beyond)

    @pl.when(has_out)
    def _():
        back_out.start()

    @pl.when(has_beyond)
    def _():
        for copy in own_halo:
            copy.wait_recv()

    attended, grad_q, gk_b, gv_b, pairs_b, rest_b = band_block(
        1, other, own, "other", "own", -1, has_beyond
    )
    ret = [remote(ret_send.at[i], ret_buf.at[i], 18 + i, partner) for i in range(8)]
    ret_send[0] = attended.astype(BF)
    ret_send[1] = grad_q.astype(BF)
    grad_send[1, 0] = gk_b[2 * ROWS :].astype(BF)
    grad_send[1, 1] = gv_b[2 * ROWS :].astype(BF)

    @pl.when(has_beyond)
    def _():
        back_far.start()

    ret[0].start()
    ret[1].start()
    own_gk = gk_a[:ROWS] + gk_b[ROWS : 2 * ROWS]
    own_gv = gv_a[:ROWS] + gv_b[ROWS : 2 * ROWS]
    other_gk = gk_b[:ROWS] + gk_a[ROWS : 2 * ROWS]
    other_gv = gv_b[:ROWS] + gv_a[ROWS : 2 * ROWS]

    turned = pairs_a + pairs_b
    line = lax.broadcasted_iota(jnp.int32, (D, D), 0)
    for bit in range(7):
        shift = 1 << bit
        rolled = jnp.concatenate([turned[:, shift:], turned[:, :shift]], axis=1)
        turned = jnp.where((line & shift) > 0, rolled, turned)
    sums = jnp.sum(turned, axis=0, keepdims=True)
    rest = jnp.sum(rest_a + rest_b, axis=1, keepdims=True)
    lane = lax.broadcasted_iota(jnp.int32, (1, D), 1)
    sums = jnp.where(lane == 0, 0.5 * sums, sums)
    sums = jnp.where(lane < BUCKETS - 1, sums, jnp.where(lane == BUCKETS - 1, rest, 0.0))
    tile_line = lax.broadcasted_iota(jnp.int32, (8, D), 0)
    bias_ctx[me] = jnp.where(tile_line == c, sums, 0.0)
    bias_out = []
    for step in range(1, ctx_count):
        copy = pltpu.make_async_remote_copy(
            src_ref=bias_ctx.at[me],
            dst_ref=bias_ctx.at[me],
            send_sem=bc_send.at[step],
            recv_sem=bc_recv.at[step],
            device_id=(row, lax.rem(me + step, ctx_count)),
            device_id_type=mesh_id,
        )
        copy.start()
        bias_out.append(copy)

    for copy in first_out:
        copy.wait_recv()
    k, v, q, g = [
        jnp.concatenate([inputs[i][:, columns(2 + c)], pair_buf[4 + i]], axis=0) for i in range(4)
    ]
    results = softmax_grads(nt(q, k) * scale, q, k, v, g, scale)[:4]
    for i in range(4):
        out_ref[4 + i, c] = results[i][:ROWS].astype(BF)
        ret_send[4 + i] = results[i][ROWS:].astype(BF)
        ret[4 + i].start()

    @pl.when(has_beyond)
    def _():
        back_out.wait_recv()

    @pl.when(has_out)
    def _():
        back_far.wait_recv()

    from_beyond = jnp.where(has_beyond, 1.0, 0.0)
    from_out = jnp.where(has_out, 1.0, 0.0)

    @pl.when(jnp.logical_not(has_beyond))
    def _():
        grad_buf[0] = jnp.zeros((2, ROWS, D), BF)

    @pl.when(jnp.logical_not(has_out))
    def _():
        grad_buf[1] = jnp.zeros((2, ROWS, D), BF)

    ret_send[2] = (other_gk + grad_buf[0, 0].astype(F32)).astype(BF)
    ret_send[3] = (other_gv + grad_buf[0, 1].astype(F32)).astype(BF)
    ret[2].start()
    ret[3].start()
    out_ref[2, c] = (own_gk + grad_buf[1, 0].astype(F32)).astype(BF)
    out_ref[3, c] = (own_gv + grad_buf[1, 1].astype(F32)).astype(BF)

    for copy in bias_out:
        copy.wait_recv()
    total = bias_ctx[0]
    for i in range(1, ctx_count):
        total = total + bias_ctx[i]
    bias_dp[row] = total
    docs_out = []
    for step in range(1, dp_count):
        copy = pltpu.make_async_remote_copy(
            src_ref=bias_dp.at[row],
            dst_ref=bias_dp.at[row],
            send_sem=bd_send.at[step],
            recv_sem=bd_recv.at[step],
            device_id=(lax.rem(row + step, dp_count), me),
            device_id_type=mesh_id,
        )
        copy.start()
        docs_out.append(copy)

    second_out.wait_recv()
    both = jnp.concatenate([s2[0], s2[1]], axis=0)
    for h in range(2):
        q, k, v, g = [both[:, (2 * i + h) * D : (2 * i + h + 1) * D] for i in range(4)]
        results = softmax_grads(nt(q, k) * scale, q, k, v, g, scale)[:4]
        for i in range(4):
            second_ref[i, :, h * D : (h + 1) * D] = results[i][:32]

    for copy in third_out:
        copy.wait_recv()
    blocks = [s3[i].astype(F32) for i in range(ctx_count)]
    upper = jnp.concatenate([block[:8] for block in blocks], axis=0).astype(BF)
    lower = jnp.concatenate([block[8:] for block in blocks], axis=0).astype(BF)
    for h in range(2):
        q, k = [upper[:, (2 * i + h) * D : (2 * i + h + 1) * D] for i in range(2)]
        v, g = [lower[:, (2 * i + h) * D : (2 * i + h + 1) * D] for i in range(2)]
        results = softmax_grads(nt(q, k) * scale, q, k, v, g, scale)[:4]
        for i in range(4):
            third_ref[i, :, h * D : (h + 1) * D] = results[i][:8]

    for copy in docs_out:
        copy.wait_recv()
    total = bias_dp[0]
    for i in range(1, dp_count):
        total = total + bias_dp[i]
    bias_ref[...] = total

    for i in (4, 5, 6, 7, 0, 1, 2, 3):
        ret[i].wait_recv()
        out_ref[i, 1 - c] = ret_buf[i]

    for copy in band_out + first_out + [clause_out, second_out] + third_out + bias_out + docs_out + ret:
        copy.wait_send()

    @pl.when(has_out)
    def _():
        for copy in own_halo + [back_out]:
            copy.wait_send()

    @pl.when(has_beyond)
    def _():
        for copy in far_halo + [back_far]:
            copy.wait_send()


def layout_kernel(heads_ref, second_ref, third_ref, *outs):
    for i, out in enumerate(outs):
        for h in range(2):
            out[:, h * D : (h + 1) * D] = heads_ref[i, h]
            out[:, (2 + h) * D : (3 + h) * D] = heads_ref[4 + i, h]
            seconds = second_ref[i, :, h * D : (h + 1) * D].astype(BF)
            spread = tn(selector(32, DILATION_SECOND, h * DILATION_SECOND // 2), seconds)
            out[:, (4 + h) * D : (5 + h) * D] = spread.astype(BF)
            thirds = third_ref[i, :, h * D : (h + 1) * D].astype(BF)
            spread = tn(selector(8, DILATION_THIRD, h * DILATION_THIRD // 2), thirds)
            out[:, (6 + h) * D : (7 + h) * D] = spread.astype(BF)


def paired(ctx_count, dp_count, query, key, value, grad_out, clause, bias_table):
    vmem = pl.BlockSpec(memory_space=pltpu.VMEM)
    smem = pl.BlockSpec(memory_space=pltpu.SMEM)
    rows = jnp.broadcast_to(clause, (8, ROWS))
    dma = pltpu.SemaphoreType.DMA
    block = (ROWS, D)
    heads, second, third, bias = pl.pallas_call(
        lambda *refs: main_kernel(ctx_count, dp_count, *refs),
        out_shape=[
            jax.ShapeDtypeStruct((8, 2) + block, BF),
            jax.ShapeDtypeStruct((4, 32, 2 * D), F32),
            jax.ShapeDtypeStruct((4, 8, 2 * D), F32),
            jax.ShapeDtypeStruct((8, D), F32),
        ],
        in_specs=[smem] + [vmem] * 5,
        out_specs=[vmem] * 4,
        scratch_shapes=[
            pltpu.VMEM((8,) + block, BF),
            pltpu.VMEM((2, 2) + block, BF),
            pltpu.VMEM((2, 8, ROWS), jnp.int32),
            pltpu.VMEM((8, ROWS), jnp.int32),
            pltpu.VMEM((2, 2) + block, BF),
            pltpu.VMEM((2, 2) + block, BF),
            pltpu.VMEM((8,) + block, BF),
            pltpu.VMEM((8,) + block, BF),
            pltpu.VMEM((2, 32, 8 * D), BF),
            pltpu.VMEM((ctx_count, 16, 4 * D), BF),
            pltpu.VMEM((ctx_count, 8, D), F32),
            pltpu.VMEM((dp_count, 8, D), F32),
            dma((26,)),
            dma((26,)),
            dma((ctx_count,)),
            dma((ctx_count,)),
            dma((ctx_count,)),
            dma((ctx_count,)),
            dma((dp_count,)),
            dma((dp_count,)),
        ],
        compiler_params=pltpu.CompilerParams(
            collective_id=0, has_side_effects=True, vmem_limit_bytes=48 * 1024 * 1024
        ),
        name="attend",
    )(bias_table, rows, query[0], key[0], value[0], grad_out[0])
    outs = pl.pallas_call(
        layout_kernel,
        out_shape=[jax.ShapeDtypeStruct((ROWS, HEADS * D), BF)] * 4,
        in_specs=[vmem] * 3,
        out_specs=[vmem] * 4,
        compiler_params=pltpu.CompilerParams(vmem_limit_bytes=32 * 1024 * 1024),
        name="layout",
    )(heads, second, third)
    return tuple(out[None] for out in outs) + (bias[:2, :BUCKETS].T,)


def solution(mesh):
    ctx_count, dp_count = mesh.shape["ctx"], mesh.shape["dp"]
    if ctx_count != 8:
        return general(mesh)
    spec = P("dp", "ctx", None)

    def body(*arrays):
        return paired(ctx_count, dp_count, *arrays)

    return jax.shard_map(
        body,
        mesh=mesh,
        in_specs=(spec, spec, spec, spec, P("dp", "ctx"), P()),
        out_specs=(spec, spec, spec, spec, P()),
        check_vma=False,
    )
```

```python
import jax
import jax.numpy as jnp
from jax import lax
from jax.experimental import pallas as pl
from jax.experimental.pallas import tpu as pltpu
from jax.sharding import PartitionSpec as P

HEADS = 8
WINDOW = 512
BUCKETS = 32
DILATION_FIRST = 1
DILATION_SECOND = 8
DILATION_THIRD = 32


def swapped(block, axis, bit):
    count = lax.axis_size(axis)
    route = []
    for low in range(count):
        high = low | 1 << bit
        if high != low and high < count:
            route += [(low, high), (high, low)]
    return lax.ppermute(block, axis, route)


def shifted(value, axis, steps):
    count = lax.axis_size(axis)
    leading, last = (max(0, -steps), min(count, count - steps))
    return lax.ppermute(value, axis, [(source, source + steps) for source in range(leading, last)])


def with_halo(shard, sides, width):
    for axis, dim in sides:
        size, length = (lax.axis_size(axis), shard.shape[dim])
        up = [(i, (i + 1) % size) for i in range(size - 1)]
        down = [(j, i) for i, j in up]
        last = lax.slice_in_dim(shard, length - width, length, axis=dim)
        leading = lax.slice_in_dim(shard, 0, width, axis=dim)
        before = lax.ppermute(last, axis, up)
        after = lax.ppermute(leading, axis, down)
        shard = jnp.concatenate([before, shard, after], axis=dim)
    return shard


def sample_rows(matrix, initial_flag, dilation_rate):
    count = matrix.shape[0] // dilation_rate
    head_dim = matrix.shape[1] // HEADS
    grid = matrix.reshape(count, dilation_rate, HEADS, head_dim)
    return jnp.concatenate(
        [grid[:, 0, initial_flag], grid[:, dilation_rate // 2, initial_flag + 1]], axis=1
    )


def spread_rows(sampled, dilation_rate):
    count = sampled.shape[0]
    grid = jnp.zeros((count, dilation_rate) + sampled.shape[1:], sampled.dtype)
    grid = grid.at[:, 0, 0].set(sampled[:, 0]).at[:, dilation_rate // 2, 1].set(sampled[:, 1])
    return grid.reshape((count * dilation_rate,) + sampled.shape[1:])


def upper_half(bit):
    index = lax.axis_index("ctx")
    return index // 2**bit % 2 == 1


def double_rows(block, bits):
    for bit in range(bits):
        other = swapped(block, "ctx", bit)
        block = jnp.where(
            upper_half(bit),
            jnp.concatenate([other, block], axis=0),
            jnp.concatenate([block, other], axis=0),
        )
    return block


def halve_sums(block, bits):
    for bit in reversed(range(bits)):
        half = block.shape[0] // 2
        lower, higher = (block[:half], block[half:])
        upper = upper_half(bit)
        outgoing = jnp.where(upper, lower, higher)
        staying = jnp.where(upper, higher, lower)
        block = staying + swapped(outgoing.astype(jnp.bfloat16), "ctx", bit).astype(outgoing.dtype)
    return block


def span_rows(block, bits):
    return double_rows(block, bits)


def span_sums(block, bits):
    return halve_sums(block, bits)


def rows_side(score_matrix, every_key_rows, every_value_rows, gradient_list, score_scale):
    top = jnp.max(score_matrix, axis=-1, keepdims=True)
    raised = jnp.exp(score_matrix - top)
    totals = jnp.sum(raised, axis=-1, keepdims=True)
    shares = raised / totals
    softmax_weights = shares.astype(jnp.bfloat16)
    attended = jnp.einsum(
        "ezb,beo->zeo", softmax_weights, every_value_rows, preferred_element_type=jnp.float32
    )
    weight_gradient = jnp.einsum(
        "wvx,yvx->vwy", gradient_list, every_value_rows, preferred_element_type=jnp.float32
    )
    delta = jnp.sum(shares * weight_gradient, axis=-1, keepdims=True)
    logit_grads = shares * (weight_gradient - delta)
    score_gradient = logit_grads.astype(jnp.bfloat16)
    query_gradient = (
        jnp.einsum(
            "ezb,beo->zeo", score_gradient, every_key_rows, preferred_element_type=jnp.float32
        )
        * score_scale
    )
    return (
        attended,
        query_gradient,
        softmax_weights,
        score_gradient,
        logit_grads,
        top,
        totals,
        delta,
    )


def keys_side(softmax_weights, score_gradient, query_matrix, gradient_list, score_scale):
    key_gradient = (
        jnp.einsum("vjb,jvw->bvw", score_gradient, query_matrix, preferred_element_type=jnp.float32)
        * score_scale
    )
    value_gradient = jnp.einsum(
        "vjb,jvw->bvw", softmax_weights, gradient_list, preferred_element_type=jnp.float32
    )
    return (key_gradient, value_gradient)


def bucket_lookup(bucket, table):
    running = jnp.zeros((table.shape[1],) + bucket.shape, jnp.float32)
    for level in range(BUCKETS):
        running = jnp.where(bucket[None] == level, table[level][:, None, None], running)
    return running


def bucket_sums(bucket, logit_grads):
    totals = [
        jnp.sum(jnp.where(bucket[None] == level, logit_grads, 0.0), axis=(1, 2))
        for level in range(BUCKETS)
    ]
    return jnp.stack(totals, axis=0)


def pass_rim(rim, offset):
    return shifted(rim.astype(jnp.bfloat16), "ctx", offset).astype(rim.dtype)


def band_part(query_rows, key_rows, value_rows, grad_rows, clause_rows, table, score_scale):
    rows, width = query_rows.shape
    head_dim = width // HEADS
    wide = 2 * head_dim
    half = WINDOW // 2
    pair_rows = jnp.concatenate([key_rows[:, :wide], value_rows[:, :wide]], axis=1)
    extended, extended_clause = (
        with_halo(pair_rows, (("ctx", 0),), half),
        with_halo(clause_rows, (("ctx", 0),), half),
    )
    reach = rows + 2 * half
    nearby_key_rows = extended[:, :wide].reshape(reach, 2, head_dim)
    values_near = extended[:, wide:].reshape(reach, 2, head_dim)
    query_matrix = query_rows[:, :wide].reshape(rows, 2, head_dim)
    gradient_list = grad_rows[:, :wide].reshape(rows, 2, head_dim)
    start = lax.axis_index("ctx") * rows
    length = rows * lax.axis_size("ctx")
    local_query = jnp.arange(rows)[:, None]
    local_key = jnp.arange(reach)[None, :] - half
    global_key = start + local_key
    allowed = (jnp.abs(local_query - local_key) < half) & (global_key >= 0) & (global_key < length)
    bucket = jnp.minimum(jnp.abs(clause_rows[:, None] - extended_clause[None, :]), BUCKETS - 1)
    score_matrix = (
        jnp.einsum(
            "wvx,yvx->vwy", query_matrix, nearby_key_rows, preferred_element_type=jnp.float32
        )
        * score_scale
    )
    score_matrix = jnp.where(allowed[None], score_matrix + bucket_lookup(bucket, table), -jnp.inf)
    attended, query_gradient, softmax_weights, score_gradient, logit_grads, top, totals, delta = (
        rows_side(score_matrix, nearby_key_rows, values_near, gradient_list, score_scale)
    )
    key_gradient, value_gradient = keys_side(
        softmax_weights, score_gradient, query_matrix, gradient_list, score_scale
    )
    sums = jnp.concatenate(
        [key_gradient.reshape(reach, wide), value_gradient.reshape(reach, wide)], axis=1
    )
    own = sums[half : half + rows]
    from_next = pass_rim(sums[:half], -1)
    from_prev = pass_rim(sums[half + rows :], 1)
    own = own.at[rows - half :].add(from_next).at[:half].add(from_prev)
    own_key = own[:, :wide].reshape(rows, 2, head_dim)
    own_value = own[:, wide:].reshape(rows, 2, head_dim)
    return (attended, query_gradient, own_key, own_value, bucket_sums(bucket, logit_grads))


def dilated(
    query_rows, key_rows, value_rows, grad_rows, initial_flag, dilation_rate, bits, score_scale
):
    head_dim = query_rows.shape[1] // HEADS
    wide = 2 * head_dim
    picked_query = sample_rows(query_rows, initial_flag, dilation_rate)
    picked_key = sample_rows(key_rows, initial_flag, dilation_rate)
    picked_value = sample_rows(value_rows, initial_flag, dilation_rate)
    picked_grad = sample_rows(grad_rows, initial_flag, dilation_rate)
    count = picked_query.shape[0]
    gathered = span_rows(jnp.concatenate([picked_key, picked_value], axis=1), bits)
    gathered_rows = gathered.shape[0]
    every_key_rows = gathered[:, :wide].reshape(gathered_rows, 2, head_dim)
    every_value_rows = gathered[:, wide:].reshape(gathered_rows, 2, head_dim)
    query_matrix = picked_query.reshape(count, 2, head_dim)
    gradient_list = picked_grad.reshape(count, 2, head_dim)
    score_matrix = (
        jnp.einsum("wvx,yvx->vwy", query_matrix, every_key_rows, preferred_element_type=jnp.float32)
        * score_scale
    )
    attended, query_gradient, softmax_weights, score_gradient, logit_grads, top, totals, delta = (
        rows_side(score_matrix, every_key_rows, every_value_rows, gradient_list, score_scale)
    )
    key_gradient, value_gradient = keys_side(
        softmax_weights, score_gradient, query_matrix, gradient_list, score_scale
    )
    partial_sums = jnp.concatenate(
        [key_gradient.reshape(gathered_rows, wide), value_gradient.reshape(gathered_rows, wide)],
        axis=1,
    )
    own = span_sums(partial_sums, bits)
    own_key = own[:, :wide].reshape(count, 2, head_dim)
    own_value = own[:, wide:].reshape(count, 2, head_dim)
    return (
        spread_rows(attended, dilation_rate),
        spread_rows(query_gradient, dilation_rate),
        spread_rows(own_key, dilation_rate),
        spread_rows(own_value, dilation_rate),
    )


def shards(query, key, value, grad_out, clause, bias_table):
    query_rows = query[0]
    key_rows = key[0]
    value_rows = value[0]
    grad_rows = grad_out[0]
    clause_rows = clause[0]
    rows, width = query_rows.shape
    head_dim = width // HEADS
    score_scale = head_dim ** (-0.5)
    bucket_bit_count = lax.axis_size("ctx").bit_length() - 1
    band = band_part(
        query_rows, key_rows, value_rows, grad_rows, clause_rows, bias_table, score_scale
    )
    pieces = [band[:4]]
    for initial_flag, dilation_rate, bits in (
        (2, DILATION_FIRST, max(bucket_bit_count - 5, 1)),
        (4, DILATION_SECOND, bucket_bit_count - 2),
        (6, DILATION_THIRD, bucket_bit_count),
    ):
        pieces.append(
            dilated(
                query_rows,
                key_rows,
                value_rows,
                grad_rows,
                initial_flag,
                dilation_rate,
                bits,
                score_scale,
            )
        )
    bias_grad = lax.psum(band[4], ("dp", "ctx"))
    joined = [
        jnp.concatenate([piece[slot] for piece in pieces], axis=1)
        .reshape(1, rows, width)
        .astype(jnp.bfloat16)
        for slot in range(4)
    ]
    return (joined[0], joined[1], joined[2], joined[3], bias_grad)


def general(mesh):
    in_specs = (
        P("dp", "ctx", None),
        P("dp", "ctx", None),
        P("dp", "ctx", None),
        P("dp", "ctx", None),
        P("dp", "ctx"),
        P(),
    )
    out_specs = (
        P("dp", "ctx", None),
        P("dp", "ctx", None),
        P("dp", "ctx", None),
        P("dp", "ctx", None),
        P(),
    )
    return jax.shard_map(shards, mesh=mesh, in_specs=in_specs, out_specs=out_specs, check_vma=False)


ROWS = 256
D = 128
BF = jnp.bfloat16
F32 = jnp.float32


def mm(a, b, dims):
    return lax.dot_general(a, b, (dims, ((), ())), preferred_element_type=F32)


def nt(a, b):
    return mm(a, b, ((1,), (1,)))


def nn(a, b):
    return mm(a, b, ((1,), (0,)))


def tn(a, b):
    return mm(a, b, ((0,), (0,)))


def halves(x):
    high = x.astype(BF)
    return high, (x - high.astype(F32)).astype(BF)


def softmax_grads(scores, q, k, v, g, scale):
    top = jnp.max(scores, axis=-1, keepdims=True)
    raised = jnp.exp(scores - top)
    shares = raised * (1.0 / jnp.sum(raised, axis=-1, keepdims=True))
    weights = shares.astype(BF)
    attended = nn(weights, v)
    weight_grads = nt(g, v)
    delta = jnp.sum(shares * weight_grads, axis=-1, keepdims=True)
    logit_grads = shares * (weight_grads - delta)
    score_grads = logit_grads.astype(BF)
    grad_q = nn(score_grads, k) * scale
    grad_k = tn(score_grads, q) * scale
    grad_v = tn(weights, g)
    return attended, grad_q, grad_k, grad_v, logit_grads


def selector(count, step, offset):
    row = lax.broadcasted_iota(jnp.int32, (count, ROWS), 0)
    col = lax.broadcasted_iota(jnp.int32, (count, ROWS), 1)
    return (col == row * step + offset).astype(BF)


def clause_column(row_form):
    whole = jnp.broadcast_to(row_form[...], (8, ROWS))
    index = lax.broadcasted_iota(jnp.int32, whole.shape, 0)
    parts = jnp.where(index == 0, whole >> 6, jnp.where(index == 1, whole & 63, 0))
    line = lax.broadcasted_iota(jnp.int32, (8, D), 0)
    factor = jnp.where(line == 0, 64.0, jnp.where(line == 1, 1.0, 0.0))
    column = tn(parts.astype(F32).astype(BF), factor.astype(BF))
    return column.astype(jnp.int32)


def one_hot(column):
    lane = lax.broadcasted_iota(jnp.int32, (ROWS, D), 1)
    return (lane == (column & 127)).astype(F32).astype(BF)


def main_kernel(
    ctx_count, dp_count,
    table_hbm, clause_hbm, q_ref, k_ref, v_ref, g_ref,
    out_ref, second_ref, third_ref, bias_ref,
    table_ref, clause_ref, local, sampled, mine_send, local_sem, out_sem,
    pair_buf, halo_buf, halo_clause, pair_clause, grad_buf, grad_send, ret_send,
    s2, s3, bias_ctx, bias_dp,
    send_sem, recv_sem, s3_send, s3_recv, bc_send, bc_recv, bd_send, bd_recv,
):
    me = lax.axis_index("ctx")
    row = lax.axis_index("dp")
    c = lax.rem(me, 2)
    partner = me + 1 - 2 * c
    outward = me - 2 + 4 * c
    beyond = me + 2 - 4 * c
    has_out = (outward >= 0) & (outward < ctx_count)
    has_beyond = (beyond >= 0) & (beyond < ctx_count)
    scale = D**-0.5
    mesh_id = pl.DeviceIdType.MESH

    def columns(head):
        return pl.ds(pl.multiple_of(head * D, D), D)

    inputs = (k_ref, v_ref, q_ref, g_ref)
    loads = [
        pltpu.make_async_copy(ref.at[:, columns(2 * j + c)], local.at[i, j], local_sem.at[2 * i + j])
        for i, ref in enumerate(inputs)
        for j in range(2)
    ]
    sample_loads = [
        pltpu.make_async_copy(ref.at[:, 4 * D :], sampled.at[i], local_sem.at[8 + i])
        for i, ref in enumerate(inputs)
    ]
    small_loads = [
        pltpu.make_async_copy(clause_hbm, clause_ref, local_sem.at[12]),
        pltpu.make_async_copy(table_hbm, table_ref, local_sem.at[13]),
    ]
    for copy in sample_loads + small_loads + loads:
        copy.start()

    barrier = pltpu.get_barrier_semaphore()
    for step in range(1, ctx_count):
        pl.semaphore_signal(
            barrier, inc=1, device_id=(row, lax.rem(me + step, ctx_count)), device_id_type=mesh_id
        )
    for step in range(1, dp_count):
        pl.semaphore_signal(
            barrier, inc=1, device_id=(lax.rem(row + step, dp_count), me), device_id_type=mesh_id
        )
    pl.semaphore_wait(barrier, ctx_count + dp_count - 2)

    def remote(src, dst, index, target):
        return pltpu.make_async_remote_copy(
            src_ref=src,
            dst_ref=dst,
            send_sem=send_sem.at[index],
            recv_sem=recv_sem.at[index],
            device_id=(row, target),
            device_id_type=mesh_id,
        )

    band_out = [
        remote(inputs[i].at[:, columns(1 - c)], pair_buf.at[i], i, partner) for i in range(4)
    ]
    first_out = [
        remote(inputs[i].at[:, columns(3 - c)], pair_buf.at[4 + i], 4 + i, partner)
        for i in range(4)
    ]
    clause_out = remote(clause_hbm, pair_clause, 8, partner)
    own_halo = [
        remote(k_ref.at[:, columns(c)], halo_buf.at[1, 0], 9, outward),
        remote(v_ref.at[:, columns(c)], halo_buf.at[1, 1], 10, outward),
        remote(clause_hbm, halo_clause.at[1], 11, outward),
    ]
    far_halo = [
        remote(pair_buf.at[0], halo_buf.at[0, 0], 12, beyond),
        remote(pair_buf.at[1], halo_buf.at[0, 1], 13, beyond),
        remote(pair_clause, halo_clause.at[0], 14, beyond),
    ]

    clause_out.start()
    for copy in band_out[:2]:
        copy.start()

    @pl.when(has_out)
    def _():
        for copy in own_halo:
            copy.start()

    for copy in sample_loads:
        copy.wait()
    for i, ref in enumerate((sampled.at[2], sampled.at[0], sampled.at[1], sampled.at[3])):
        for h in range(2):
            part = nn(selector(32, DILATION_SECOND, h * DILATION_SECOND // 2), ref[:, h * D : (h + 1) * D])
            s2[0, :, (2 * i + h) * D : (2 * i + h + 1) * D] = part.astype(BF)

    def thirds(refs):
        return jnp.concatenate(
            [
                nn(selector(8, DILATION_THIRD, h * DILATION_THIRD // 2), ref[:, (2 + h) * D : (3 + h) * D])
                for ref in refs
                for h in range(2)
            ],
            axis=1,
        )

    s3[0] = jnp.concatenate([thirds((sampled.at[2], sampled.at[0])), thirds((sampled.at[1], sampled.at[3]))], axis=0).astype(BF)
    second_out = remote(s2.at[0], s2.at[1], 15, partner)
    second_out.start()
    third_out = []
    for step in range(1, ctx_count):
        copy = pltpu.make_async_remote_copy(
            src_ref=s3.at[0],
            dst_ref=s3.at[ctx_count - step],
            send_sem=s3_send.at[step],
            recv_sem=s3_recv.at[ctx_count - step],
            device_id=(row, lax.rem(me + step, ctx_count)),
            device_id_type=mesh_id,
        )
        copy.start()
        third_out.append(copy)
    for copy in first_out + band_out[2:]:
        copy.start()

    for copy in small_loads:
        copy.wait()
    line = lax.broadcasted_iota(jnp.int32, (D, D), 0)
    lane = lax.broadcasted_iota(jnp.int32, (D, D), 1)
    apart = jnp.abs(((lane - line + 64) & 127) - 64)
    table = jnp.zeros((D, D), F32)
    for level in range(BUCKETS):
        table = jnp.where(apart == level, table_ref[level, c], table)
    far_bias = table_ref[BUCKETS - 1, c]
    table_high, table_low = halves(table)

    clause_out.wait_recv()
    band_out[0].wait_recv()
    band_out[1].wait_recv()

    @pl.when(has_beyond)
    def _():
        for copy in far_halo:
            copy.start()

    @pl.when(jnp.logical_not(has_out))
    def _():
        halo_buf[0] = jnp.zeros((2, ROWS, D), BF)
        halo_clause[0] = jnp.zeros((1, ROWS), jnp.int32)

    @pl.when(jnp.logical_not(has_beyond))
    def _():
        halo_buf[1] = jnp.zeros((2, ROWS, D), BF)
        halo_clause[1] = jnp.zeros((1, ROWS), jnp.int32)

    second_out.wait_recv()
    both = jnp.concatenate([s2[0], s2[1]], axis=0)
    for h in range(2):
        q, k, v, g = [both[:, (2 * i + h) * D : (2 * i + h + 1) * D] for i in range(4)]
        results = softmax_grads(nt(q, k) * scale, q, k, v, g, scale)[:4]
        for i in range(4):
            second_ref[i, :, h * D : (h + 1) * D] = results[i][:32]

    for copy in third_out:
        copy.wait_recv()
    blocks = [s3[i].astype(F32) for i in range(ctx_count)]
    upper = jnp.concatenate([block[:8] for block in blocks], axis=0).astype(BF)
    lower = jnp.concatenate([block[8:] for block in blocks], axis=0).astype(BF)
    for h in range(2):
        q, k = [upper[:, (2 * i + h) * D : (2 * i + h + 1) * D] for i in range(2)]
        v, g = [lower[:, (2 * i + h) * D : (2 * i + h + 1) * D] for i in range(2)]
        results = softmax_grads(nt(q, k) * scale, q, k, v, g, scale)[:4]
        for i in range(4):
            third_ref[i, :, h * D : (h + 1) * D] = results[i][:8]

    for copy in loads:
        copy.wait()
    own = [local[i, 0] for i in range(4)]
    other = [pair_buf[0], pair_buf[1]]
    clauses = {"own": clause_ref, "other": pair_clause}
    cols = {name: clause_column(ref) for name, ref in clauses.items()}
    hots = {name: one_hot(col) for name, col in cols.items()}
    line = lax.broadcasted_iota(jnp.int32, (ROWS, ROWS), 0)
    lane = lax.broadcasted_iota(jnp.int32, (ROWS, ROWS), 1)
    diff = (line - lane) * (1 - 2 * c)

    def band_block(slot, mine, near, mine_name, near_name, sign, halo_valid):
        k = jnp.concatenate([mine[0], near[0], halo_buf[slot, 0]], axis=0)
        v = jnp.concatenate([mine[1], near[1], halo_buf[slot, 1]], axis=0)
        q, g = mine[2], mine[3]
        halo_hot = one_hot(clause_column(halo_clause.at[slot]))
        key_hot = jnp.concatenate([hots[mine_name], hots[near_name], halo_hot], axis=0)
        key_row = jnp.concatenate(
            [clauses[mine_name][0:1, :], clauses[near_name][0:1, :], halo_clause[slot, 0:1, :]],
            axis=1,
        )
        query_hot = hots[mine_name]
        close = jnp.abs(cols[mine_name][:, 0:1] - key_row) < BUCKETS - 1
        spread = jnp.concatenate(
            [nn(query_hot, table_high).astype(BF), nn(query_hot, table_low).astype(BF)], axis=1
        )
        bias = nt(spread, jnp.concatenate([key_hot, key_hot], axis=1))
        signed = diff * sign
        reach = jnp.where(halo_valid, 0, ROWS)
        allowed = jnp.concatenate(
            [jnp.ones((ROWS, ROWS), jnp.int32), jnp.where(signed > 0, 1, 0), jnp.where(-signed > reach, 1, 0)],
            axis=1,
        )
        scores = nt(q, k) * scale + jnp.where(close, bias, far_bias)
        scores = jnp.where(allowed > 0, scores, -jnp.inf)
        attended, grad_q, grad_k, grad_v, logit_grads = softmax_grads(scores, q, k, v, g, scale)
        kept = jnp.where(close, logit_grads, 0.0)
        rest = jnp.sum(jnp.where(close, 0.0, logit_grads), axis=0, keepdims=True)
        high, low = halves(kept)
        by_clause = nn(high, key_hot) + nn(low, key_hot)
        high, low = halves(by_clause)
        pairs = tn(query_hot, high) + tn(query_hot, low) + tn(high, query_hot) + tn(low, query_hot)
        return attended, grad_q, grad_k, grad_v, pairs, rest

    @pl.when(has_out)
    def _():
        for copy in far_halo:
            copy.wait_recv()

    attended, grad_q, gk_a, gv_a, pairs_a, rest_a = band_block(
        0, own, other, "own", "other", 1, has_out
    )
    keeps = [
        pltpu.make_async_copy(mine_send.at[i], out_ref.at[i, c], out_sem.at[i]) for i in range(8)
    ]

    def keep(i, value):
        mine_send[i] = value.astype(BF)
        keeps[i].start()

    keep(0, attended)
    keep(1, grad_q)
    grad_send[0, 0] = gk_a[2 * ROWS :].astype(BF)
    grad_send[0, 1] = gv_a[2 * ROWS :].astype(BF)
    back_out = remote(grad_send.at[0], grad_buf.at[0], 16, outward)
    back_far = remote(grad_send.at[1], grad_buf.at[1], 17, beyond)

    @pl.when(has_out)
    def _():
        back_out.start()

    ret = [remote(ret_send.at[i], out_ref.at[i, c], 18 + i, partner) for i in range(8)]
    for copy in first_out:
        copy.wait_recv()
    k, v, q, g = [
        jnp.concatenate([local[i, 1], pair_buf[4 + i]], axis=0) for i in range(4)
    ]
    results = softmax_grads(nt(q, k) * scale, q, k, v, g, scale)[:4]
    for i in range(4):
        ret_send[4 + i] = results[i][ROWS:].astype(BF)
        ret[4 + i].start()
        keep(4 + i, results[i][:ROWS])

    band_out[2].wait_recv()
    band_out[3].wait_recv()
    other += [pair_buf[2], pair_buf[3]]

    @pl.when(has_beyond)
    def _():
        for copy in own_halo:
            copy.wait_recv()

    attended, grad_q, gk_b, gv_b, pairs_b, rest_b = band_block(
        1, other, own, "other", "own", -1, has_beyond
    )
    ret_send[0] = attended.astype(BF)
    ret_send[1] = grad_q.astype(BF)
    grad_send[1, 0] = gk_b[2 * ROWS :].astype(BF)
    grad_send[1, 1] = gv_b[2 * ROWS :].astype(BF)

    @pl.when(has_beyond)
    def _():
        back_far.start()

    ret[0].start()
    ret[1].start()
    own_gk = gk_a[:ROWS] + gk_b[ROWS : 2 * ROWS]
    own_gv = gv_a[:ROWS] + gv_b[ROWS : 2 * ROWS]
    other_gk = gk_b[:ROWS] + gk_a[ROWS : 2 * ROWS]
    other_gv = gv_b[:ROWS] + gv_a[ROWS : 2 * ROWS]

    turned = pairs_a + pairs_b
    line = lax.broadcasted_iota(jnp.int32, (D, D), 0)
    for bit in range(7):
        shift = 1 << bit
        rolled = jnp.concatenate([turned[:, shift:], turned[:, :shift]], axis=1)
        turned = jnp.where((line & shift) > 0, rolled, turned)
    sums = jnp.sum(turned, axis=0, keepdims=True)
    rest = jnp.sum(rest_a + rest_b, axis=1, keepdims=True)
    lane = lax.broadcasted_iota(jnp.int32, (1, D), 1)
    sums = jnp.where(lane == 0, 0.5 * sums, sums)
    sums = jnp.where(lane < BUCKETS - 1, sums, jnp.where(lane == BUCKETS - 1, rest, 0.0))
    tile_line = lax.broadcasted_iota(jnp.int32, (8, D), 0)
    bias_ctx[me] = jnp.where(tile_line == c, sums, 0.0)
    bias_out = []
    for step in range(1, ctx_count):
        copy = pltpu.make_async_remote_copy(
            src_ref=bias_ctx.at[me],
            dst_ref=bias_ctx.at[me],
            send_sem=bc_send.at[step],
            recv_sem=bc_recv.at[step],
            device_id=(row, lax.rem(me + step, ctx_count)),
            device_id_type=mesh_id,
        )
        copy.start()
        bias_out.append(copy)

    @pl.when(has_beyond)
    def _():
        back_out.wait_recv()

    @pl.when(has_out)
    def _():
        back_far.wait_recv()

    @pl.when(jnp.logical_not(has_beyond))
    def _():
        grad_buf[0] = jnp.zeros((2, ROWS, D), BF)

    @pl.when(jnp.logical_not(has_out))
    def _():
        grad_buf[1] = jnp.zeros((2, ROWS, D), BF)

    ret_send[2] = (other_gk + grad_buf[0, 0].astype(F32)).astype(BF)
    ret_send[3] = (other_gv + grad_buf[0, 1].astype(F32)).astype(BF)
    ret[2].start()
    ret[3].start()
    keep(2, own_gk + grad_buf[1, 0].astype(F32))
    keep(3, own_gv + grad_buf[1, 1].astype(F32))

    for copy in bias_out:
        copy.wait_recv()
    total = bias_ctx[0]
    for i in range(1, ctx_count):
        total = total + bias_ctx[i]
    bias_dp[row] = total
    docs_out = []
    for step in range(1, dp_count):
        copy = pltpu.make_async_remote_copy(
            src_ref=bias_dp.at[row],
            dst_ref=bias_dp.at[row],
            send_sem=bd_send.at[step],
            recv_sem=bd_recv.at[step],
            device_id=(lax.rem(row + step, dp_count), me),
            device_id_type=mesh_id,
        )
        copy.start()
        docs_out.append(copy)

    for copy in docs_out:
        copy.wait_recv()
    total = bias_dp[0]
    for i in range(1, dp_count):
        total = total + bias_dp[i]
    bias_ref[...] = total

    for copy in ret:
        copy.wait_recv()
    for copy in keeps:
        copy.wait()

    for copy in band_out + first_out + [clause_out, second_out] + third_out + bias_out + docs_out + ret:
        copy.wait_send()

    @pl.when(has_out)
    def _():
        for copy in own_halo + [back_out]:
            copy.wait_send()

    @pl.when(has_beyond)
    def _():
        for copy in far_halo + [back_far]:
            copy.wait_send()


def layout_kernel(heads_ref, second_ref, third_ref, tile_ref, *outs):
    bias_ref = outs[4]
    row = lax.broadcasted_iota(jnp.int32, (BUCKETS, D), 0)
    col = lax.broadcasted_iota(jnp.int32, (BUCKETS, D), 1)
    for h in range(2):
        picked = jnp.where(row == col, tile_ref[h : h + 1, :], 0.0)
        bias_ref[:, h : h + 1] = jnp.sum(picked, axis=1, keepdims=True)
    for i, out in enumerate(outs[:4]):
        for h in range(2):
            out[:, h * D : (h + 1) * D] = heads_ref[i, h]
            out[:, (2 + h) * D : (3 + h) * D] = heads_ref[4 + i, h]
            seconds = second_ref[i, :, h * D : (h + 1) * D].astype(BF)
            spread = tn(selector(32, DILATION_SECOND, h * DILATION_SECOND // 2), seconds)
            out[:, (4 + h) * D : (5 + h) * D] = spread.astype(BF)
            thirds = third_ref[i, :, h * D : (h + 1) * D].astype(BF)
            spread = tn(selector(8, DILATION_THIRD, h * DILATION_THIRD // 2), thirds)
            out[:, (6 + h) * D : (7 + h) * D] = spread.astype(BF)


def paired(ctx_count, dp_count, query, key, value, grad_out, clause, bias_table):
    vmem = pl.BlockSpec(memory_space=pltpu.VMEM)
    far = pl.BlockSpec(memory_space=pltpu.HBM)
    dma = pltpu.SemaphoreType.DMA
    block = (ROWS, D)
    heads, second, third, bias = pl.pallas_call(
        lambda *refs: main_kernel(ctx_count, dp_count, *refs),
        out_shape=[
            jax.ShapeDtypeStruct((8, 2) + block, BF),
            jax.ShapeDtypeStruct((4, 32, 2 * D), F32),
            jax.ShapeDtypeStruct((4, 8, 2 * D), F32),
            jax.ShapeDtypeStruct((8, D), F32),
        ],
        in_specs=[far] * 6,
        out_specs=[far] + [vmem] * 3,
        scratch_shapes=[
            pltpu.SMEM((BUCKETS, 2), F32),
            pltpu.VMEM((1, ROWS), jnp.int32),
            pltpu.VMEM((4, 2) + block, BF),
            pltpu.VMEM((4, ROWS, 4 * D), BF),
            pltpu.VMEM((8,) + block, BF),
            dma((14,)),
            dma((8,)),
            pltpu.VMEM((8,) + block, BF),
            pltpu.VMEM((2, 2) + block, BF),
            pltpu.VMEM((2, 1, ROWS), jnp.int32),
            pltpu.VMEM((1, ROWS), jnp.int32),
            pltpu.VMEM((2, 2) + block, BF),
            pltpu.VMEM((2, 2) + block, BF),
            pltpu.VMEM((8,) + block, BF),
            pltpu.VMEM((2, 32, 8 * D), BF),
            pltpu.VMEM((ctx_count, 16, 4 * D), BF),
            pltpu.VMEM((ctx_count, 8, D), F32),
            pltpu.VMEM((dp_count, 8, D), F32),
            dma((26,)),
            dma((26,)),
            dma((ctx_count,)),
            dma((ctx_count,)),
            dma((ctx_count,)),
            dma((ctx_count,)),
            dma((dp_count,)),
            dma((dp_count,)),
        ],
        compiler_params=pltpu.CompilerParams(
            collective_id=0, has_side_effects=True, vmem_limit_bytes=48 * 1024 * 1024
        ),
        name="attend",
    )(bias_table, clause, query[0], key[0], value[0], grad_out[0])
    outs = pl.pallas_call(
        layout_kernel,
        out_shape=[jax.ShapeDtypeStruct((ROWS, HEADS * D), BF)] * 4
        + [jax.ShapeDtypeStruct((BUCKETS, 2), F32)],
        in_specs=[vmem] * 4,
        out_specs=[vmem] * 5,
        compiler_params=pltpu.CompilerParams(vmem_limit_bytes=32 * 1024 * 1024),
        name="layout",
    )(heads, second, third, bias)
    return tuple(out[None] for out in outs[:4]) + (outs[4],)


def solution(mesh):
    ctx_count, dp_count = mesh.shape["ctx"], mesh.shape["dp"]
    if ctx_count != 8:
        return general(mesh)
    spec = P("dp", "ctx", None)

    def body(*arrays):
        return paired(ctx_count, dp_count, *arrays)

    return jax.shard_map(
        body,
        mesh=mesh,
        in_specs=(spec, spec, spec, spec, P("dp", "ctx"), P()),
        out_specs=(spec, spec, spec, spec, P()),
        check_vma=False,
    )
```

```python
import jax
import jax.numpy as jnp
from jax import lax
from jax.experimental import pallas as pl
from jax.experimental.pallas import tpu as pltpu
from jax.sharding import PartitionSpec as P

HEADS = 8
WINDOW = 512
BUCKETS = 32
DILATION_FIRST = 1
DILATION_SECOND = 8
DILATION_THIRD = 32


def swapped(block, axis, bit):
    count = lax.axis_size(axis)
    route = []
    for low in range(count):
        high = low | 1 << bit
        if high != low and high < count:
            route += [(low, high), (high, low)]
    return lax.ppermute(block, axis, route)


def shifted(value, axis, steps):
    count = lax.axis_size(axis)
    leading, last = (max(0, -steps), min(count, count - steps))
    return lax.ppermute(value, axis, [(source, source + steps) for source in range(leading, last)])


def with_halo(shard, sides, width):
    for axis, dim in sides:
        size, length = (lax.axis_size(axis), shard.shape[dim])
        up = [(i, (i + 1) % size) for i in range(size - 1)]
        down = [(j, i) for i, j in up]
        last = lax.slice_in_dim(shard, length - width, length, axis=dim)
        leading = lax.slice_in_dim(shard, 0, width, axis=dim)
        before = lax.ppermute(last, axis, up)
        after = lax.ppermute(leading, axis, down)
        shard = jnp.concatenate([before, shard, after], axis=dim)
    return shard


def sample_rows(matrix, initial_flag, dilation_rate):
    count = matrix.shape[0] // dilation_rate
    head_dim = matrix.shape[1] // HEADS
    grid = matrix.reshape(count, dilation_rate, HEADS, head_dim)
    return jnp.concatenate(
        [grid[:, 0, initial_flag], grid[:, dilation_rate // 2, initial_flag + 1]], axis=1
    )


def spread_rows(sampled, dilation_rate):
    count = sampled.shape[0]
    grid = jnp.zeros((count, dilation_rate) + sampled.shape[1:], sampled.dtype)
    grid = grid.at[:, 0, 0].set(sampled[:, 0]).at[:, dilation_rate // 2, 1].set(sampled[:, 1])
    return grid.reshape((count * dilation_rate,) + sampled.shape[1:])


def upper_half(bit):
    index = lax.axis_index("ctx")
    return index // 2**bit % 2 == 1


def double_rows(block, bits):
    for bit in range(bits):
        other = swapped(block, "ctx", bit)
        block = jnp.where(
            upper_half(bit),
            jnp.concatenate([other, block], axis=0),
            jnp.concatenate([block, other], axis=0),
        )
    return block


def halve_sums(block, bits):
    for bit in reversed(range(bits)):
        half = block.shape[0] // 2
        lower, higher = (block[:half], block[half:])
        upper = upper_half(bit)
        outgoing = jnp.where(upper, lower, higher)
        staying = jnp.where(upper, higher, lower)
        block = staying + swapped(outgoing.astype(jnp.bfloat16), "ctx", bit).astype(outgoing.dtype)
    return block


def span_rows(block, bits):
    return double_rows(block, bits)


def span_sums(block, bits):
    return halve_sums(block, bits)


def rows_side(score_matrix, every_key_rows, every_value_rows, gradient_list, score_scale):
    top = jnp.max(score_matrix, axis=-1, keepdims=True)
    raised = jnp.exp(score_matrix - top)
    totals = jnp.sum(raised, axis=-1, keepdims=True)
    shares = raised / totals
    softmax_weights = shares.astype(jnp.bfloat16)
    attended = jnp.einsum(
        "ezb,beo->zeo", softmax_weights, every_value_rows, preferred_element_type=jnp.float32
    )
    weight_gradient = jnp.einsum(
        "wvx,yvx->vwy", gradient_list, every_value_rows, preferred_element_type=jnp.float32
    )
    delta = jnp.sum(shares * weight_gradient, axis=-1, keepdims=True)
    logit_grads = shares * (weight_gradient - delta)
    score_gradient = logit_grads.astype(jnp.bfloat16)
    query_gradient = (
        jnp.einsum(
            "ezb,beo->zeo", score_gradient, every_key_rows, preferred_element_type=jnp.float32
        )
        * score_scale
    )
    return (
        attended,
        query_gradient,
        softmax_weights,
        score_gradient,
        logit_grads,
        top,
        totals,
        delta,
    )


def keys_side(softmax_weights, score_gradient, query_matrix, gradient_list, score_scale):
    key_gradient = (
        jnp.einsum("vjb,jvw->bvw", score_gradient, query_matrix, preferred_element_type=jnp.float32)
        * score_scale
    )
    value_gradient = jnp.einsum(
        "vjb,jvw->bvw", softmax_weights, gradient_list, preferred_element_type=jnp.float32
    )
    return (key_gradient, value_gradient)


def bucket_lookup(bucket, table):
    running = jnp.zeros((table.shape[1],) + bucket.shape, jnp.float32)
    for level in range(BUCKETS):
        running = jnp.where(bucket[None] == level, table[level][:, None, None], running)
    return running


def bucket_sums(bucket, logit_grads):
    totals = [
        jnp.sum(jnp.where(bucket[None] == level, logit_grads, 0.0), axis=(1, 2))
        for level in range(BUCKETS)
    ]
    return jnp.stack(totals, axis=0)


def pass_rim(rim, offset):
    return shifted(rim.astype(jnp.bfloat16), "ctx", offset).astype(rim.dtype)


def band_part(query_rows, key_rows, value_rows, grad_rows, clause_rows, table, score_scale):
    rows, width = query_rows.shape
    head_dim = width // HEADS
    wide = 2 * head_dim
    half = WINDOW // 2
    pair_rows = jnp.concatenate([key_rows[:, :wide], value_rows[:, :wide]], axis=1)
    extended, extended_clause = (
        with_halo(pair_rows, (("ctx", 0),), half),
        with_halo(clause_rows, (("ctx", 0),), half),
    )
    reach = rows + 2 * half
    nearby_key_rows = extended[:, :wide].reshape(reach, 2, head_dim)
    values_near = extended[:, wide:].reshape(reach, 2, head_dim)
    query_matrix = query_rows[:, :wide].reshape(rows, 2, head_dim)
    gradient_list = grad_rows[:, :wide].reshape(rows, 2, head_dim)
    start = lax.axis_index("ctx") * rows
    length = rows * lax.axis_size("ctx")
    local_query = jnp.arange(rows)[:, None]
    local_key = jnp.arange(reach)[None, :] - half
    global_key = start + local_key
    allowed = (jnp.abs(local_query - local_key) < half) & (global_key >= 0) & (global_key < length)
    bucket = jnp.minimum(jnp.abs(clause_rows[:, None] - extended_clause[None, :]), BUCKETS - 1)
    score_matrix = (
        jnp.einsum(
            "wvx,yvx->vwy", query_matrix, nearby_key_rows, preferred_element_type=jnp.float32
        )
        * score_scale
    )
    score_matrix = jnp.where(allowed[None], score_matrix + bucket_lookup(bucket, table), -jnp.inf)
    attended, query_gradient, softmax_weights, score_gradient, logit_grads, top, totals, delta = (
        rows_side(score_matrix, nearby_key_rows, values_near, gradient_list, score_scale)
    )
    key_gradient, value_gradient = keys_side(
        softmax_weights, score_gradient, query_matrix, gradient_list, score_scale
    )
    sums = jnp.concatenate(
        [key_gradient.reshape(reach, wide), value_gradient.reshape(reach, wide)], axis=1
    )
    own = sums[half : half + rows]
    from_next = pass_rim(sums[:half], -1)
    from_prev = pass_rim(sums[half + rows :], 1)
    own = own.at[rows - half :].add(from_next).at[:half].add(from_prev)
    own_key = own[:, :wide].reshape(rows, 2, head_dim)
    own_value = own[:, wide:].reshape(rows, 2, head_dim)
    return (attended, query_gradient, own_key, own_value, bucket_sums(bucket, logit_grads))


def dilated(
    query_rows, key_rows, value_rows, grad_rows, initial_flag, dilation_rate, bits, score_scale
):
    head_dim = query_rows.shape[1] // HEADS
    wide = 2 * head_dim
    picked_query = sample_rows(query_rows, initial_flag, dilation_rate)
    picked_key = sample_rows(key_rows, initial_flag, dilation_rate)
    picked_value = sample_rows(value_rows, initial_flag, dilation_rate)
    picked_grad = sample_rows(grad_rows, initial_flag, dilation_rate)
    count = picked_query.shape[0]
    gathered = span_rows(jnp.concatenate([picked_key, picked_value], axis=1), bits)
    gathered_rows = gathered.shape[0]
    every_key_rows = gathered[:, :wide].reshape(gathered_rows, 2, head_dim)
    every_value_rows = gathered[:, wide:].reshape(gathered_rows, 2, head_dim)
    query_matrix = picked_query.reshape(count, 2, head_dim)
    gradient_list = picked_grad.reshape(count, 2, head_dim)
    score_matrix = (
        jnp.einsum("wvx,yvx->vwy", query_matrix, every_key_rows, preferred_element_type=jnp.float32)
        * score_scale
    )
    attended, query_gradient, softmax_weights, score_gradient, logit_grads, top, totals, delta = (
        rows_side(score_matrix, every_key_rows, every_value_rows, gradient_list, score_scale)
    )
    key_gradient, value_gradient = keys_side(
        softmax_weights, score_gradient, query_matrix, gradient_list, score_scale
    )
    partial_sums = jnp.concatenate(
        [key_gradient.reshape(gathered_rows, wide), value_gradient.reshape(gathered_rows, wide)],
        axis=1,
    )
    own = span_sums(partial_sums, bits)
    own_key = own[:, :wide].reshape(count, 2, head_dim)
    own_value = own[:, wide:].reshape(count, 2, head_dim)
    return (
        spread_rows(attended, dilation_rate),
        spread_rows(query_gradient, dilation_rate),
        spread_rows(own_key, dilation_rate),
        spread_rows(own_value, dilation_rate),
    )


def shards(query, key, value, grad_out, clause, bias_table):
    query_rows = query[0]
    key_rows = key[0]
    value_rows = value[0]
    grad_rows = grad_out[0]
    clause_rows = clause[0]
    rows, width = query_rows.shape
    head_dim = width // HEADS
    score_scale = head_dim ** (-0.5)
    bucket_bit_count = lax.axis_size("ctx").bit_length() - 1
    band = band_part(
        query_rows, key_rows, value_rows, grad_rows, clause_rows, bias_table, score_scale
    )
    pieces = [band[:4]]
    for initial_flag, dilation_rate, bits in (
        (2, DILATION_FIRST, max(bucket_bit_count - 5, 1)),
        (4, DILATION_SECOND, bucket_bit_count - 2),
        (6, DILATION_THIRD, bucket_bit_count),
    ):
        pieces.append(
            dilated(
                query_rows,
                key_rows,
                value_rows,
                grad_rows,
                initial_flag,
                dilation_rate,
                bits,
                score_scale,
            )
        )
    bias_grad = lax.psum(band[4], ("dp", "ctx"))
    joined = [
        jnp.concatenate([piece[slot] for piece in pieces], axis=1)
        .reshape(1, rows, width)
        .astype(jnp.bfloat16)
        for slot in range(4)
    ]
    return (joined[0], joined[1], joined[2], joined[3], bias_grad)


def general(mesh):
    in_specs = (
        P("dp", "ctx", None),
        P("dp", "ctx", None),
        P("dp", "ctx", None),
        P("dp", "ctx", None),
        P("dp", "ctx"),
        P(),
    )
    out_specs = (
        P("dp", "ctx", None),
        P("dp", "ctx", None),
        P("dp", "ctx", None),
        P("dp", "ctx", None),
        P(),
    )
    return jax.shard_map(shards, mesh=mesh, in_specs=in_specs, out_specs=out_specs, check_vma=False)


ROWS = 256
D = 128
BF = jnp.bfloat16
F32 = jnp.float32


def mm(a, b, dims):
    return lax.dot_general(a, b, (dims, ((), ())), preferred_element_type=F32)


def nt(a, b):
    return mm(a, b, ((1,), (1,)))


def nn(a, b):
    return mm(a, b, ((1,), (0,)))


def tn(a, b):
    return mm(a, b, ((0,), (0,)))


def halves(x):
    high = x.astype(BF)
    return high, (x - high.astype(F32)).astype(BF)


def softmax_grads(scores, q, k, v, g, scale):
    top = jnp.max(scores, axis=-1, keepdims=True)
    raised = jnp.exp(scores - top)
    shares = raised * (1.0 / jnp.sum(raised, axis=-1, keepdims=True))
    weights = shares.astype(BF)
    attended = nn(weights, v)
    weight_grads = nt(g, v)
    delta = jnp.sum(shares * weight_grads, axis=-1, keepdims=True)
    logit_grads = shares * (weight_grads - delta)
    score_grads = logit_grads.astype(BF)
    grad_q = nn(score_grads, k) * scale
    grad_k = tn(score_grads, q) * scale
    grad_v = tn(weights, g)
    return attended, grad_q, grad_k, grad_v, logit_grads


def softmax_rows(rows, chunk, score_ref, grad_ref, weight_ref, score_grad_ref, shape_scores, take_grads):
    for start in range(0, rows, chunk):
        at = pl.ds(start, chunk)
        scores = shape_scores(at, start, score_ref[at, :])
        top = jnp.max(scores, axis=-1, keepdims=True)
        raised = jnp.exp(scores - top)
        shares = raised * (1.0 / jnp.sum(raised, axis=-1, keepdims=True))
        weight_ref[at, :] = shares.astype(BF)
        weight_grads = grad_ref[at, :]
        delta = jnp.sum(shares * weight_grads, axis=-1, keepdims=True)
        logit_grads = shares * (weight_grads - delta)
        score_grad_ref[at, :] = logit_grads.astype(BF)
        take_grads(at, logit_grads)


def selector(count, step, offset):
    row = lax.broadcasted_iota(jnp.int32, (count, ROWS), 0)
    col = lax.broadcasted_iota(jnp.int32, (count, ROWS), 1)
    return (col == row * step + offset).astype(BF)


def clause_column(row_form):
    whole = jnp.broadcast_to(row_form[...], (8, ROWS))
    index = lax.broadcasted_iota(jnp.int32, whole.shape, 0)
    parts = jnp.where(index == 0, whole >> 6, jnp.where(index == 1, whole & 63, 0))
    line = lax.broadcasted_iota(jnp.int32, (8, D), 0)
    factor = jnp.where(line == 0, 64.0, jnp.where(line == 1, 1.0, 0.0))
    column = tn(parts.astype(F32).astype(BF), factor.astype(BF))
    return column.astype(jnp.int32)


def one_hot(column):
    lane = lax.broadcasted_iota(jnp.int32, (ROWS, D), 1)
    return (lane == (column & 127)).astype(F32).astype(BF)


def main_kernel(
    ctx_count, dp_count,
    table_hbm, clause_hbm, q_ref, k_ref, v_ref, g_ref,
    out_ref, second_ref, third_ref, bias_ref,
    table_ref, clause_ref, local, sampled, mine_send, local_sem, out_sem,
    pair_buf, halo_buf, halo_clause, pair_clause, grad_buf, grad_send, ret_send,
    s2, s3, bias_ctx, bias_dp,
    band_scores, band_bias, band_wg, band_w, band_sg, band_high, band_low, pair_scores, pair_wg, pair_w, pair_sg,
    send_sem, recv_sem, s3_send, s3_recv, bc_send, bc_recv, bd_send, bd_recv,
):
    me = lax.axis_index("ctx")
    row = lax.axis_index("dp")
    c = lax.rem(me, 2)
    partner = me + 1 - 2 * c
    outward = me - 2 + 4 * c
    beyond = me + 2 - 4 * c
    has_out = (outward >= 0) & (outward < ctx_count)
    has_beyond = (beyond >= 0) & (beyond < ctx_count)
    scale = D**-0.5
    mesh_id = pl.DeviceIdType.MESH

    def columns(head):
        return pl.ds(pl.multiple_of(head * D, D), D)

    inputs = (k_ref, v_ref, q_ref, g_ref)
    loads = [
        pltpu.make_async_copy(ref.at[:, columns(2 * j + c)], local.at[i, j], local_sem.at[2 * i + j])
        for i, ref in enumerate(inputs)
        for j in range(2)
    ]
    sample_loads = [
        pltpu.make_async_copy(ref.at[:, 4 * D :], sampled.at[i], local_sem.at[8 + i])
        for i, ref in enumerate(inputs)
    ]
    small_loads = [
        pltpu.make_async_copy(clause_hbm, clause_ref, local_sem.at[12]),
        pltpu.make_async_copy(table_hbm, table_ref, local_sem.at[13]),
    ]
    for copy in sample_loads + small_loads + loads:
        copy.start()

    barrier = pltpu.get_barrier_semaphore()
    for step in range(1, ctx_count):
        pl.semaphore_signal(
            barrier, inc=1, device_id=(row, lax.rem(me + step, ctx_count)), device_id_type=mesh_id
        )
    for step in range(1, dp_count):
        pl.semaphore_signal(
            barrier, inc=1, device_id=(lax.rem(row + step, dp_count), me), device_id_type=mesh_id
        )
    pl.semaphore_wait(barrier, ctx_count + dp_count - 2)

    def remote(src, dst, index, target):
        return pltpu.make_async_remote_copy(
            src_ref=src,
            dst_ref=dst,
            send_sem=send_sem.at[index],
            recv_sem=recv_sem.at[index],
            device_id=(row, target),
            device_id_type=mesh_id,
        )

    band_out = [
        remote(inputs[i].at[:, columns(1 - c)], pair_buf.at[i], i, partner) for i in range(4)
    ]
    first_out = [
        remote(inputs[i].at[:, columns(3 - c)], pair_buf.at[4 + i], 4 + i, partner)
        for i in range(4)
    ]
    clause_out = remote(clause_hbm, pair_clause, 8, partner)
    own_halo = [
        remote(k_ref.at[:, columns(c)], halo_buf.at[1, 0], 9, outward),
        remote(v_ref.at[:, columns(c)], halo_buf.at[1, 1], 10, outward),
        remote(clause_hbm, halo_clause.at[1], 11, outward),
    ]
    far_halo = [
        remote(pair_buf.at[0], halo_buf.at[0, 0], 12, beyond),
        remote(pair_buf.at[1], halo_buf.at[0, 1], 13, beyond),
        remote(pair_clause, halo_clause.at[0], 14, beyond),
    ]

    clause_out.start()
    for copy in band_out[:2]:
        copy.start()

    @pl.when(has_out)
    def _():
        for copy in own_halo:
            copy.start()

    for copy in sample_loads:
        copy.wait()
    for i, ref in enumerate((sampled.at[2], sampled.at[0], sampled.at[1], sampled.at[3])):
        for h in range(2):
            part = nn(selector(32, DILATION_SECOND, h * DILATION_SECOND // 2), ref[:, h * D : (h + 1) * D])
            s2[0, :, (2 * i + h) * D : (2 * i + h + 1) * D] = part.astype(BF)

    def thirds(refs):
        return jnp.concatenate(
            [
                nn(selector(8, DILATION_THIRD, h * DILATION_THIRD // 2), ref[:, (2 + h) * D : (3 + h) * D])
                for ref in refs
                for h in range(2)
            ],
            axis=1,
        )

    s3[0] = jnp.concatenate([thirds((sampled.at[2], sampled.at[0])), thirds((sampled.at[1], sampled.at[3]))], axis=0).astype(BF)
    second_out = remote(s2.at[0], s2.at[1], 15, partner)
    second_out.start()
    third_pair = pltpu.make_async_remote_copy(
        src_ref=s3.at[0],
        dst_ref=s3.at[1],
        send_sem=s3_send.at[0],
        recv_sem=s3_recv.at[0],
        device_id=(row, partner),
        device_id_type=mesh_id,
    )
    third_pair.start()
    for copy in first_out + band_out[2:]:
        copy.start()

    for copy in small_loads:
        copy.wait()
    line = lax.broadcasted_iota(jnp.int32, (D, D), 0)
    lane = lax.broadcasted_iota(jnp.int32, (D, D), 1)
    apart = jnp.abs(((lane - line + 64) & 127) - 64)
    table = jnp.zeros((D, D), F32)
    for level in range(BUCKETS):
        table = jnp.where(apart == level, table_ref[c, level], table)
    far_bias = table_ref[c, BUCKETS - 1]
    table_high, table_low = halves(table)

    clause_out.wait_recv()
    band_out[0].wait_recv()
    band_out[1].wait_recv()

    @pl.when(has_beyond)
    def _():
        for copy in far_halo:
            copy.start()

    @pl.when(jnp.logical_not(has_out))
    def _():
        halo_buf[0] = jnp.zeros((2, ROWS, D), BF)
        halo_clause[0] = jnp.zeros((1, ROWS), jnp.int32)

    @pl.when(jnp.logical_not(has_beyond))
    def _():
        halo_buf[1] = jnp.zeros((2, ROWS, D), BF)
        halo_clause[1] = jnp.zeros((1, ROWS), jnp.int32)

    third_pair.wait_recv()
    third_out = []
    for step in range(1, ctx_count // 2):
        copy = pltpu.make_async_remote_copy(
            src_ref=s3.at[pl.ds(0, 2)],
            dst_ref=s3.at[pl.ds(ctx_count - 2 * step, 2)],
            send_sem=s3_send.at[step],
            recv_sem=s3_recv.at[step],
            device_id=(row, lax.rem(me + 2 * step, ctx_count)),
            device_id_type=mesh_id,
        )
        copy.start()
        third_out.append(copy)

    second_out.wait_recv()
    both = jnp.concatenate([s2[0], s2[1]], axis=0)
    for h in range(2):
        q, k, v, g = [both[:, (2 * i + h) * D : (2 * i + h + 1) * D] for i in range(4)]
        results = softmax_grads(nt(q, k) * scale, q, k, v, g, scale)[:4]
        for i in range(4):
            second_ref[i, :, h * D : (h + 1) * D] = results[i][:32]

    for copy in third_out:
        copy.wait_recv()
    blocks = [s3[i].astype(F32) for i in range(ctx_count)]
    upper = jnp.concatenate([block[:8] for block in blocks], axis=0).astype(BF)
    lower = jnp.concatenate([block[8:] for block in blocks], axis=0).astype(BF)
    for h in range(2):
        q, k = [upper[:, (2 * i + h) * D : (2 * i + h + 1) * D] for i in range(2)]
        v, g = [lower[:, (2 * i + h) * D : (2 * i + h + 1) * D] for i in range(2)]
        results = softmax_grads(nt(q, k) * scale, q, k, v, g, scale)[:4]
        for i in range(4):
            third_ref[i, :, h * D : (h + 1) * D] = results[i][:8]

    for copy in loads:
        copy.wait()
    own = [local[i, 0] for i in range(4)]
    other = [pair_buf[0], pair_buf[1]]
    clauses = {"own": clause_ref, "other": pair_clause}
    cols = {name: clause_column(ref) for name, ref in clauses.items()}
    hots = {name: one_hot(col) for name, col in cols.items()}
    def band_block(slot, mine, near, mine_name, near_name, sign, halo_valid):
        k = jnp.concatenate([mine[0], near[0], halo_buf[slot, 0]], axis=0)
        v = jnp.concatenate([mine[1], near[1], halo_buf[slot, 1]], axis=0)
        q, g = mine[2], mine[3]
        halo_hot = one_hot(clause_column(halo_clause.at[slot]))
        key_hot = jnp.concatenate([hots[mine_name], hots[near_name], halo_hot], axis=0)
        key_row = jnp.concatenate(
            [clauses[mine_name][0:1, :], clauses[near_name][0:1, :], halo_clause[slot, 0:1, :]],
            axis=1,
        )
        query_hot = hots[mine_name]
        spread = jnp.concatenate(
            [nn(query_hot, table_high).astype(BF), nn(query_hot, table_low).astype(BF)], axis=1
        )
        band_bias[...] = nt(spread, jnp.concatenate([key_hot, key_hot], axis=1))
        band_scores[...] = nt(q, k)
        band_wg[...] = nt(g, v)
        reach = jnp.where(halo_valid, 0, ROWS)
        col = cols[mine_name]
        turn = (1 - 2 * c) * sign
        chunk = 32

        def near_clauses(start):
            return jnp.abs(col[start : start + chunk, 0:1] - key_row) < BUCKETS - 1

        def shape_scores(at, start, scores):
            close = near_clauses(start)
            scores = scores * scale + jnp.where(close, band_bias[at, :], far_bias)
            row_index = lax.broadcasted_iota(jnp.int32, (chunk, ROWS), 0) + start
            col_index = lax.broadcasted_iota(jnp.int32, (chunk, ROWS), 1)
            signed = (row_index - col_index) * turn
            return jnp.concatenate(
                [
                    scores[:, :ROWS],
                    jnp.where(signed > 0, scores[:, ROWS : 2 * ROWS], -jnp.inf),
                    jnp.where(-signed > reach, scores[:, 2 * ROWS :], -jnp.inf),
                ],
                axis=1,
            )

        def take_grads(at, logit_grads):
            high, low = halves(jnp.where(near_clauses(at.start), logit_grads, 0.0))
            band_high[at, :] = high
            band_low[at, :] = low

        softmax_rows(ROWS, chunk, band_scores, band_wg, band_w, band_sg, shape_scores, take_grads)
        weights, score_grads = band_w[...], band_sg[...]
        attended = nn(weights, v)
        grad_q = nn(score_grads, k) * scale
        grad_k = tn(score_grads, q) * scale
        grad_v = tn(weights, g)
        by_clause = nn(band_high[...], key_hot) + nn(band_low[...], key_hot)
        high, low = halves(by_clause)
        pairs = tn(query_hot, high) + tn(query_hot, low) + tn(high, query_hot) + tn(low, query_hot)
        return attended, grad_q, grad_k, grad_v, pairs

    @pl.when(has_out)
    def _():
        for copy in far_halo:
            copy.wait_recv()

    attended, grad_q, gk_a, gv_a, pairs_a = band_block(
        0, own, other, "own", "other", 1, has_out
    )
    keeps = [
        pltpu.make_async_copy(mine_send.at[i], out_ref.at[i, c], out_sem.at[i]) for i in range(8)
    ]

    def keep(i, value):
        mine_send[i] = value.astype(BF)
        keeps[i].start()

    keep(0, attended)
    keep(1, grad_q)
    grad_send[0, 0] = gk_a[2 * ROWS :].astype(BF)
    grad_send[0, 1] = gv_a[2 * ROWS :].astype(BF)
    back_out = remote(grad_send.at[0], grad_buf.at[0], 16, outward)
    back_far = remote(grad_send.at[1], grad_buf.at[1], 17, beyond)

    @pl.when(has_out)
    def _():
        back_out.start()

    ret = [remote(ret_send.at[i], out_ref.at[i, c], 18 + i, partner) for i in range(8)]
    for copy in first_out:
        copy.wait_recv()
    k, v, q, g = [
        jnp.concatenate([local[i, 1], pair_buf[4 + i]], axis=0) for i in range(4)
    ]
    pair_scores[...] = nt(q, k)
    pair_wg[...] = nt(g, v)
    softmax_rows(
        2 * ROWS, 32, pair_scores, pair_wg, pair_w, pair_sg,
        lambda at, start, scores: scores * scale, lambda at, logit_grads: None,
    )
    weights, score_grads = pair_w[...], pair_sg[...]
    results = (
        nn(weights, v), nn(score_grads, k) * scale, tn(score_grads, q) * scale, tn(weights, g)
    )
    for i in range(4):
        ret_send[4 + i] = results[i][ROWS:].astype(BF)
        ret[4 + i].start()
        keep(4 + i, results[i][:ROWS])

    band_out[2].wait_recv()
    band_out[3].wait_recv()
    other += [pair_buf[2], pair_buf[3]]

    @pl.when(has_beyond)
    def _():
        for copy in own_halo:
            copy.wait_recv()

    attended, grad_q, gk_b, gv_b, pairs_b = band_block(
        1, other, own, "other", "own", -1, has_beyond
    )
    ret_send[0] = attended.astype(BF)
    ret_send[1] = grad_q.astype(BF)
    grad_send[1, 0] = gk_b[2 * ROWS :].astype(BF)
    grad_send[1, 1] = gv_b[2 * ROWS :].astype(BF)

    @pl.when(has_beyond)
    def _():
        back_far.start()

    ret[0].start()
    ret[1].start()
    own_gk = gk_a[:ROWS] + gk_b[ROWS : 2 * ROWS]
    own_gv = gv_a[:ROWS] + gv_b[ROWS : 2 * ROWS]
    other_gk = gk_b[:ROWS] + gk_a[ROWS : 2 * ROWS]
    other_gv = gv_b[:ROWS] + gv_a[ROWS : 2 * ROWS]

    turned = pairs_a + pairs_b
    line = lax.broadcasted_iota(jnp.int32, (D, D), 0)
    for bit in range(7):
        shift = 1 << bit
        rolled = jnp.concatenate([turned[:, shift:], turned[:, :shift]], axis=1)
        turned = jnp.where((line & shift) > 0, rolled, turned)
    sums = jnp.sum(turned, axis=0, keepdims=True)
    lane = lax.broadcasted_iota(jnp.int32, (1, D), 1)
    sums = jnp.where(lane == 0, 0.5 * sums, sums)
    sums = jnp.where(lane < BUCKETS - 1, sums, 0.0)
    sums = jnp.where(lane == BUCKETS - 1, -jnp.sum(sums, axis=1, keepdims=True), sums)
    tile_line = lax.broadcasted_iota(jnp.int32, (8, D), 0)
    bias_ctx[me] = jnp.where(tile_line == c, sums, 0.0)
    bias_out = []
    for step in range(1, ctx_count):
        copy = pltpu.make_async_remote_copy(
            src_ref=bias_ctx.at[me],
            dst_ref=bias_ctx.at[me],
            send_sem=bc_send.at[step],
            recv_sem=bc_recv.at[step],
            device_id=(row, lax.rem(me + step, ctx_count)),
            device_id_type=mesh_id,
        )
        copy.start()
        bias_out.append(copy)

    @pl.when(has_beyond)
    def _():
        back_out.wait_recv()

    @pl.when(has_out)
    def _():
        back_far.wait_recv()

    @pl.when(jnp.logical_not(has_beyond))
    def _():
        grad_buf[0] = jnp.zeros((2, ROWS, D), BF)

    @pl.when(jnp.logical_not(has_out))
    def _():
        grad_buf[1] = jnp.zeros((2, ROWS, D), BF)

    ret_send[2] = (other_gk + grad_buf[0, 0].astype(F32)).astype(BF)
    ret_send[3] = (other_gv + grad_buf[0, 1].astype(F32)).astype(BF)
    ret[2].start()
    ret[3].start()
    keep(2, own_gk + grad_buf[1, 0].astype(F32))
    keep(3, own_gv + grad_buf[1, 1].astype(F32))

    for copy in bias_out:
        copy.wait_recv()
    total = bias_ctx[0]
    for i in range(1, ctx_count):
        total = total + bias_ctx[i]
    bias_dp[row] = total
    docs_out = []
    for step in range(1, dp_count):
        copy = pltpu.make_async_remote_copy(
            src_ref=bias_dp.at[row],
            dst_ref=bias_dp.at[row],
            send_sem=bd_send.at[step],
            recv_sem=bd_recv.at[step],
            device_id=(lax.rem(row + step, dp_count), me),
            device_id_type=mesh_id,
        )
        copy.start()
        docs_out.append(copy)

    for copy in docs_out:
        copy.wait_recv()
    total = bias_dp[0]
    for i in range(1, dp_count):
        total = total + bias_dp[i]
    bias_ref[...] = total

    for copy in ret:
        copy.wait_recv()
    for copy in keeps:
        copy.wait()

    for copy in band_out + first_out + [clause_out, second_out, third_pair] + third_out + bias_out + docs_out + ret:
        copy.wait_send()

    @pl.when(has_out)
    def _():
        for copy in own_halo + [back_out]:
            copy.wait_send()

    @pl.when(has_beyond)
    def _():
        for copy in far_halo + [back_far]:
            copy.wait_send()


def layout_kernel(heads_ref, second_ref, third_ref, tile_ref, *outs):
    outs[4][...] = tile_ref[0:2, 0:BUCKETS]
    for i, out in enumerate(outs[:4]):
        for h in range(2):
            out[:, h * D : (h + 1) * D] = heads_ref[i, h]
            out[:, (2 + h) * D : (3 + h) * D] = heads_ref[4 + i, h]
            seconds = second_ref[i, :, h * D : (h + 1) * D].astype(BF)
            spread = tn(selector(32, DILATION_SECOND, h * DILATION_SECOND // 2), seconds)
            out[:, (4 + h) * D : (5 + h) * D] = spread.astype(BF)
            thirds = third_ref[i, :, h * D : (h + 1) * D].astype(BF)
            spread = tn(selector(8, DILATION_THIRD, h * DILATION_THIRD // 2), thirds)
            out[:, (6 + h) * D : (7 + h) * D] = spread.astype(BF)


def paired(ctx_count, dp_count, query, key, value, grad_out, clause, bias_table):
    vmem = pl.BlockSpec(memory_space=pltpu.VMEM)
    far = pl.BlockSpec(memory_space=pltpu.HBM)
    dma = pltpu.SemaphoreType.DMA
    block = (ROWS, D)
    heads, second, third, bias = pl.pallas_call(
        lambda *refs: main_kernel(ctx_count, dp_count, *refs),
        out_shape=[
            jax.ShapeDtypeStruct((8, 2) + block, BF),
            jax.ShapeDtypeStruct((4, 32, 2 * D), F32),
            jax.ShapeDtypeStruct((4, 8, 2 * D), F32),
            jax.ShapeDtypeStruct((8, D), F32),
        ],
        in_specs=[far] * 6,
        out_specs=[far] + [vmem] * 3,
        scratch_shapes=[
            pltpu.SMEM((2, BUCKETS), F32),
            pltpu.VMEM((1, ROWS), jnp.int32),
            pltpu.VMEM((4, 2) + block, BF),
            pltpu.VMEM((4, ROWS, 4 * D), BF),
            pltpu.VMEM((8,) + block, BF),
            dma((14,)),
            dma((8,)),
            pltpu.VMEM((8,) + block, BF),
            pltpu.VMEM((2, 2) + block, BF),
            pltpu.VMEM((2, 1, ROWS), jnp.int32),
            pltpu.VMEM((1, ROWS), jnp.int32),
            pltpu.VMEM((2, 2) + block, BF),
            pltpu.VMEM((2, 2) + block, BF),
            pltpu.VMEM((8,) + block, BF),
            pltpu.VMEM((2, 32, 8 * D), BF),
            pltpu.VMEM((ctx_count, 16, 4 * D), BF),
            pltpu.VMEM((ctx_count, 8, D), F32),
            pltpu.VMEM((dp_count, 8, D), F32),
            pltpu.VMEM((ROWS, 3 * ROWS), F32),
            pltpu.VMEM((ROWS, 3 * ROWS), F32),
            pltpu.VMEM((ROWS, 3 * ROWS), F32),
            pltpu.VMEM((ROWS, 3 * ROWS), BF),
            pltpu.VMEM((ROWS, 3 * ROWS), BF),
            pltpu.VMEM((ROWS, 3 * ROWS), BF),
            pltpu.VMEM((ROWS, 3 * ROWS), BF),
            pltpu.VMEM((2 * ROWS, 2 * ROWS), F32),
            pltpu.VMEM((2 * ROWS, 2 * ROWS), F32),
            pltpu.VMEM((2 * ROWS, 2 * ROWS), BF),
            pltpu.VMEM((2 * ROWS, 2 * ROWS), BF),
            dma((26,)),
            dma((26,)),
            dma((ctx_count,)),
            dma((ctx_count,)),
            dma((ctx_count,)),
            dma((ctx_count,)),
            dma((dp_count,)),
            dma((dp_count,)),
        ],
        compiler_params=pltpu.CompilerParams(
            collective_id=0, has_side_effects=True, vmem_limit_bytes=64 * 1024 * 1024
        ),
        name="attend",
    )(bias_table.T, clause, query[0], key[0], value[0], grad_out[0])
    outs = pl.pallas_call(
        layout_kernel,
        out_shape=[jax.ShapeDtypeStruct((ROWS, HEADS * D), BF)] * 4
        + [jax.ShapeDtypeStruct((2, BUCKETS), F32)],
        in_specs=[vmem] * 4,
        out_specs=[vmem] * 5,
        compiler_params=pltpu.CompilerParams(vmem_limit_bytes=64 * 1024 * 1024),
        name="layout",
    )(heads, second, third, bias)
    return tuple(out[None] for out in outs[:4]) + (outs[4].T,)


def solution(mesh):
    ctx_count, dp_count = mesh.shape["ctx"], mesh.shape["dp"]
    if ctx_count != 8:
        return general(mesh)
    spec = P("dp", "ctx", None)

    def body(*arrays):
        return paired(ctx_count, dp_count, *arrays)

    return jax.shard_map(
        body,
        mesh=mesh,
        in_specs=(spec, spec, spec, spec, P("dp", "ctx"), P()),
        out_specs=(spec, spec, spec, spec, P()),
        check_vma=False,
    )
```

```python
import jax
import jax.numpy as jnp
from jax import lax
from jax.experimental import pallas as pl
from jax.experimental.pallas import tpu as pltpu
from jax.sharding import PartitionSpec as P

HEADS = 8
WINDOW = 512
BUCKETS = 32
DILATION_FIRST = 1
DILATION_SECOND = 8
DILATION_THIRD = 32


def swapped(block, axis, bit):
    count = lax.axis_size(axis)
    route = []
    for low in range(count):
        high = low | 1 << bit
        if high != low and high < count:
            route += [(low, high), (high, low)]
    return lax.ppermute(block, axis, route)


def shifted(value, axis, steps):
    count = lax.axis_size(axis)
    leading, last = (max(0, -steps), min(count, count - steps))
    return lax.ppermute(value, axis, [(source, source + steps) for source in range(leading, last)])


def with_halo(shard, sides, width):
    for axis, dim in sides:
        size, length = (lax.axis_size(axis), shard.shape[dim])
        up = [(i, (i + 1) % size) for i in range(size - 1)]
        down = [(j, i) for i, j in up]
        last = lax.slice_in_dim(shard, length - width, length, axis=dim)
        leading = lax.slice_in_dim(shard, 0, width, axis=dim)
        before = lax.ppermute(last, axis, up)
        after = lax.ppermute(leading, axis, down)
        shard = jnp.concatenate([before, shard, after], axis=dim)
    return shard


def sample_rows(matrix, initial_flag, dilation_rate):
    count = matrix.shape[0] // dilation_rate
    head_dim = matrix.shape[1] // HEADS
    grid = matrix.reshape(count, dilation_rate, HEADS, head_dim)
    return jnp.concatenate(
        [grid[:, 0, initial_flag], grid[:, dilation_rate // 2, initial_flag + 1]], axis=1
    )


def spread_rows(sampled, dilation_rate):
    count = sampled.shape[0]
    grid = jnp.zeros((count, dilation_rate) + sampled.shape[1:], sampled.dtype)
    grid = grid.at[:, 0, 0].set(sampled[:, 0]).at[:, dilation_rate // 2, 1].set(sampled[:, 1])
    return grid.reshape((count * dilation_rate,) + sampled.shape[1:])


def upper_half(bit):
    index = lax.axis_index("ctx")
    return index // 2**bit % 2 == 1


def double_rows(block, bits):
    for bit in range(bits):
        other = swapped(block, "ctx", bit)
        block = jnp.where(
            upper_half(bit),
            jnp.concatenate([other, block], axis=0),
            jnp.concatenate([block, other], axis=0),
        )
    return block


def halve_sums(block, bits):
    for bit in reversed(range(bits)):
        half = block.shape[0] // 2
        lower, higher = (block[:half], block[half:])
        upper = upper_half(bit)
        outgoing = jnp.where(upper, lower, higher)
        staying = jnp.where(upper, higher, lower)
        block = staying + swapped(outgoing.astype(jnp.bfloat16), "ctx", bit).astype(outgoing.dtype)
    return block


def span_rows(block, bits):
    return double_rows(block, bits)


def span_sums(block, bits):
    return halve_sums(block, bits)


def rows_side(score_matrix, every_key_rows, every_value_rows, gradient_list, score_scale):
    top = jnp.max(score_matrix, axis=-1, keepdims=True)
    raised = jnp.exp(score_matrix - top)
    totals = jnp.sum(raised, axis=-1, keepdims=True)
    shares = raised / totals
    softmax_weights = shares.astype(jnp.bfloat16)
    attended = jnp.einsum(
        "ezb,beo->zeo", softmax_weights, every_value_rows, preferred_element_type=jnp.float32
    )
    weight_gradient = jnp.einsum(
        "wvx,yvx->vwy", gradient_list, every_value_rows, preferred_element_type=jnp.float32
    )
    delta = jnp.sum(shares * weight_gradient, axis=-1, keepdims=True)
    logit_grads = shares * (weight_gradient - delta)
    score_gradient = logit_grads.astype(jnp.bfloat16)
    query_gradient = (
        jnp.einsum(
            "ezb,beo->zeo", score_gradient, every_key_rows, preferred_element_type=jnp.float32
        )
        * score_scale
    )
    return (
        attended,
        query_gradient,
        softmax_weights,
        score_gradient,
        logit_grads,
        top,
        totals,
        delta,
    )


def keys_side(softmax_weights, score_gradient, query_matrix, gradient_list, score_scale):
    key_gradient = (
        jnp.einsum("vjb,jvw->bvw", score_gradient, query_matrix, preferred_element_type=jnp.float32)
        * score_scale
    )
    value_gradient = jnp.einsum(
        "vjb,jvw->bvw", softmax_weights, gradient_list, preferred_element_type=jnp.float32
    )
    return (key_gradient, value_gradient)


def bucket_lookup(bucket, table):
    running = jnp.zeros((table.shape[1],) + bucket.shape, jnp.float32)
    for level in range(BUCKETS):
        running = jnp.where(bucket[None] == level, table[level][:, None, None], running)
    return running


def bucket_sums(bucket, logit_grads):
    totals = [
        jnp.sum(jnp.where(bucket[None] == level, logit_grads, 0.0), axis=(1, 2))
        for level in range(BUCKETS)
    ]
    return jnp.stack(totals, axis=0)


def pass_rim(rim, offset):
    return shifted(rim.astype(jnp.bfloat16), "ctx", offset).astype(rim.dtype)


def band_part(query_rows, key_rows, value_rows, grad_rows, clause_rows, table, score_scale):
    rows, width = query_rows.shape
    head_dim = width // HEADS
    wide = 2 * head_dim
    half = WINDOW // 2
    pair_rows = jnp.concatenate([key_rows[:, :wide], value_rows[:, :wide]], axis=1)
    extended, extended_clause = (
        with_halo(pair_rows, (("ctx", 0),), half),
        with_halo(clause_rows, (("ctx", 0),), half),
    )
    reach = rows + 2 * half
    nearby_key_rows = extended[:, :wide].reshape(reach, 2, head_dim)
    values_near = extended[:, wide:].reshape(reach, 2, head_dim)
    query_matrix = query_rows[:, :wide].reshape(rows, 2, head_dim)
    gradient_list = grad_rows[:, :wide].reshape(rows, 2, head_dim)
    start = lax.axis_index("ctx") * rows
    length = rows * lax.axis_size("ctx")
    local_query = jnp.arange(rows)[:, None]
    local_key = jnp.arange(reach)[None, :] - half
    global_key = start + local_key
    allowed = (jnp.abs(local_query - local_key) < half) & (global_key >= 0) & (global_key < length)
    bucket = jnp.minimum(jnp.abs(clause_rows[:, None] - extended_clause[None, :]), BUCKETS - 1)
    score_matrix = (
        jnp.einsum(
            "wvx,yvx->vwy", query_matrix, nearby_key_rows, preferred_element_type=jnp.float32
        )
        * score_scale
    )
    score_matrix = jnp.where(allowed[None], score_matrix + bucket_lookup(bucket, table), -jnp.inf)
    attended, query_gradient, softmax_weights, score_gradient, logit_grads, top, totals, delta = (
        rows_side(score_matrix, nearby_key_rows, values_near, gradient_list, score_scale)
    )
    key_gradient, value_gradient = keys_side(
        softmax_weights, score_gradient, query_matrix, gradient_list, score_scale
    )
    sums = jnp.concatenate(
        [key_gradient.reshape(reach, wide), value_gradient.reshape(reach, wide)], axis=1
    )
    own = sums[half : half + rows]
    from_next = pass_rim(sums[:half], -1)
    from_prev = pass_rim(sums[half + rows :], 1)
    own = own.at[rows - half :].add(from_next).at[:half].add(from_prev)
    own_key = own[:, :wide].reshape(rows, 2, head_dim)
    own_value = own[:, wide:].reshape(rows, 2, head_dim)
    return (attended, query_gradient, own_key, own_value, bucket_sums(bucket, logit_grads))


def dilated(
    query_rows, key_rows, value_rows, grad_rows, initial_flag, dilation_rate, bits, score_scale
):
    head_dim = query_rows.shape[1] // HEADS
    wide = 2 * head_dim
    picked_query = sample_rows(query_rows, initial_flag, dilation_rate)
    picked_key = sample_rows(key_rows, initial_flag, dilation_rate)
    picked_value = sample_rows(value_rows, initial_flag, dilation_rate)
    picked_grad = sample_rows(grad_rows, initial_flag, dilation_rate)
    count = picked_query.shape[0]
    gathered = span_rows(jnp.concatenate([picked_key, picked_value], axis=1), bits)
    gathered_rows = gathered.shape[0]
    every_key_rows = gathered[:, :wide].reshape(gathered_rows, 2, head_dim)
    every_value_rows = gathered[:, wide:].reshape(gathered_rows, 2, head_dim)
    query_matrix = picked_query.reshape(count, 2, head_dim)
    gradient_list = picked_grad.reshape(count, 2, head_dim)
    score_matrix = (
        jnp.einsum("wvx,yvx->vwy", query_matrix, every_key_rows, preferred_element_type=jnp.float32)
        * score_scale
    )
    attended, query_gradient, softmax_weights, score_gradient, logit_grads, top, totals, delta = (
        rows_side(score_matrix, every_key_rows, every_value_rows, gradient_list, score_scale)
    )
    key_gradient, value_gradient = keys_side(
        softmax_weights, score_gradient, query_matrix, gradient_list, score_scale
    )
    partial_sums = jnp.concatenate(
        [key_gradient.reshape(gathered_rows, wide), value_gradient.reshape(gathered_rows, wide)],
        axis=1,
    )
    own = span_sums(partial_sums, bits)
    own_key = own[:, :wide].reshape(count, 2, head_dim)
    own_value = own[:, wide:].reshape(count, 2, head_dim)
    return (
        spread_rows(attended, dilation_rate),
        spread_rows(query_gradient, dilation_rate),
        spread_rows(own_key, dilation_rate),
        spread_rows(own_value, dilation_rate),
    )


def shards(query, key, value, grad_out, clause, bias_table):
    query_rows = query[0]
    key_rows = key[0]
    value_rows = value[0]
    grad_rows = grad_out[0]
    clause_rows = clause[0]
    rows, width = query_rows.shape
    head_dim = width // HEADS
    score_scale = head_dim ** (-0.5)
    bucket_bit_count = lax.axis_size("ctx").bit_length() - 1
    band = band_part(
        query_rows, key_rows, value_rows, grad_rows, clause_rows, bias_table, score_scale
    )
    pieces = [band[:4]]
    for initial_flag, dilation_rate, bits in (
        (2, DILATION_FIRST, max(bucket_bit_count - 5, 1)),
        (4, DILATION_SECOND, bucket_bit_count - 2),
        (6, DILATION_THIRD, bucket_bit_count),
    ):
        pieces.append(
            dilated(
                query_rows,
                key_rows,
                value_rows,
                grad_rows,
                initial_flag,
                dilation_rate,
                bits,
                score_scale,
            )
        )
    bias_grad = lax.psum(band[4], ("dp", "ctx"))
    joined = [
        jnp.concatenate([piece[slot] for piece in pieces], axis=1)
        .reshape(1, rows, width)
        .astype(jnp.bfloat16)
        for slot in range(4)
    ]
    return (joined[0], joined[1], joined[2], joined[3], bias_grad)


def general(mesh):
    in_specs = (
        P("dp", "ctx", None),
        P("dp", "ctx", None),
        P("dp", "ctx", None),
        P("dp", "ctx", None),
        P("dp", "ctx"),
        P(),
    )
    out_specs = (
        P("dp", "ctx", None),
        P("dp", "ctx", None),
        P("dp", "ctx", None),
        P("dp", "ctx", None),
        P(),
    )
    return jax.shard_map(shards, mesh=mesh, in_specs=in_specs, out_specs=out_specs, check_vma=False)


ROWS = 256
D = 128
BF = jnp.bfloat16
F32 = jnp.float32


def mm(a, b, dims):
    return lax.dot_general(a, b, (dims, ((), ())), preferred_element_type=F32)


def nt(a, b):
    return mm(a, b, ((1,), (1,)))


def nn(a, b):
    return mm(a, b, ((1,), (0,)))


def tn(a, b):
    return mm(a, b, ((0,), (0,)))


def halves(x):
    high = x.astype(BF)
    return high, (x - high.astype(F32)).astype(BF)


def softmax_grads(scores, q, k, v, g, scale):
    top = jnp.max(scores, axis=-1, keepdims=True)
    raised = jnp.exp(scores - top)
    shares = raised * (1.0 / jnp.sum(raised, axis=-1, keepdims=True))
    weights = shares.astype(BF)
    attended = nn(weights, v)
    weight_grads = nt(g, v)
    delta = jnp.sum(shares * weight_grads, axis=-1, keepdims=True)
    logit_grads = shares * (weight_grads - delta)
    score_grads = logit_grads.astype(BF)
    grad_q = nn(score_grads, k) * scale
    grad_k = tn(score_grads, q) * scale
    grad_v = tn(weights, g)
    return attended, grad_q, grad_k, grad_v, logit_grads


def softmax_rows(rows, chunk, score_ref, grad_ref, weight_ref, score_grad_ref, shape_scores, take_grads):
    for start in range(0, rows, chunk):
        at = pl.ds(start, chunk)
        scores = shape_scores(at, start, score_ref[at, :])
        top = jnp.max(scores, axis=-1, keepdims=True)
        raised = jnp.exp(scores - top)
        shares = raised * (1.0 / jnp.sum(raised, axis=-1, keepdims=True))
        weight_ref[at, :] = shares.astype(BF)
        weight_grads = grad_ref[at, :]
        delta = jnp.sum(shares * weight_grads, axis=-1, keepdims=True)
        logit_grads = shares * (weight_grads - delta)
        score_grad_ref[at, :] = logit_grads.astype(BF)
        take_grads(at, logit_grads)


def selector(count, step, offset):
    row = lax.broadcasted_iota(jnp.int32, (count, ROWS), 0)
    col = lax.broadcasted_iota(jnp.int32, (count, ROWS), 1)
    return (col == row * step + offset).astype(BF)


def clause_column(row_form):
    whole = jnp.broadcast_to(row_form[...], (8, ROWS))
    index = lax.broadcasted_iota(jnp.int32, whole.shape, 0)
    parts = jnp.where(index == 0, whole >> 6, jnp.where(index == 1, whole & 63, 0))
    line = lax.broadcasted_iota(jnp.int32, (8, D), 0)
    factor = jnp.where(line == 0, 64.0, jnp.where(line == 1, 1.0, 0.0))
    column = tn(parts.astype(F32).astype(BF), factor.astype(BF))
    return column.astype(jnp.int32)


def one_hot(column):
    lane = lax.broadcasted_iota(jnp.int32, (ROWS, D), 1)
    return (lane == (column & 127)).astype(F32).astype(BF)


def main_kernel(
    ctx_count, dp_count,
    table_hbm, clause_hbm, q_ref, k_ref, v_ref, g_ref,
    out_ref, second_out_ref, third_out_ref, bias_ref,
    second_ref, third_ref, table_ref, clause_ref, local, sampled, mine_send, local_sem, out_sem,
    pair_buf, halo_buf, halo_clause, pair_clause, grad_buf, grad_send, ret_send,
    s2, s3, bias_ctx, bias_dp,
    band_scores, band_bias, band_wg, band_w, band_sg, band_high, band_low, pair_scores, pair_wg, pair_w, pair_sg,
    send_sem, recv_sem, s3_send, s3_recv, bc_send, bc_recv, bd_send, bd_recv,
):
    me = lax.axis_index("ctx")
    row = lax.axis_index("dp")
    c = lax.rem(me, 2)
    partner = me + 1 - 2 * c
    outward = me - 2 + 4 * c
    beyond = me + 2 - 4 * c
    has_out = (outward >= 0) & (outward < ctx_count)
    has_beyond = (beyond >= 0) & (beyond < ctx_count)
    scale = D**-0.5
    mesh_id = pl.DeviceIdType.MESH

    def columns(head):
        return pl.ds(pl.multiple_of(head * D, D), D)

    inputs = (k_ref, v_ref, q_ref, g_ref)
    loads = [
        pltpu.make_async_copy(ref.at[:, columns(head)], local.at[i, j], local_sem.at[3 * i + j])
        for i, ref in enumerate(inputs)
        for j, head in enumerate((c, 2, 3))
    ]
    sample_loads = [
        pltpu.make_async_copy(ref.at[:, 4 * D :], sampled.at[i], local_sem.at[12 + i])
        for i, ref in enumerate(inputs)
    ]
    small_loads = [
        pltpu.make_async_copy(clause_hbm, clause_ref, local_sem.at[16]),
        pltpu.make_async_copy(table_hbm, table_ref, local_sem.at[17]),
    ]
    for copy in sample_loads + small_loads + loads:
        copy.start()

    barrier = pltpu.get_barrier_semaphore()
    for step in range(1, ctx_count):
        pl.semaphore_signal(
            barrier, inc=1, device_id=(row, lax.rem(me + step, ctx_count)), device_id_type=mesh_id
        )
    for step in range(1, dp_count):
        pl.semaphore_signal(
            barrier, inc=1, device_id=(lax.rem(row + step, dp_count), me), device_id_type=mesh_id
        )
    pl.semaphore_wait(barrier, ctx_count + dp_count - 2)

    def remote(src, dst, index, target):
        return pltpu.make_async_remote_copy(
            src_ref=src,
            dst_ref=dst,
            send_sem=send_sem.at[index],
            recv_sem=recv_sem.at[index],
            device_id=(row, target),
            device_id_type=mesh_id,
        )

    band_out = [
        remote(inputs[i].at[:, columns(1 - c)], pair_buf.at[i], i, partner) for i in range(4)
    ]
    first_out = [
        remote(inputs[i].at[:, columns(2 + h)], pair_buf.at[4 + 4 * h + i], 18 + 4 * h + i, partner)
        for h in range(2)
        for i in range(4)
    ]
    clause_out = remote(clause_hbm, pair_clause, 8, partner)
    own_halo = [
        remote(k_ref.at[:, columns(c)], halo_buf.at[1, 0], 9, outward),
        remote(v_ref.at[:, columns(c)], halo_buf.at[1, 1], 10, outward),
        remote(clause_hbm, halo_clause.at[1], 11, outward),
    ]
    far_halo = [
        remote(pair_buf.at[0], halo_buf.at[0, 0], 12, beyond),
        remote(pair_buf.at[1], halo_buf.at[0, 1], 13, beyond),
        remote(pair_clause, halo_clause.at[0], 14, beyond),
    ]

    clause_out.start()
    for copy in band_out[:2]:
        copy.start()

    @pl.when(has_out)
    def _():
        for copy in own_halo:
            copy.start()

    for copy in sample_loads:
        copy.wait()
    for i, ref in enumerate((sampled.at[2], sampled.at[0], sampled.at[1], sampled.at[3])):
        for h in range(2):
            part = nn(selector(32, DILATION_SECOND, h * DILATION_SECOND // 2), ref[:, h * D : (h + 1) * D])
            s2[0, :, (2 * i + h) * D : (2 * i + h + 1) * D] = part.astype(BF)

    def thirds(refs):
        return jnp.concatenate(
            [
                nn(selector(8, DILATION_THIRD, h * DILATION_THIRD // 2), ref[:, (2 + h) * D : (3 + h) * D])
                for ref in refs
                for h in range(2)
            ],
            axis=1,
        )

    s3[0] = jnp.concatenate([thirds((sampled.at[2], sampled.at[0])), thirds((sampled.at[1], sampled.at[3]))], axis=0).astype(BF)
    second_out = remote(s2.at[0], s2.at[1], 15, partner)
    second_out.start()
    third_pair = pltpu.make_async_remote_copy(
        src_ref=s3.at[0],
        dst_ref=s3.at[1],
        send_sem=s3_send.at[0],
        recv_sem=s3_recv.at[0],
        device_id=(row, partner),
        device_id_type=mesh_id,
    )
    third_pair.start()
    for copy in band_out[2:] + first_out[:4]:
        copy.start()

    for copy in small_loads:
        copy.wait()
    line = lax.broadcasted_iota(jnp.int32, (D, D), 0)
    lane = lax.broadcasted_iota(jnp.int32, (D, D), 1)
    apart = jnp.abs(((lane - line + 64) & 127) - 64)
    table = jnp.zeros((D, D), F32)
    for level in range(BUCKETS):
        table = jnp.where(apart == level, table_ref[c, level], table)
    far_bias = table_ref[c, BUCKETS - 1]
    table_high, table_low = halves(table)

    clause_out.wait_recv()
    band_out[0].wait_recv()
    band_out[1].wait_recv()

    @pl.when(has_beyond)
    def _():
        for copy in far_halo:
            copy.start()

    @pl.when(jnp.logical_not(has_out))
    def _():
        halo_buf[0] = jnp.zeros((2, ROWS, D), BF)
        halo_clause[0] = jnp.zeros((1, ROWS), jnp.int32)

    @pl.when(jnp.logical_not(has_beyond))
    def _():
        halo_buf[1] = jnp.zeros((2, ROWS, D), BF)
        halo_clause[1] = jnp.zeros((1, ROWS), jnp.int32)

    third_pair.wait_recv()
    third_out = []
    for step in range(1, ctx_count // 2):
        copy = pltpu.make_async_remote_copy(
            src_ref=s3.at[pl.ds(0, 2)],
            dst_ref=s3.at[pl.ds(ctx_count - 2 * step, 2)],
            send_sem=s3_send.at[step],
            recv_sem=s3_recv.at[step],
            device_id=(row, lax.rem(me + 2 * step, ctx_count)),
            device_id_type=mesh_id,
        )
        copy.start()
        third_out.append(copy)

    second_out.wait_recv()
    both = jnp.concatenate([s2[0], s2[1]], axis=0)
    for h in range(2):
        q, k, v, g = [both[:, (2 * i + h) * D : (2 * i + h + 1) * D] for i in range(4)]
        results = softmax_grads(nt(q, k) * scale, q, k, v, g, scale)[:4]
        for i in range(4):
            second_ref[i, :, h * D : (h + 1) * D] = results[i][:32]

    for copy in third_out:
        copy.wait_recv()
    blocks = [s3[i].astype(F32) for i in range(ctx_count)]
    upper = jnp.concatenate([block[:8] for block in blocks], axis=0).astype(BF)
    lower = jnp.concatenate([block[8:] for block in blocks], axis=0).astype(BF)
    for h in range(2):
        q, k = [upper[:, (2 * i + h) * D : (2 * i + h + 1) * D] for i in range(2)]
        v, g = [lower[:, (2 * i + h) * D : (2 * i + h + 1) * D] for i in range(2)]
        results = softmax_grads(nt(q, k) * scale, q, k, v, g, scale)[:4]
        for i in range(4):
            third_ref[i, :, h * D : (h + 1) * D] = results[i][:8]

    smalls = [
        pltpu.make_async_copy(second_ref, second_out_ref, out_sem.at[12]),
        pltpu.make_async_copy(third_ref, third_out_ref, out_sem.at[13]),
    ]
    for copy in smalls:
        copy.start()
    for copy in loads:
        copy.wait()
    own = [local[i, 0] for i in range(4)]
    other = [pair_buf[0], pair_buf[1]]
    clauses = {"own": clause_ref, "other": pair_clause}
    cols = {name: clause_column(ref) for name, ref in clauses.items()}
    hots = {name: one_hot(col) for name, col in cols.items()}
    def band_block(slot, mine, near, mine_name, near_name, sign, halo_valid):
        k = jnp.concatenate([mine[0], near[0], halo_buf[slot, 0]], axis=0)
        v = jnp.concatenate([mine[1], near[1], halo_buf[slot, 1]], axis=0)
        q, g = mine[2], mine[3]
        halo_hot = one_hot(clause_column(halo_clause.at[slot]))
        key_hot = jnp.concatenate([hots[mine_name], hots[near_name], halo_hot], axis=0)
        key_row = jnp.concatenate(
            [clauses[mine_name][0:1, :], clauses[near_name][0:1, :], halo_clause[slot, 0:1, :]],
            axis=1,
        )
        query_hot = hots[mine_name]
        spread = jnp.concatenate(
            [nn(query_hot, table_high).astype(BF), nn(query_hot, table_low).astype(BF)], axis=1
        )
        band_bias[...] = nt(spread, jnp.concatenate([key_hot, key_hot], axis=1))
        band_scores[...] = nt(q, k)
        band_wg[...] = nt(g, v)
        reach = jnp.where(halo_valid, 0, ROWS)
        col = cols[mine_name]
        turn = (1 - 2 * c) * sign
        chunk = 32

        def near_clauses(start):
            return jnp.abs(col[start : start + chunk, 0:1] - key_row) < BUCKETS - 1

        def shape_scores(at, start, scores):
            close = near_clauses(start)
            scores = scores * scale + jnp.where(close, band_bias[at, :], far_bias)
            row_index = lax.broadcasted_iota(jnp.int32, (chunk, ROWS), 0) + start
            col_index = lax.broadcasted_iota(jnp.int32, (chunk, ROWS), 1)
            signed = (row_index - col_index) * turn
            return jnp.concatenate(
                [
                    scores[:, :ROWS],
                    jnp.where(signed > 0, scores[:, ROWS : 2 * ROWS], -jnp.inf),
                    jnp.where(-signed > reach, scores[:, 2 * ROWS :], -jnp.inf),
                ],
                axis=1,
            )

        def take_grads(at, logit_grads):
            high, low = halves(jnp.where(near_clauses(at.start), logit_grads, 0.0))
            band_high[at, :] = high
            band_low[at, :] = low

        softmax_rows(ROWS, chunk, band_scores, band_wg, band_w, band_sg, shape_scores, take_grads)
        weights, score_grads = band_w[...], band_sg[...]
        attended = nn(weights, v)
        grad_q = nn(score_grads, k) * scale
        grad_k = tn(score_grads, q) * scale
        grad_v = tn(weights, g)
        by_clause = nn(band_high[...], key_hot) + nn(band_low[...], key_hot)
        high, low = halves(by_clause)
        pairs = tn(query_hot, high) + tn(query_hot, low) + tn(high, query_hot) + tn(low, query_hot)
        return attended, grad_q, grad_k, grad_v, pairs

    @pl.when(has_out)
    def _():
        for copy in far_halo:
            copy.wait_recv()

    attended, grad_q, gk_a, gv_a, pairs_a = band_block(
        0, own, other, "own", "other", 1, has_out
    )
    keeps = [
        pltpu.make_async_copy(mine_send.at[i], out_ref.at[i, c], out_sem.at[i]) for i in range(4)
    ] + [
        pltpu.make_async_copy(mine_send.at[4 + 4 * h + i], out_ref.at[4 + i, h], out_sem.at[4 + 4 * h + i])
        for h in range(2)
        for i in range(4)
    ]

    def keep(i, value):
        mine_send[i] = value.astype(BF)
        keeps[i].start()

    keep(0, attended)
    keep(1, grad_q)
    grad_send[0, 0] = gk_a[2 * ROWS :].astype(BF)
    grad_send[0, 1] = gv_a[2 * ROWS :].astype(BF)
    back_out = remote(grad_send.at[0], grad_buf.at[0], 16, outward)
    back_far = remote(grad_send.at[1], grad_buf.at[1], 17, beyond)

    @pl.when(has_out)
    def _():
        back_out.start()

    ret = [remote(ret_send.at[i], out_ref.at[i, c], 4 + i, partner) for i in range(4)]
    for copy in first_out[4:]:
        copy.start()
    band_out[2].wait_recv()
    band_out[3].wait_recv()
    other += [pair_buf[2], pair_buf[3]]

    @pl.when(has_beyond)
    def _():
        for copy in own_halo:
            copy.wait_recv()

    attended, grad_q, gk_b, gv_b, pairs_b = band_block(
        1, other, own, "other", "own", -1, has_beyond
    )
    ret_send[0] = attended.astype(BF)
    ret_send[1] = grad_q.astype(BF)
    grad_send[1, 0] = gk_b[2 * ROWS :].astype(BF)
    grad_send[1, 1] = gv_b[2 * ROWS :].astype(BF)

    @pl.when(has_beyond)
    def _():
        back_far.start()

    ret[0].start()
    ret[1].start()
    own_gk = gk_a[:ROWS] + gk_b[ROWS : 2 * ROWS]
    own_gv = gv_a[:ROWS] + gv_b[ROWS : 2 * ROWS]
    other_gk = gk_b[:ROWS] + gk_a[ROWS : 2 * ROWS]
    other_gv = gv_b[:ROWS] + gv_a[ROWS : 2 * ROWS]

    turned = pairs_a + pairs_b
    line = lax.broadcasted_iota(jnp.int32, (D, D), 0)
    for bit in range(7):
        shift = 1 << bit
        rolled = jnp.concatenate([turned[:, shift:], turned[:, :shift]], axis=1)
        turned = jnp.where((line & shift) > 0, rolled, turned)
    sums = jnp.sum(turned, axis=0, keepdims=True)
    lane = lax.broadcasted_iota(jnp.int32, (1, D), 1)
    sums = jnp.where(lane == 0, 0.5 * sums, sums)
    sums = jnp.where(lane < BUCKETS - 1, sums, 0.0)
    sums = jnp.where(lane == BUCKETS - 1, -jnp.sum(sums, axis=1, keepdims=True), sums)
    tile_line = lax.broadcasted_iota(jnp.int32, (8, D), 0)
    bias_ctx[me] = jnp.where(tile_line == c, sums, 0.0)
    bias_out = []
    for step in range(1, ctx_count):
        copy = pltpu.make_async_remote_copy(
            src_ref=bias_ctx.at[me],
            dst_ref=bias_ctx.at[me],
            send_sem=bc_send.at[step],
            recv_sem=bc_recv.at[step],
            device_id=(row, lax.rem(me + step, ctx_count)),
            device_id_type=mesh_id,
        )
        copy.start()
        bias_out.append(copy)

    def first_group(h):
        for copy in first_out[4 * h : 4 * h + 4]:
            copy.wait_recv()
        k, v, q, g = [
            jnp.concatenate([local[i, 1 + h], pair_buf[4 + 4 * h + i]], axis=0) for i in range(4)
        ]
        pair_scores[...] = nt(q, k)
        pair_wg[...] = nt(g, v)
        softmax_rows(
            2 * ROWS, 32, pair_scores, pair_wg, pair_w, pair_sg,
            lambda at, start, scores: scores * scale, lambda at, logit_grads: None,
        )
        keep(4 + 4 * h, nn(pair_w[:ROWS, :], v))
        keep(5 + 4 * h, nn(pair_sg[:ROWS, :], k) * scale)
        keep(6 + 4 * h, tn(pair_sg[:, :ROWS], q) * scale)
        keep(7 + 4 * h, tn(pair_w[:, :ROWS], g))

    first_group(0)

    @pl.when(has_beyond)
    def _():
        back_out.wait_recv()

    @pl.when(has_out)
    def _():
        back_far.wait_recv()

    @pl.when(jnp.logical_not(has_beyond))
    def _():
        grad_buf[0] = jnp.zeros((2, ROWS, D), BF)

    @pl.when(jnp.logical_not(has_out))
    def _():
        grad_buf[1] = jnp.zeros((2, ROWS, D), BF)

    ret_send[2] = (other_gk + grad_buf[0, 0].astype(F32)).astype(BF)
    ret_send[3] = (other_gv + grad_buf[0, 1].astype(F32)).astype(BF)
    ret[2].start()
    ret[3].start()
    keep(2, own_gk + grad_buf[1, 0].astype(F32))
    keep(3, own_gv + grad_buf[1, 1].astype(F32))

    for copy in bias_out:
        copy.wait_recv()
    total = bias_ctx[0]
    for i in range(1, ctx_count):
        total = total + bias_ctx[i]
    bias_dp[row] = total
    docs_out = []
    for step in range(1, dp_count):
        copy = pltpu.make_async_remote_copy(
            src_ref=bias_dp.at[row],
            dst_ref=bias_dp.at[row],
            send_sem=bd_send.at[step],
            recv_sem=bd_recv.at[step],
            device_id=(lax.rem(row + step, dp_count), me),
            device_id_type=mesh_id,
        )
        copy.start()
        docs_out.append(copy)

    first_group(1)

    for copy in docs_out:
        copy.wait_recv()
    total = bias_dp[0]
    for i in range(1, dp_count):
        total = total + bias_dp[i]
    bias_ref[...] = total

    for copy in ret:
        copy.wait_recv()
    for copy in keeps + smalls:
        copy.wait()

    for copy in band_out + first_out + [clause_out, second_out, third_pair] + third_out + bias_out + docs_out + ret:
        copy.wait_send()

    @pl.when(has_out)
    def _():
        for copy in own_halo + [back_out]:
            copy.wait_send()

    @pl.when(has_beyond)
    def _():
        for copy in far_halo + [back_far]:
            copy.wait_send()


def layout_kernel(heads_hbm, second_ref, third_ref, tile_ref, *refs):
    outs, bias_ref, heads, full, in_sem, out_sem = refs[:4], refs[4], *refs[5:]
    loads = [pltpu.make_async_copy(heads_hbm.at[i], heads.at[i], in_sem.at[i]) for i in range(8)]
    stores = [pltpu.make_async_copy(full.at[i], outs[i], out_sem.at[i]) for i in range(4)]
    for i in range(4):
        loads[i].start()
        loads[4 + i].start()
    bias_ref[...] = tile_ref[0:2, 0:BUCKETS]
    for i in range(4):
        for h in range(2):
            seconds = second_ref[i, :, h * D : (h + 1) * D].astype(BF)
            spread = tn(selector(32, DILATION_SECOND, h * DILATION_SECOND // 2), seconds)
            full[i, :, (4 + h) * D : (5 + h) * D] = spread.astype(BF)
            thirds = third_ref[i, :, h * D : (h + 1) * D].astype(BF)
            spread = tn(selector(8, DILATION_THIRD, h * DILATION_THIRD // 2), thirds)
            full[i, :, (6 + h) * D : (7 + h) * D] = spread.astype(BF)
        loads[i].wait()
        loads[4 + i].wait()
        for h in range(2):
            full[i, :, h * D : (h + 1) * D] = heads[i, h]
            full[i, :, (2 + h) * D : (3 + h) * D] = heads[4 + i, h]
        stores[i].start()
    for copy in stores:
        copy.wait()


def paired(ctx_count, dp_count, query, key, value, grad_out, clause, bias_table):
    vmem = pl.BlockSpec(memory_space=pltpu.VMEM)
    far = pl.BlockSpec(memory_space=pltpu.HBM)
    dma = pltpu.SemaphoreType.DMA
    block = (ROWS, D)
    heads, second, third, bias = pl.pallas_call(
        lambda *refs: main_kernel(ctx_count, dp_count, *refs),
        out_shape=[
            jax.ShapeDtypeStruct((8, 2) + block, BF),
            jax.ShapeDtypeStruct((4, 32, 2 * D), F32),
            jax.ShapeDtypeStruct((4, 8, 2 * D), F32),
            jax.ShapeDtypeStruct((8, D), F32),
        ],
        in_specs=[far] * 6,
        out_specs=[far] * 3 + [vmem],
        scratch_shapes=[
            pltpu.VMEM((4, 32, 2 * D), F32),
            pltpu.VMEM((4, 8, 2 * D), F32),
            pltpu.SMEM((2, BUCKETS), F32),
            pltpu.VMEM((1, ROWS), jnp.int32),
            pltpu.VMEM((4, 3) + block, BF),
            pltpu.VMEM((4, ROWS, 4 * D), BF),
            pltpu.VMEM((12,) + block, BF),
            dma((18,)),
            dma((14,)),
            pltpu.VMEM((12,) + block, BF),
            pltpu.VMEM((2, 2) + block, BF),
            pltpu.VMEM((2, 1, ROWS), jnp.int32),
            pltpu.VMEM((1, ROWS), jnp.int32),
            pltpu.VMEM((2, 2) + block, BF),
            pltpu.VMEM((2, 2) + block, BF),
            pltpu.VMEM((4,) + block, BF),
            pltpu.VMEM((2, 32, 8 * D), BF),
            pltpu.VMEM((ctx_count, 16, 4 * D), BF),
            pltpu.VMEM((ctx_count, 8, D), F32),
            pltpu.VMEM((dp_count, 8, D), F32),
            pltpu.VMEM((ROWS, 3 * ROWS), F32),
            pltpu.VMEM((ROWS, 3 * ROWS), F32),
            pltpu.VMEM((ROWS, 3 * ROWS), F32),
            pltpu.VMEM((ROWS, 3 * ROWS), BF),
            pltpu.VMEM((ROWS, 3 * ROWS), BF),
            pltpu.VMEM((ROWS, 3 * ROWS), BF),
            pltpu.VMEM((ROWS, 3 * ROWS), BF),
            pltpu.VMEM((2 * ROWS, 2 * ROWS), F32),
            pltpu.VMEM((2 * ROWS, 2 * ROWS), F32),
            pltpu.VMEM((2 * ROWS, 2 * ROWS), BF),
            pltpu.VMEM((2 * ROWS, 2 * ROWS), BF),
            dma((26,)),
            dma((26,)),
            dma((ctx_count,)),
            dma((ctx_count,)),
            dma((ctx_count,)),
            dma((ctx_count,)),
            dma((dp_count,)),
            dma((dp_count,)),
        ],
        compiler_params=pltpu.CompilerParams(
            collective_id=0, has_side_effects=True, vmem_limit_bytes=64 * 1024 * 1024
        ),
        name="attend",
    )(bias_table.T, clause, query[0], key[0], value[0], grad_out[0])
    outs = pl.pallas_call(
        layout_kernel,
        out_shape=[jax.ShapeDtypeStruct((ROWS, HEADS * D), BF)] * 4
        + [jax.ShapeDtypeStruct((2, BUCKETS), F32)],
        in_specs=[far] + [vmem] * 3,
        out_specs=[far] * 4 + [vmem],
        scratch_shapes=[
            pltpu.VMEM((8, 2) + block, BF),
            pltpu.VMEM((4, ROWS, HEADS * D), BF),
            dma((8,)),
            dma((4,)),
        ],
        compiler_params=pltpu.CompilerParams(vmem_limit_bytes=64 * 1024 * 1024),
        name="layout",
    )(heads, second, third, bias)
    return tuple(out[None] for out in outs[:4]) + (outs[4].T,)


def solution(mesh):
    ctx_count, dp_count = mesh.shape["ctx"], mesh.shape["dp"]
    if ctx_count != 8:
        return general(mesh)
    spec = P("dp", "ctx", None)

    def body(*arrays):
        return paired(ctx_count, dp_count, *arrays)

    return jax.shard_map(
        body,
        mesh=mesh,
        in_specs=(spec, spec, spec, spec, P("dp", "ctx"), P()),
        out_specs=(spec, spec, spec, spec, P()),
        check_vma=False,
    )
```

```python
import jax
import jax.numpy as jnp
from jax import lax
from jax.experimental import pallas as pl
from jax.experimental.pallas import tpu as pltpu
from jax.sharding import PartitionSpec as P

HEADS = 8
WINDOW = 512
BUCKETS = 32
DILATION_FIRST = 1
DILATION_SECOND = 8
DILATION_THIRD = 32


def swapped(block, axis, bit):
    count = lax.axis_size(axis)
    route = []
    for low in range(count):
        high = low | 1 << bit
        if high != low and high < count:
            route += [(low, high), (high, low)]
    return lax.ppermute(block, axis, route)


def shifted(value, axis, steps):
    count = lax.axis_size(axis)
    leading, last = (max(0, -steps), min(count, count - steps))
    return lax.ppermute(value, axis, [(source, source + steps) for source in range(leading, last)])


def with_halo(shard, sides, width):
    for axis, dim in sides:
        size, length = (lax.axis_size(axis), shard.shape[dim])
        up = [(i, (i + 1) % size) for i in range(size - 1)]
        down = [(j, i) for i, j in up]
        last = lax.slice_in_dim(shard, length - width, length, axis=dim)
        leading = lax.slice_in_dim(shard, 0, width, axis=dim)
        before = lax.ppermute(last, axis, up)
        after = lax.ppermute(leading, axis, down)
        shard = jnp.concatenate([before, shard, after], axis=dim)
    return shard


def sample_rows(matrix, initial_flag, dilation_rate):
    count = matrix.shape[0] // dilation_rate
    head_dim = matrix.shape[1] // HEADS
    grid = matrix.reshape(count, dilation_rate, HEADS, head_dim)
    return jnp.concatenate(
        [grid[:, 0, initial_flag], grid[:, dilation_rate // 2, initial_flag + 1]], axis=1
    )


def spread_rows(sampled, dilation_rate):
    count = sampled.shape[0]
    grid = jnp.zeros((count, dilation_rate) + sampled.shape[1:], sampled.dtype)
    grid = grid.at[:, 0, 0].set(sampled[:, 0]).at[:, dilation_rate // 2, 1].set(sampled[:, 1])
    return grid.reshape((count * dilation_rate,) + sampled.shape[1:])


def upper_half(bit):
    index = lax.axis_index("ctx")
    return index // 2**bit % 2 == 1


def double_rows(block, bits):
    for bit in range(bits):
        other = swapped(block, "ctx", bit)
        block = jnp.where(
            upper_half(bit),
            jnp.concatenate([other, block], axis=0),
            jnp.concatenate([block, other], axis=0),
        )
    return block


def halve_sums(block, bits):
    for bit in reversed(range(bits)):
        half = block.shape[0] // 2
        lower, higher = (block[:half], block[half:])
        upper = upper_half(bit)
        outgoing = jnp.where(upper, lower, higher)
        staying = jnp.where(upper, higher, lower)
        block = staying + swapped(outgoing.astype(jnp.bfloat16), "ctx", bit).astype(outgoing.dtype)
    return block


def span_rows(block, bits):
    return double_rows(block, bits)


def span_sums(block, bits):
    return halve_sums(block, bits)


def rows_side(score_matrix, every_key_rows, every_value_rows, gradient_list, score_scale):
    top = jnp.max(score_matrix, axis=-1, keepdims=True)
    raised = jnp.exp(score_matrix - top)
    totals = jnp.sum(raised, axis=-1, keepdims=True)
    shares = raised / totals
    softmax_weights = shares.astype(jnp.bfloat16)
    attended = jnp.einsum(
        "ezb,beo->zeo", softmax_weights, every_value_rows, preferred_element_type=jnp.float32
    )
    weight_gradient = jnp.einsum(
        "wvx,yvx->vwy", gradient_list, every_value_rows, preferred_element_type=jnp.float32
    )
    delta = jnp.sum(shares * weight_gradient, axis=-1, keepdims=True)
    logit_grads = shares * (weight_gradient - delta)
    score_gradient = logit_grads.astype(jnp.bfloat16)
    query_gradient = (
        jnp.einsum(
            "ezb,beo->zeo", score_gradient, every_key_rows, preferred_element_type=jnp.float32
        )
        * score_scale
    )
    return (
        attended,
        query_gradient,
        softmax_weights,
        score_gradient,
        logit_grads,
        top,
        totals,
        delta,
    )


def keys_side(softmax_weights, score_gradient, query_matrix, gradient_list, score_scale):
    key_gradient = (
        jnp.einsum("vjb,jvw->bvw", score_gradient, query_matrix, preferred_element_type=jnp.float32)
        * score_scale
    )
    value_gradient = jnp.einsum(
        "vjb,jvw->bvw", softmax_weights, gradient_list, preferred_element_type=jnp.float32
    )
    return (key_gradient, value_gradient)


def bucket_lookup(bucket, table):
    running = jnp.zeros((table.shape[1],) + bucket.shape, jnp.float32)
    for level in range(BUCKETS):
        running = jnp.where(bucket[None] == level, table[level][:, None, None], running)
    return running


def bucket_sums(bucket, logit_grads):
    totals = [
        jnp.sum(jnp.where(bucket[None] == level, logit_grads, 0.0), axis=(1, 2))
        for level in range(BUCKETS)
    ]
    return jnp.stack(totals, axis=0)


def pass_rim(rim, offset):
    return shifted(rim.astype(jnp.bfloat16), "ctx", offset).astype(rim.dtype)


def band_part(query_rows, key_rows, value_rows, grad_rows, clause_rows, table, score_scale):
    rows, width = query_rows.shape
    head_dim = width // HEADS
    wide = 2 * head_dim
    half = WINDOW // 2
    pair_rows = jnp.concatenate([key_rows[:, :wide], value_rows[:, :wide]], axis=1)
    extended, extended_clause = (
        with_halo(pair_rows, (("ctx", 0),), half),
        with_halo(clause_rows, (("ctx", 0),), half),
    )
    reach = rows + 2 * half
    nearby_key_rows = extended[:, :wide].reshape(reach, 2, head_dim)
    values_near = extended[:, wide:].reshape(reach, 2, head_dim)
    query_matrix = query_rows[:, :wide].reshape(rows, 2, head_dim)
    gradient_list = grad_rows[:, :wide].reshape(rows, 2, head_dim)
    start = lax.axis_index("ctx") * rows
    length = rows * lax.axis_size("ctx")
    local_query = jnp.arange(rows)[:, None]
    local_key = jnp.arange(reach)[None, :] - half
    global_key = start + local_key
    allowed = (jnp.abs(local_query - local_key) < half) & (global_key >= 0) & (global_key < length)
    bucket = jnp.minimum(jnp.abs(clause_rows[:, None] - extended_clause[None, :]), BUCKETS - 1)
    score_matrix = (
        jnp.einsum(
            "wvx,yvx->vwy", query_matrix, nearby_key_rows, preferred_element_type=jnp.float32
        )
        * score_scale
    )
    score_matrix = jnp.where(allowed[None], score_matrix + bucket_lookup(bucket, table), -jnp.inf)
    attended, query_gradient, softmax_weights, score_gradient, logit_grads, top, totals, delta = (
        rows_side(score_matrix, nearby_key_rows, values_near, gradient_list, score_scale)
    )
    key_gradient, value_gradient = keys_side(
        softmax_weights, score_gradient, query_matrix, gradient_list, score_scale
    )
    sums = jnp.concatenate(
        [key_gradient.reshape(reach, wide), value_gradient.reshape(reach, wide)], axis=1
    )
    own = sums[half : half + rows]
    from_next = pass_rim(sums[:half], -1)
    from_prev = pass_rim(sums[half + rows :], 1)
    own = own.at[rows - half :].add(from_next).at[:half].add(from_prev)
    own_key = own[:, :wide].reshape(rows, 2, head_dim)
    own_value = own[:, wide:].reshape(rows, 2, head_dim)
    return (attended, query_gradient, own_key, own_value, bucket_sums(bucket, logit_grads))


def dilated(
    query_rows, key_rows, value_rows, grad_rows, initial_flag, dilation_rate, bits, score_scale
):
    head_dim = query_rows.shape[1] // HEADS
    wide = 2 * head_dim
    picked_query = sample_rows(query_rows, initial_flag, dilation_rate)
    picked_key = sample_rows(key_rows, initial_flag, dilation_rate)
    picked_value = sample_rows(value_rows, initial_flag, dilation_rate)
    picked_grad = sample_rows(grad_rows, initial_flag, dilation_rate)
    count = picked_query.shape[0]
    gathered = span_rows(jnp.concatenate([picked_key, picked_value], axis=1), bits)
    gathered_rows = gathered.shape[0]
    every_key_rows = gathered[:, :wide].reshape(gathered_rows, 2, head_dim)
    every_value_rows = gathered[:, wide:].reshape(gathered_rows, 2, head_dim)
    query_matrix = picked_query.reshape(count, 2, head_dim)
    gradient_list = picked_grad.reshape(count, 2, head_dim)
    score_matrix = (
        jnp.einsum("wvx,yvx->vwy", query_matrix, every_key_rows, preferred_element_type=jnp.float32)
        * score_scale
    )
    attended, query_gradient, softmax_weights, score_gradient, logit_grads, top, totals, delta = (
        rows_side(score_matrix, every_key_rows, every_value_rows, gradient_list, score_scale)
    )
    key_gradient, value_gradient = keys_side(
        softmax_weights, score_gradient, query_matrix, gradient_list, score_scale
    )
    partial_sums = jnp.concatenate(
        [key_gradient.reshape(gathered_rows, wide), value_gradient.reshape(gathered_rows, wide)],
        axis=1,
    )
    own = span_sums(partial_sums, bits)
    own_key = own[:, :wide].reshape(count, 2, head_dim)
    own_value = own[:, wide:].reshape(count, 2, head_dim)
    return (
        spread_rows(attended, dilation_rate),
        spread_rows(query_gradient, dilation_rate),
        spread_rows(own_key, dilation_rate),
        spread_rows(own_value, dilation_rate),
    )


def shards(query, key, value, grad_out, clause, bias_table):
    query_rows = query[0]
    key_rows = key[0]
    value_rows = value[0]
    grad_rows = grad_out[0]
    clause_rows = clause[0]
    rows, width = query_rows.shape
    head_dim = width // HEADS
    score_scale = head_dim ** (-0.5)
    bucket_bit_count = lax.axis_size("ctx").bit_length() - 1
    band = band_part(
        query_rows, key_rows, value_rows, grad_rows, clause_rows, bias_table, score_scale
    )
    pieces = [band[:4]]
    for initial_flag, dilation_rate, bits in (
        (2, DILATION_FIRST, max(bucket_bit_count - 5, 1)),
        (4, DILATION_SECOND, bucket_bit_count - 2),
        (6, DILATION_THIRD, bucket_bit_count),
    ):
        pieces.append(
            dilated(
                query_rows,
                key_rows,
                value_rows,
                grad_rows,
                initial_flag,
                dilation_rate,
                bits,
                score_scale,
            )
        )
    bias_grad = lax.psum(band[4], ("dp", "ctx"))
    joined = [
        jnp.concatenate([piece[slot] for piece in pieces], axis=1)
        .reshape(1, rows, width)
        .astype(jnp.bfloat16)
        for slot in range(4)
    ]
    return (joined[0], joined[1], joined[2], joined[3], bias_grad)


def general(mesh):
    in_specs = (
        P("dp", "ctx", None),
        P("dp", "ctx", None),
        P("dp", "ctx", None),
        P("dp", "ctx", None),
        P("dp", "ctx"),
        P(),
    )
    out_specs = (
        P("dp", "ctx", None),
        P("dp", "ctx", None),
        P("dp", "ctx", None),
        P("dp", "ctx", None),
        P(),
    )
    return jax.shard_map(shards, mesh=mesh, in_specs=in_specs, out_specs=out_specs, check_vma=False)


ROWS = 256
D = 128
BF = jnp.bfloat16
F32 = jnp.float32


def mm(a, b, dims):
    return lax.dot_general(a, b, (dims, ((), ())), preferred_element_type=F32)


def nt(a, b):
    return mm(a, b, ((1,), (1,)))


def nn(a, b):
    return mm(a, b, ((1,), (0,)))


def tn(a, b):
    return mm(a, b, ((0,), (0,)))


def halves(x):
    high = x.astype(BF)
    return high, (x - high.astype(F32)).astype(BF)


def softmax_grads(scores, q, k, v, g, scale):
    top = jnp.max(scores, axis=-1, keepdims=True)
    raised = jnp.exp(scores - top)
    shares = raised * (1.0 / jnp.sum(raised, axis=-1, keepdims=True))
    weights = shares.astype(BF)
    attended = nn(weights, v)
    weight_grads = nt(g, v)
    delta = jnp.sum(shares * weight_grads, axis=-1, keepdims=True)
    logit_grads = shares * (weight_grads - delta)
    score_grads = logit_grads.astype(BF)
    grad_q = nn(score_grads, k) * scale
    grad_k = tn(score_grads, q) * scale
    grad_v = tn(weights, g)
    return attended, grad_q, grad_k, grad_v, logit_grads


def softmax_rows(rows, chunk, score_ref, grad_ref, weight_ref, score_grad_ref, shape_scores, take_grads):
    for start in range(0, rows, chunk):
        at = pl.ds(start, chunk)
        scores = shape_scores(at, start, score_ref[at, :])
        top = jnp.max(scores, axis=-1, keepdims=True)
        raised = jnp.exp(scores - top)
        shares = raised * (1.0 / jnp.sum(raised, axis=-1, keepdims=True))
        weight_ref[at, :] = shares.astype(BF)
        weight_grads = grad_ref[at, :]
        delta = jnp.sum(shares * weight_grads, axis=-1, keepdims=True)
        logit_grads = shares * (weight_grads - delta)
        score_grad_ref[at, :] = logit_grads.astype(BF)
        take_grads(at, logit_grads)


def selector(count, step, offset):
    row = lax.broadcasted_iota(jnp.int32, (count, ROWS), 0)
    col = lax.broadcasted_iota(jnp.int32, (count, ROWS), 1)
    return (col == row * step + offset).astype(BF)


def clause_column(row_form):
    whole = jnp.broadcast_to(row_form[...], (8, ROWS))
    index = lax.broadcasted_iota(jnp.int32, whole.shape, 0)
    parts = jnp.where(index == 0, whole >> 6, jnp.where(index == 1, whole & 63, 0))
    line = lax.broadcasted_iota(jnp.int32, (8, D), 0)
    factor = jnp.where(line == 0, 64.0, jnp.where(line == 1, 1.0, 0.0))
    column = tn(parts.astype(F32).astype(BF), factor.astype(BF))
    return column.astype(jnp.int32)


def one_hot(column):
    lane = lax.broadcasted_iota(jnp.int32, (ROWS, D), 1)
    return (lane == (column & 127)).astype(F32).astype(BF)


def main_kernel(
    ctx_count, dp_count,
    table_hbm, clause_hbm, q_ref, k_ref, v_ref, g_ref,
    out_ref, second_out_ref, third_out_ref, bias_ref,
    second_ref, third_ref, table_ref, clause_ref, local, sampled, mine_send, local_sem, out_sem,
    pair_buf, halo_buf, halo_clause, pair_clause, grad_buf, grad_send, ret_send,
    s2, s3, bias_ctx, bias_dp,
    band_scores, band_bias, band_wg, band_w, band_sg, band_high, band_low, pair_scores, pair_wg, pair_w, pair_sg,
    send_sem, recv_sem, s3_send, s3_recv, bc_send, bc_recv, bd_send, bd_recv,
):
    me = lax.axis_index("ctx")
    row = lax.axis_index("dp")
    c = lax.rem(me, 2)
    partner = me + 1 - 2 * c
    outward = me - 2 + 4 * c
    beyond = me + 2 - 4 * c
    has_out = (outward >= 0) & (outward < ctx_count)
    has_beyond = (beyond >= 0) & (beyond < ctx_count)
    scale = D**-0.5
    mesh_id = pl.DeviceIdType.MESH

    def columns(head):
        return pl.ds(pl.multiple_of(head * D, D), D)

    inputs = (k_ref, v_ref, q_ref, g_ref)
    parts = [
        [
            pltpu.make_async_copy(ref.at[:, columns(head)], local.at[j, i], local_sem.at[4 * j + i])
            for i, ref in enumerate(inputs)
        ]
        for j, head in enumerate((c, 2, 3, 1 - c))
    ]
    sample_loads = [
        pltpu.make_async_copy(ref.at[:, 4 * D :], sampled.at[i], local_sem.at[16 + i])
        for i, ref in enumerate(inputs)
    ]
    small_loads = [
        pltpu.make_async_copy(clause_hbm, clause_ref, local_sem.at[20]),
        pltpu.make_async_copy(table_hbm, table_ref, local_sem.at[21]),
    ]
    for copy in parts[3] + parts[0][:2] + sample_loads + small_loads + parts[1] + parts[2] + parts[0][2:]:
        copy.start()

    barrier = pltpu.get_barrier_semaphore()
    for step in range(1, ctx_count):
        pl.semaphore_signal(
            barrier, inc=1, device_id=(row, lax.rem(me + step, ctx_count)), device_id_type=mesh_id
        )
    for step in range(1, dp_count):
        pl.semaphore_signal(
            barrier, inc=1, device_id=(lax.rem(row + step, dp_count), me), device_id_type=mesh_id
        )
    pl.semaphore_wait(barrier, ctx_count + dp_count - 2)

    def remote(src, dst, index, target):
        return pltpu.make_async_remote_copy(
            src_ref=src,
            dst_ref=dst,
            send_sem=send_sem.at[index],
            recv_sem=recv_sem.at[index],
            device_id=(row, target),
            device_id_type=mesh_id,
        )

    band_out = [
        remote(local.at[3, pl.ds(2 * i, 2)], pair_buf.at[pl.ds(2 * i, 2)], i, partner) for i in range(2)
    ]
    first_out = [
        remote(local.at[1 + h], pair_buf.at[pl.ds(4 + 4 * h, 4)], 2 + h, partner) for h in range(2)
    ]
    clause_out = remote(clause_hbm, pair_clause, 8, partner)
    own_halo = [
        remote(local.at[0, pl.ds(0, 2)], halo_buf.at[1], 9, outward),
        remote(clause_hbm, halo_clause.at[1], 11, outward),
    ]
    far_halo = [
        remote(pair_buf.at[pl.ds(0, 2)], halo_buf.at[0], 12, beyond),
        remote(pair_clause, halo_clause.at[0], 14, beyond),
    ]

    clause_out.start()
    for copy in parts[3][:2]:
        copy.wait()
    band_out[0].start()
    for copy in parts[0][:2]:
        copy.wait()

    @pl.when(has_out)
    def _():
        for copy in own_halo:
            copy.start()

    for copy in sample_loads:
        copy.wait()
    for i, ref in enumerate((sampled.at[2], sampled.at[0], sampled.at[1], sampled.at[3])):
        for h in range(2):
            part = nn(selector(32, DILATION_SECOND, h * DILATION_SECOND // 2), ref[:, h * D : (h + 1) * D])
            s2[0, :, (2 * i + h) * D : (2 * i + h + 1) * D] = part.astype(BF)

    def thirds(refs):
        return jnp.concatenate(
            [
                nn(selector(8, DILATION_THIRD, h * DILATION_THIRD // 2), ref[:, (2 + h) * D : (3 + h) * D])
                for ref in refs
                for h in range(2)
            ],
            axis=1,
        )

    s3[0] = jnp.concatenate([thirds((sampled.at[2], sampled.at[0])), thirds((sampled.at[1], sampled.at[3]))], axis=0).astype(BF)
    second_out = remote(s2.at[0], s2.at[1], 15, partner)
    second_out.start()
    third_pair = pltpu.make_async_remote_copy(
        src_ref=s3.at[0],
        dst_ref=s3.at[1],
        send_sem=s3_send.at[0],
        recv_sem=s3_recv.at[0],
        device_id=(row, partner),
        device_id_type=mesh_id,
    )
    third_pair.start()
    for copy in parts[3][2:]:
        copy.wait()
    band_out[1].start()
    for copy in parts[1]:
        copy.wait()
    first_out[0].start()

    for copy in small_loads:
        copy.wait()
    line = lax.broadcasted_iota(jnp.int32, (D, D), 0)
    lane = lax.broadcasted_iota(jnp.int32, (D, D), 1)
    apart = jnp.abs(((lane - line + 64) & 127) - 64)
    table = jnp.zeros((D, D), F32)
    for level in range(BUCKETS):
        table = jnp.where(apart == level, table_ref[c, level], table)
    far_bias = table_ref[c, BUCKETS - 1]
    table_high, table_low = halves(table)

    clause_out.wait_recv()
    band_out[0].wait_recv()

    @pl.when(has_beyond)
    def _():
        for copy in far_halo:
            copy.start()

    @pl.when(jnp.logical_not(has_out))
    def _():
        halo_buf[0] = jnp.zeros((2, ROWS, D), BF)
        halo_clause[0] = jnp.zeros((1, ROWS), jnp.int32)

    @pl.when(jnp.logical_not(has_beyond))
    def _():
        halo_buf[1] = jnp.zeros((2, ROWS, D), BF)
        halo_clause[1] = jnp.zeros((1, ROWS), jnp.int32)

    third_pair.wait_recv()
    third_out = []
    for step in range(1, ctx_count // 2):
        copy = pltpu.make_async_remote_copy(
            src_ref=s3.at[pl.ds(0, 2)],
            dst_ref=s3.at[pl.ds(ctx_count - 2 * step, 2)],
            send_sem=s3_send.at[step],
            recv_sem=s3_recv.at[step],
            device_id=(row, lax.rem(me + 2 * step, ctx_count)),
            device_id_type=mesh_id,
        )
        copy.start()
        third_out.append(copy)

    second_out.wait_recv()
    both = jnp.concatenate([s2[0], s2[1]], axis=0)
    for h in range(2):
        q, k, v, g = [both[:, (2 * i + h) * D : (2 * i + h + 1) * D] for i in range(4)]
        results = softmax_grads(nt(q, k) * scale, q, k, v, g, scale)[:4]
        for i in range(4):
            second_ref[i, :, h * D : (h + 1) * D] = results[i][:32]

    for copy in third_out:
        copy.wait_recv()
    blocks = [s3[i].astype(F32) for i in range(ctx_count)]
    upper = jnp.concatenate([block[:8] for block in blocks], axis=0).astype(BF)
    lower = jnp.concatenate([block[8:] for block in blocks], axis=0).astype(BF)
    for h in range(2):
        q, k = [upper[:, (2 * i + h) * D : (2 * i + h + 1) * D] for i in range(2)]
        v, g = [lower[:, (2 * i + h) * D : (2 * i + h + 1) * D] for i in range(2)]
        results = softmax_grads(nt(q, k) * scale, q, k, v, g, scale)[:4]
        for i in range(4):
            third_ref[i, :, h * D : (h + 1) * D] = results[i][:8]

    smalls = [
        pltpu.make_async_copy(second_ref, second_out_ref, out_sem.at[12]),
        pltpu.make_async_copy(third_ref, third_out_ref, out_sem.at[13]),
    ]
    for copy in smalls:
        copy.start()
    for copy in parts[2] + parts[0][2:]:
        copy.wait()
    own = [local[0, i] for i in range(4)]
    other = [pair_buf[0], pair_buf[1]]
    clauses = {"own": clause_ref, "other": pair_clause}
    cols = {name: clause_column(ref) for name, ref in clauses.items()}
    hots = {name: one_hot(col) for name, col in cols.items()}
    def band_block(slot, mine, near, mine_name, near_name, sign, halo_valid):
        k = jnp.concatenate([mine[0], near[0], halo_buf[slot, 0]], axis=0)
        v = jnp.concatenate([mine[1], near[1], halo_buf[slot, 1]], axis=0)
        q, g = mine[2], mine[3]
        halo_hot = one_hot(clause_column(halo_clause.at[slot]))
        key_hot = jnp.concatenate([hots[mine_name], hots[near_name], halo_hot], axis=0)
        key_row = jnp.concatenate(
            [clauses[mine_name][0:1, :], clauses[near_name][0:1, :], halo_clause[slot, 0:1, :]],
            axis=1,
        )
        query_hot = hots[mine_name]
        spread = jnp.concatenate(
            [nn(query_hot, table_high).astype(BF), nn(query_hot, table_low).astype(BF)], axis=1
        )
        band_bias[...] = nt(spread, jnp.concatenate([key_hot, key_hot], axis=1))
        band_scores[...] = nt(q, k)
        band_wg[...] = nt(g, v)
        reach = jnp.where(halo_valid, 0, ROWS)
        col = cols[mine_name]
        turn = (1 - 2 * c) * sign
        chunk = 32

        def near_clauses(start):
            return jnp.abs(col[start : start + chunk, 0:1] - key_row) < BUCKETS - 1

        def shape_scores(at, start, scores):
            close = near_clauses(start)
            scores = scores * scale + jnp.where(close, band_bias[at, :], far_bias)
            row_index = lax.broadcasted_iota(jnp.int32, (chunk, ROWS), 0) + start
            col_index = lax.broadcasted_iota(jnp.int32, (chunk, ROWS), 1)
            signed = (row_index - col_index) * turn
            return jnp.concatenate(
                [
                    scores[:, :ROWS],
                    jnp.where(signed > 0, scores[:, ROWS : 2 * ROWS], -jnp.inf),
                    jnp.where(-signed > reach, scores[:, 2 * ROWS :], -jnp.inf),
                ],
                axis=1,
            )

        def take_grads(at, logit_grads):
            high, low = halves(jnp.where(near_clauses(at.start), logit_grads, 0.0))
            band_high[at, :] = high
            band_low[at, :] = low

        softmax_rows(ROWS, chunk, band_scores, band_wg, band_w, band_sg, shape_scores, take_grads)
        weights, score_grads = band_w[...], band_sg[...]
        attended = nn(weights, v)
        grad_q = nn(score_grads, k) * scale
        grad_k = tn(score_grads, q) * scale
        grad_v = tn(weights, g)
        by_clause = nn(band_high[...], key_hot) + nn(band_low[...], key_hot)
        high, low = halves(by_clause)
        pairs = tn(query_hot, high) + tn(query_hot, low) + tn(high, query_hot) + tn(low, query_hot)
        return attended, grad_q, grad_k, grad_v, pairs

    @pl.when(has_out)
    def _():
        for copy in far_halo:
            copy.wait_recv()

    attended, grad_q, gk_a, gv_a, pairs_a = band_block(
        0, own, other, "own", "other", 1, has_out
    )
    keeps = [
        pltpu.make_async_copy(mine_send.at[i], out_ref.at[i, c], out_sem.at[i]) for i in range(4)
    ] + [
        pltpu.make_async_copy(mine_send.at[4 + 4 * h + i], out_ref.at[4 + i, h], out_sem.at[4 + 4 * h + i])
        for h in range(2)
        for i in range(4)
    ]

    def keep(i, value):
        mine_send[i] = value.astype(BF)
        keeps[i].start()

    keep(0, attended)
    keep(1, grad_q)
    grad_send[0, 0] = gk_a[2 * ROWS :].astype(BF)
    grad_send[0, 1] = gv_a[2 * ROWS :].astype(BF)
    back_out = remote(grad_send.at[0], grad_buf.at[0], 16, outward)
    back_far = remote(grad_send.at[1], grad_buf.at[1], 17, beyond)

    @pl.when(has_out)
    def _():
        back_out.start()

    ret = [remote(ret_send.at[i], out_ref.at[i, c], 4 + i, partner) for i in range(4)]
    first_out[1].start()
    band_out[1].wait_recv()
    other += [pair_buf[2], pair_buf[3]]

    @pl.when(has_beyond)
    def _():
        for copy in own_halo:
            copy.wait_recv()

    attended, grad_q, gk_b, gv_b, pairs_b = band_block(
        1, other, own, "other", "own", -1, has_beyond
    )
    ret_send[0] = attended.astype(BF)
    ret_send[1] = grad_q.astype(BF)
    grad_send[1, 0] = gk_b[2 * ROWS :].astype(BF)
    grad_send[1, 1] = gv_b[2 * ROWS :].astype(BF)

    @pl.when(has_beyond)
    def _():
        back_far.start()

    ret[0].start()
    ret[1].start()
    own_gk = gk_a[:ROWS] + gk_b[ROWS : 2 * ROWS]
    own_gv = gv_a[:ROWS] + gv_b[ROWS : 2 * ROWS]
    other_gk = gk_b[:ROWS] + gk_a[ROWS : 2 * ROWS]
    other_gv = gv_b[:ROWS] + gv_a[ROWS : 2 * ROWS]

    turned = pairs_a + pairs_b
    line = lax.broadcasted_iota(jnp.int32, (D, D), 0)
    for bit in range(7):
        shift = 1 << bit
        rolled = jnp.concatenate([turned[:, shift:], turned[:, :shift]], axis=1)
        turned = jnp.where((line & shift) > 0, rolled, turned)
    sums = jnp.sum(turned, axis=0, keepdims=True)
    lane = lax.broadcasted_iota(jnp.int32, (1, D), 1)
    sums = jnp.where(lane == 0, 0.5 * sums, sums)
    sums = jnp.where(lane < BUCKETS - 1, sums, 0.0)
    sums = jnp.where(lane == BUCKETS - 1, -jnp.sum(sums, axis=1, keepdims=True), sums)
    tile_line = lax.broadcasted_iota(jnp.int32, (8, D), 0)
    bias_ctx[me] = jnp.where(tile_line == c, sums, 0.0)
    bias_out = []
    for step in range(1, ctx_count):
        copy = pltpu.make_async_remote_copy(
            src_ref=bias_ctx.at[me],
            dst_ref=bias_ctx.at[me],
            send_sem=bc_send.at[step],
            recv_sem=bc_recv.at[step],
            device_id=(row, lax.rem(me + step, ctx_count)),
            device_id_type=mesh_id,
        )
        copy.start()
        bias_out.append(copy)

    def first_group(h):
        first_out[h].wait_recv()
        k, v, q, g = [
            jnp.concatenate([local[1 + h, i], pair_buf[4 + 4 * h + i]], axis=0) for i in range(4)
        ]
        pair_scores[...] = nt(q, k)
        pair_wg[...] = nt(g, v)
        softmax_rows(
            2 * ROWS, 32, pair_scores, pair_wg, pair_w, pair_sg,
            lambda at, start, scores: scores * scale, lambda at, logit_grads: None,
        )
        keep(4 + 4 * h, nn(pair_w[:ROWS, :], v))
        keep(5 + 4 * h, nn(pair_sg[:ROWS, :], k) * scale)
        keep(6 + 4 * h, tn(pair_sg[:, :ROWS], q) * scale)
        keep(7 + 4 * h, tn(pair_w[:, :ROWS], g))

    first_group(0)

    @pl.when(has_beyond)
    def _():
        back_out.wait_recv()

    @pl.when(has_out)
    def _():
        back_far.wait_recv()

    @pl.when(jnp.logical_not(has_beyond))
    def _():
        grad_buf[0] = jnp.zeros((2, ROWS, D), BF)

    @pl.when(jnp.logical_not(has_out))
    def _():
        grad_buf[1] = jnp.zeros((2, ROWS, D), BF)

    ret_send[2] = (other_gk + grad_buf[0, 0].astype(F32)).astype(BF)
    ret_send[3] = (other_gv + grad_buf[0, 1].astype(F32)).astype(BF)
    ret[2].start()
    ret[3].start()
    keep(2, own_gk + grad_buf[1, 0].astype(F32))
    keep(3, own_gv + grad_buf[1, 1].astype(F32))

    for copy in bias_out:
        copy.wait_recv()
    total = bias_ctx[0]
    for i in range(1, ctx_count):
        total = total + bias_ctx[i]
    bias_dp[row] = total
    docs_out = []
    for step in range(1, dp_count):
        copy = pltpu.make_async_remote_copy(
            src_ref=bias_dp.at[row],
            dst_ref=bias_dp.at[row],
            send_sem=bd_send.at[step],
            recv_sem=bd_recv.at[step],
            device_id=(lax.rem(row + step, dp_count), me),
            device_id_type=mesh_id,
        )
        copy.start()
        docs_out.append(copy)

    first_group(1)

    for copy in docs_out:
        copy.wait_recv()
    total = bias_dp[0]
    for i in range(1, dp_count):
        total = total + bias_dp[i]
    bias_ref[...] = total

    for copy in ret:
        copy.wait_recv()
    for copy in keeps + smalls:
        copy.wait()

    for copy in band_out + first_out + [clause_out, second_out, third_pair] + third_out + bias_out + docs_out + ret:
        copy.wait_send()

    @pl.when(has_out)
    def _():
        for copy in own_halo + [back_out]:
            copy.wait_send()

    @pl.when(has_beyond)
    def _():
        for copy in far_halo + [back_far]:
            copy.wait_send()


def layout_kernel(heads_ref, second_ref, third_ref, tile_ref, *outs):
    outs[4][...] = tile_ref[0:2, 0:BUCKETS]
    for i, out in enumerate(outs[:4]):
        for h in range(2):
            out[:, h * D : (h + 1) * D] = heads_ref[i, h]
            out[:, (2 + h) * D : (3 + h) * D] = heads_ref[4 + i, h]
            seconds = second_ref[i, :, h * D : (h + 1) * D].astype(BF)
            spread = tn(selector(32, DILATION_SECOND, h * DILATION_SECOND // 2), seconds)
            out[:, (4 + h) * D : (5 + h) * D] = spread.astype(BF)
            thirds = third_ref[i, :, h * D : (h + 1) * D].astype(BF)
            spread = tn(selector(8, DILATION_THIRD, h * DILATION_THIRD // 2), thirds)
            out[:, (6 + h) * D : (7 + h) * D] = spread.astype(BF)


def paired(ctx_count, dp_count, query, key, value, grad_out, clause, bias_table):
    vmem = pl.BlockSpec(memory_space=pltpu.VMEM)
    far = pl.BlockSpec(memory_space=pltpu.HBM)
    dma = pltpu.SemaphoreType.DMA
    block = (ROWS, D)
    heads, second, third, bias = pl.pallas_call(
        lambda *refs: main_kernel(ctx_count, dp_count, *refs),
        out_shape=[
            jax.ShapeDtypeStruct((8, 2) + block, BF),
            jax.ShapeDtypeStruct((4, 32, 2 * D), F32),
            jax.ShapeDtypeStruct((4, 8, 2 * D), F32),
            jax.ShapeDtypeStruct((8, D), F32),
        ],
        in_specs=[far] * 6,
        out_specs=[far] * 3 + [vmem],
        scratch_shapes=[
            pltpu.VMEM((4, 32, 2 * D), F32),
            pltpu.VMEM((4, 8, 2 * D), F32),
            pltpu.SMEM((2, BUCKETS), F32),
            pltpu.VMEM((1, ROWS), jnp.int32),
            pltpu.VMEM((4, 4) + block, BF),
            pltpu.VMEM((4, ROWS, 4 * D), BF),
            pltpu.VMEM((12,) + block, BF),
            dma((22,)),
            dma((14,)),
            pltpu.VMEM((12,) + block, BF),
            pltpu.VMEM((2, 2) + block, BF),
            pltpu.VMEM((2, 1, ROWS), jnp.int32),
            pltpu.VMEM((1, ROWS), jnp.int32),
            pltpu.VMEM((2, 2) + block, BF),
            pltpu.VMEM((2, 2) + block, BF),
            pltpu.VMEM((4,) + block, BF),
            pltpu.VMEM((2, 32, 8 * D), BF),
            pltpu.VMEM((ctx_count, 16, 4 * D), BF),
            pltpu.VMEM((ctx_count, 8, D), F32),
            pltpu.VMEM((dp_count, 8, D), F32),
            pltpu.VMEM((ROWS, 3 * ROWS), F32),
            pltpu.VMEM((ROWS, 3 * ROWS), F32),
            pltpu.VMEM((ROWS, 3 * ROWS), F32),
            pltpu.VMEM((ROWS, 3 * ROWS), BF),
            pltpu.VMEM((ROWS, 3 * ROWS), BF),
            pltpu.VMEM((ROWS, 3 * ROWS), BF),
            pltpu.VMEM((ROWS, 3 * ROWS), BF),
            pltpu.VMEM((2 * ROWS, 2 * ROWS), F32),
            pltpu.VMEM((2 * ROWS, 2 * ROWS), F32),
            pltpu.VMEM((2 * ROWS, 2 * ROWS), BF),
            pltpu.VMEM((2 * ROWS, 2 * ROWS), BF),
            dma((26,)),
            dma((26,)),
            dma((ctx_count,)),
            dma((ctx_count,)),
            dma((ctx_count,)),
            dma((ctx_count,)),
            dma((dp_count,)),
            dma((dp_count,)),
        ],
        compiler_params=pltpu.CompilerParams(
            collective_id=0, has_side_effects=True, vmem_limit_bytes=64 * 1024 * 1024
        ),
        name="attend",
    )(bias_table.T, clause, query[0], key[0], value[0], grad_out[0])
    outs = pl.pallas_call(
        layout_kernel,
        out_shape=[jax.ShapeDtypeStruct((ROWS, HEADS * D), BF)] * 4
        + [jax.ShapeDtypeStruct((2, BUCKETS), F32)],
        in_specs=[vmem] * 4,
        out_specs=[vmem] * 5,
        compiler_params=pltpu.CompilerParams(vmem_limit_bytes=64 * 1024 * 1024),
        name="layout",
    )(heads, second, third, bias)
    return tuple(out[None] for out in outs[:4]) + (outs[4].T,)


def solution(mesh):
    ctx_count, dp_count = mesh.shape["ctx"], mesh.shape["dp"]
    if ctx_count != 8:
        return general(mesh)
    spec = P("dp", "ctx", None)

    def body(*arrays):
        return paired(ctx_count, dp_count, *arrays)

    return jax.shard_map(
        body,
        mesh=mesh,
        in_specs=(spec, spec, spec, spec, P("dp", "ctx"), P()),
        out_specs=(spec, spec, spec, spec, P()),
        check_vma=False,
    )
```

```python
import jax
import jax.numpy as jnp
from jax import lax
from jax.experimental import pallas as pl
from jax.experimental.pallas import tpu as pltpu
from jax.sharding import PartitionSpec as P

HEADS = 8
WINDOW = 512
BUCKETS = 32
DILATION_FIRST = 1
DILATION_SECOND = 8
DILATION_THIRD = 32


def swapped(block, axis, bit):
    count = lax.axis_size(axis)
    route = []
    for low in range(count):
        high = low | 1 << bit
        if high != low and high < count:
            route += [(low, high), (high, low)]
    return lax.ppermute(block, axis, route)


def shifted(value, axis, steps):
    count = lax.axis_size(axis)
    leading, last = (max(0, -steps), min(count, count - steps))
    return lax.ppermute(value, axis, [(source, source + steps) for source in range(leading, last)])


def with_halo(shard, sides, width):
    for axis, dim in sides:
        size, length = (lax.axis_size(axis), shard.shape[dim])
        up = [(i, (i + 1) % size) for i in range(size - 1)]
        down = [(j, i) for i, j in up]
        last = lax.slice_in_dim(shard, length - width, length, axis=dim)
        leading = lax.slice_in_dim(shard, 0, width, axis=dim)
        before = lax.ppermute(last, axis, up)
        after = lax.ppermute(leading, axis, down)
        shard = jnp.concatenate([before, shard, after], axis=dim)
    return shard


def sample_rows(matrix, initial_flag, dilation_rate):
    count = matrix.shape[0] // dilation_rate
    head_dim = matrix.shape[1] // HEADS
    grid = matrix.reshape(count, dilation_rate, HEADS, head_dim)
    return jnp.concatenate(
        [grid[:, 0, initial_flag], grid[:, dilation_rate // 2, initial_flag + 1]], axis=1
    )


def spread_rows(sampled, dilation_rate):
    count = sampled.shape[0]
    grid = jnp.zeros((count, dilation_rate) + sampled.shape[1:], sampled.dtype)
    grid = grid.at[:, 0, 0].set(sampled[:, 0]).at[:, dilation_rate // 2, 1].set(sampled[:, 1])
    return grid.reshape((count * dilation_rate,) + sampled.shape[1:])


def upper_half(bit):
    index = lax.axis_index("ctx")
    return index // 2**bit % 2 == 1


def double_rows(block, bits):
    for bit in range(bits):
        other = swapped(block, "ctx", bit)
        block = jnp.where(
            upper_half(bit),
            jnp.concatenate([other, block], axis=0),
            jnp.concatenate([block, other], axis=0),
        )
    return block


def halve_sums(block, bits):
    for bit in reversed(range(bits)):
        half = block.shape[0] // 2
        lower, higher = (block[:half], block[half:])
        upper = upper_half(bit)
        outgoing = jnp.where(upper, lower, higher)
        staying = jnp.where(upper, higher, lower)
        block = staying + swapped(outgoing.astype(jnp.bfloat16), "ctx", bit).astype(outgoing.dtype)
    return block


def span_rows(block, bits):
    return double_rows(block, bits)


def span_sums(block, bits):
    return halve_sums(block, bits)


def rows_side(score_matrix, every_key_rows, every_value_rows, gradient_list, score_scale):
    top = jnp.max(score_matrix, axis=-1, keepdims=True)
    raised = jnp.exp(score_matrix - top)
    totals = jnp.sum(raised, axis=-1, keepdims=True)
    shares = raised / totals
    softmax_weights = shares.astype(jnp.bfloat16)
    attended = jnp.einsum(
        "ezb,beo->zeo", softmax_weights, every_value_rows, preferred_element_type=jnp.float32
    )
    weight_gradient = jnp.einsum(
        "wvx,yvx->vwy", gradient_list, every_value_rows, preferred_element_type=jnp.float32
    )
    delta = jnp.sum(shares * weight_gradient, axis=-1, keepdims=True)
    logit_grads = shares * (weight_gradient - delta)
    score_gradient = logit_grads.astype(jnp.bfloat16)
    query_gradient = (
        jnp.einsum(
            "ezb,beo->zeo", score_gradient, every_key_rows, preferred_element_type=jnp.float32
        )
        * score_scale
    )
    return (
        attended,
        query_gradient,
        softmax_weights,
        score_gradient,
        logit_grads,
        top,
        totals,
        delta,
    )


def keys_side(softmax_weights, score_gradient, query_matrix, gradient_list, score_scale):
    key_gradient = (
        jnp.einsum("vjb,jvw->bvw", score_gradient, query_matrix, preferred_element_type=jnp.float32)
        * score_scale
    )
    value_gradient = jnp.einsum(
        "vjb,jvw->bvw", softmax_weights, gradient_list, preferred_element_type=jnp.float32
    )
    return (key_gradient, value_gradient)


def bucket_lookup(bucket, table):
    running = jnp.zeros((table.shape[1],) + bucket.shape, jnp.float32)
    for level in range(BUCKETS):
        running = jnp.where(bucket[None] == level, table[level][:, None, None], running)
    return running


def bucket_sums(bucket, logit_grads):
    totals = [
        jnp.sum(jnp.where(bucket[None] == level, logit_grads, 0.0), axis=(1, 2))
        for level in range(BUCKETS)
    ]
    return jnp.stack(totals, axis=0)


def pass_rim(rim, offset):
    return shifted(rim.astype(jnp.bfloat16), "ctx", offset).astype(rim.dtype)


def band_part(query_rows, key_rows, value_rows, grad_rows, clause_rows, table, score_scale):
    rows, width = query_rows.shape
    head_dim = width // HEADS
    wide = 2 * head_dim
    half = WINDOW // 2
    pair_rows = jnp.concatenate([key_rows[:, :wide], value_rows[:, :wide]], axis=1)
    extended, extended_clause = (
        with_halo(pair_rows, (("ctx", 0),), half),
        with_halo(clause_rows, (("ctx", 0),), half),
    )
    reach = rows + 2 * half
    nearby_key_rows = extended[:, :wide].reshape(reach, 2, head_dim)
    values_near = extended[:, wide:].reshape(reach, 2, head_dim)
    query_matrix = query_rows[:, :wide].reshape(rows, 2, head_dim)
    gradient_list = grad_rows[:, :wide].reshape(rows, 2, head_dim)
    start = lax.axis_index("ctx") * rows
    length = rows * lax.axis_size("ctx")
    local_query = jnp.arange(rows)[:, None]
    local_key = jnp.arange(reach)[None, :] - half
    global_key = start + local_key
    allowed = (jnp.abs(local_query - local_key) < half) & (global_key >= 0) & (global_key < length)
    bucket = jnp.minimum(jnp.abs(clause_rows[:, None] - extended_clause[None, :]), BUCKETS - 1)
    score_matrix = (
        jnp.einsum(
            "wvx,yvx->vwy", query_matrix, nearby_key_rows, preferred_element_type=jnp.float32
        )
        * score_scale
    )
    score_matrix = jnp.where(allowed[None], score_matrix + bucket_lookup(bucket, table), -jnp.inf)
    attended, query_gradient, softmax_weights, score_gradient, logit_grads, top, totals, delta = (
        rows_side(score_matrix, nearby_key_rows, values_near, gradient_list, score_scale)
    )
    key_gradient, value_gradient = keys_side(
        softmax_weights, score_gradient, query_matrix, gradient_list, score_scale
    )
    sums = jnp.concatenate(
        [key_gradient.reshape(reach, wide), value_gradient.reshape(reach, wide)], axis=1
    )
    own = sums[half : half + rows]
    from_next = pass_rim(sums[:half], -1)
    from_prev = pass_rim(sums[half + rows :], 1)
    own = own.at[rows - half :].add(from_next).at[:half].add(from_prev)
    own_key = own[:, :wide].reshape(rows, 2, head_dim)
    own_value = own[:, wide:].reshape(rows, 2, head_dim)
    return (attended, query_gradient, own_key, own_value, bucket_sums(bucket, logit_grads))


def dilated(
    query_rows, key_rows, value_rows, grad_rows, initial_flag, dilation_rate, bits, score_scale
):
    head_dim = query_rows.shape[1] // HEADS
    wide = 2 * head_dim
    picked_query = sample_rows(query_rows, initial_flag, dilation_rate)
    picked_key = sample_rows(key_rows, initial_flag, dilation_rate)
    picked_value = sample_rows(value_rows, initial_flag, dilation_rate)
    picked_grad = sample_rows(grad_rows, initial_flag, dilation_rate)
    count = picked_query.shape[0]
    gathered = span_rows(jnp.concatenate([picked_key, picked_value], axis=1), bits)
    gathered_rows = gathered.shape[0]
    every_key_rows = gathered[:, :wide].reshape(gathered_rows, 2, head_dim)
    every_value_rows = gathered[:, wide:].reshape(gathered_rows, 2, head_dim)
    query_matrix = picked_query.reshape(count, 2, head_dim)
    gradient_list = picked_grad.reshape(count, 2, head_dim)
    score_matrix = (
        jnp.einsum("wvx,yvx->vwy", query_matrix, every_key_rows, preferred_element_type=jnp.float32)
        * score_scale
    )
    attended, query_gradient, softmax_weights, score_gradient, logit_grads, top, totals, delta = (
        rows_side(score_matrix, every_key_rows, every_value_rows, gradient_list, score_scale)
    )
    key_gradient, value_gradient = keys_side(
        softmax_weights, score_gradient, query_matrix, gradient_list, score_scale
    )
    partial_sums = jnp.concatenate(
        [key_gradient.reshape(gathered_rows, wide), value_gradient.reshape(gathered_rows, wide)],
        axis=1,
    )
    own = span_sums(partial_sums, bits)
    own_key = own[:, :wide].reshape(count, 2, head_dim)
    own_value = own[:, wide:].reshape(count, 2, head_dim)
    return (
        spread_rows(attended, dilation_rate),
        spread_rows(query_gradient, dilation_rate),
        spread_rows(own_key, dilation_rate),
        spread_rows(own_value, dilation_rate),
    )


def shards(query, key, value, grad_out, clause, bias_table):
    query_rows = query[0]
    key_rows = key[0]
    value_rows = value[0]
    grad_rows = grad_out[0]
    clause_rows = clause[0]
    rows, width = query_rows.shape
    head_dim = width // HEADS
    score_scale = head_dim ** (-0.5)
    bucket_bit_count = lax.axis_size("ctx").bit_length() - 1
    band = band_part(
        query_rows, key_rows, value_rows, grad_rows, clause_rows, bias_table, score_scale
    )
    pieces = [band[:4]]
    for initial_flag, dilation_rate, bits in (
        (2, DILATION_FIRST, max(bucket_bit_count - 5, 1)),
        (4, DILATION_SECOND, bucket_bit_count - 2),
        (6, DILATION_THIRD, bucket_bit_count),
    ):
        pieces.append(
            dilated(
                query_rows,
                key_rows,
                value_rows,
                grad_rows,
                initial_flag,
                dilation_rate,
                bits,
                score_scale,
            )
        )
    bias_grad = lax.psum(band[4], ("dp", "ctx"))
    joined = [
        jnp.concatenate([piece[slot] for piece in pieces], axis=1)
        .reshape(1, rows, width)
        .astype(jnp.bfloat16)
        for slot in range(4)
    ]
    return (joined[0], joined[1], joined[2], joined[3], bias_grad)


def general(mesh):
    in_specs = (
        P("dp", "ctx", None),
        P("dp", "ctx", None),
        P("dp", "ctx", None),
        P("dp", "ctx", None),
        P("dp", "ctx"),
        P(),
    )
    out_specs = (
        P("dp", "ctx", None),
        P("dp", "ctx", None),
        P("dp", "ctx", None),
        P("dp", "ctx", None),
        P(),
    )
    return jax.shard_map(shards, mesh=mesh, in_specs=in_specs, out_specs=out_specs, check_vma=False)


ROWS = 256
D = 128
BF = jnp.bfloat16
F32 = jnp.float32


def mm(a, b, dims):
    return lax.dot_general(a, b, (dims, ((), ())), preferred_element_type=F32)


def nt(a, b):
    return mm(a, b, ((1,), (1,)))


def nn(a, b):
    return mm(a, b, ((1,), (0,)))


def tn(a, b):
    return mm(a, b, ((0,), (0,)))


def halves(x):
    high = x.astype(BF)
    return high, (x - high.astype(F32)).astype(BF)


def softmax_grads(scores, q, k, v, g, scale):
    top = jnp.max(scores, axis=-1, keepdims=True)
    raised = jnp.exp(scores - top)
    shares = raised * (1.0 / jnp.sum(raised, axis=-1, keepdims=True))
    weights = shares.astype(BF)
    attended = nn(weights, v)
    weight_grads = nt(g, v)
    delta = jnp.sum(shares * weight_grads, axis=-1, keepdims=True)
    logit_grads = shares * (weight_grads - delta)
    score_grads = logit_grads.astype(BF)
    grad_q = nn(score_grads, k) * scale
    grad_k = tn(score_grads, q) * scale
    grad_v = tn(weights, g)
    return attended, grad_q, grad_k, grad_v, logit_grads


def softmax_rows(rows, chunk, score_ref, grad_ref, weight_ref, score_grad_ref, shape_scores, take_grads):
    for start in range(0, rows, chunk):
        at = pl.ds(start, chunk)
        scores = shape_scores(at, start, score_ref[at, :])
        top = jnp.max(scores, axis=-1, keepdims=True)
        raised = jnp.exp(scores - top)
        shares = raised * (1.0 / jnp.sum(raised, axis=-1, keepdims=True))
        weight_ref[at, :] = shares.astype(BF)
        weight_grads = grad_ref[at, :]
        delta = jnp.sum(shares * weight_grads, axis=-1, keepdims=True)
        logit_grads = shares * (weight_grads - delta)
        score_grad_ref[at, :] = logit_grads.astype(BF)
        take_grads(at, logit_grads)


def selector(count, step, offset):
    row = lax.broadcasted_iota(jnp.int32, (count, ROWS), 0)
    col = lax.broadcasted_iota(jnp.int32, (count, ROWS), 1)
    return (col == row * step + offset).astype(BF)


def clause_column(row_form):
    whole = jnp.broadcast_to(row_form[...], (8, ROWS))
    index = lax.broadcasted_iota(jnp.int32, whole.shape, 0)
    parts = jnp.where(index == 0, whole >> 6, jnp.where(index == 1, whole & 63, 0))
    line = lax.broadcasted_iota(jnp.int32, (8, D), 0)
    factor = jnp.where(line == 0, 64.0, jnp.where(line == 1, 1.0, 0.0))
    column = tn(parts.astype(F32).astype(BF), factor.astype(BF))
    return column.astype(jnp.int32)


def one_hot(column):
    lane = lax.broadcasted_iota(jnp.int32, (ROWS, D), 1)
    return (lane == (column & 127)).astype(F32).astype(BF)


def main_kernel(
    ctx_count, dp_count,
    table_hbm, clause_hbm, q_ref, k_ref, v_ref, g_ref,
    out_ref, second_out_ref, third_out_ref, bias_ref,
    second_ref, third_ref, table_ref, clause_ref, local, sampled, mine_send, local_sem, out_sem,
    pair_buf, halo_buf, halo_clause, pair_clause, grad_buf, grad_send, ret_send,
    s2, s3, bias_ctx, bias_dp,
    band_scores, band_bias, band_wg, band_w, band_sg, band_high, band_low, pair_scores, pair_wg, pair_w, pair_sg,
    send_sem, recv_sem, s3_send, s3_recv, bc_send, bc_recv, bd_send, bd_recv,
):
    me = lax.axis_index("ctx")
    row = lax.axis_index("dp")
    c = lax.rem(me, 2)
    partner = me + 1 - 2 * c
    outward = me - 2 + 4 * c
    beyond = me + 2 - 4 * c
    has_out = (outward >= 0) & (outward < ctx_count)
    has_beyond = (beyond >= 0) & (beyond < ctx_count)
    scale = D**-0.5
    mesh_id = pl.DeviceIdType.MESH

    def columns(head):
        return pl.ds(pl.multiple_of(head * D, D), D)

    inputs = (k_ref, v_ref, q_ref, g_ref)
    parts = [
        [
            pltpu.make_async_copy(ref.at[:, columns(head)], local.at[j, i], local_sem.at[4 * j + i])
            for i, ref in enumerate(inputs)
        ]
        for j, head in enumerate((c, 2, 3, 1 - c))
    ]
    sample_loads = [
        pltpu.make_async_copy(ref.at[:, 4 * D :], sampled.at[i], local_sem.at[16 + i])
        for i, ref in enumerate(inputs)
    ]
    small_loads = [
        pltpu.make_async_copy(clause_hbm, clause_ref, local_sem.at[20]),
        pltpu.make_async_copy(table_hbm, table_ref, local_sem.at[21]),
    ]
    for copy in parts[3] + parts[0][:2] + sample_loads + small_loads + parts[1] + parts[2] + parts[0][2:]:
        copy.start()

    barrier = pltpu.get_barrier_semaphore()
    for step in range(1, ctx_count):
        pl.semaphore_signal(
            barrier, inc=1, device_id=(row, lax.rem(me + step, ctx_count)), device_id_type=mesh_id
        )
    for step in range(1, dp_count):
        pl.semaphore_signal(
            barrier, inc=1, device_id=(lax.rem(row + step, dp_count), me), device_id_type=mesh_id
        )
    pl.semaphore_wait(barrier, ctx_count + dp_count - 2)

    def remote(src, dst, index, target):
        return pltpu.make_async_remote_copy(
            src_ref=src,
            dst_ref=dst,
            send_sem=send_sem.at[index],
            recv_sem=recv_sem.at[index],
            device_id=(row, target),
            device_id_type=mesh_id,
        )

    band_out = [
        remote(local.at[3, pl.ds(2 * i, 2)], pair_buf.at[pl.ds(2 * i, 2)], i, partner) for i in range(2)
    ]
    first_out = [
        remote(local.at[1 + h], pair_buf.at[pl.ds(4 + 4 * h, 4)], 2 + h, partner) for h in range(2)
    ]
    clause_out = remote(clause_hbm, pair_clause, 8, partner)
    own_halo = [
        remote(local.at[0, pl.ds(0, 2)], halo_buf.at[1], 9, outward),
        remote(clause_hbm, halo_clause.at[1], 11, outward),
    ]
    far_halo = [
        remote(pair_buf.at[pl.ds(0, 2)], halo_buf.at[0], 12, beyond),
        remote(pair_clause, halo_clause.at[0], 14, beyond),
    ]

    clause_out.start()
    for copy in parts[3][:2]:
        copy.wait()
    band_out[0].start()
    for copy in parts[0][:2]:
        copy.wait()

    @pl.when(has_out)
    def _():
        for copy in own_halo:
            copy.start()

    for copy in sample_loads:
        copy.wait()
    for i, ref in enumerate((sampled.at[2], sampled.at[0], sampled.at[1], sampled.at[3])):
        for h in range(2):
            part = nn(selector(32, DILATION_SECOND, h * DILATION_SECOND // 2), ref[:, h * D : (h + 1) * D])
            s2[0, :, (2 * i + h) * D : (2 * i + h + 1) * D] = part.astype(BF)

    def thirds(refs):
        return jnp.concatenate(
            [
                nn(selector(8, DILATION_THIRD, h * DILATION_THIRD // 2), ref[:, (2 + h) * D : (3 + h) * D])
                for ref in refs
                for h in range(2)
            ],
            axis=1,
        )

    s3[0] = jnp.concatenate([thirds((sampled.at[2], sampled.at[0])), thirds((sampled.at[1], sampled.at[3]))], axis=0).astype(BF)
    second_out = remote(s2.at[0], s2.at[1], 15, partner)
    second_out.start()
    third_pair = pltpu.make_async_remote_copy(
        src_ref=s3.at[0],
        dst_ref=s3.at[1],
        send_sem=s3_send.at[0],
        recv_sem=s3_recv.at[0],
        device_id=(row, partner),
        device_id_type=mesh_id,
    )
    third_pair.start()
    for copy in parts[3][2:]:
        copy.wait()
    band_out[1].start()
    for copy in parts[1]:
        copy.wait()
    first_out[0].start()

    for copy in small_loads:
        copy.wait()
    line = lax.broadcasted_iota(jnp.int32, (D, D), 0)
    lane = lax.broadcasted_iota(jnp.int32, (D, D), 1)
    apart = jnp.abs(((lane - line + 64) & 127) - 64)
    table = jnp.zeros((D, D), F32)
    for level in range(BUCKETS):
        table = jnp.where(apart == level, table_ref[c, level], table)
    far_bias = table_ref[c, BUCKETS - 1]
    table_high, table_low = halves(table)

    clause_out.wait_recv()
    band_out[0].wait_recv()

    @pl.when(has_beyond)
    def _():
        for copy in far_halo:
            copy.start()

    @pl.when(jnp.logical_not(has_out))
    def _():
        halo_buf[0] = jnp.zeros((2, ROWS, D), BF)
        halo_clause[0] = jnp.zeros((1, ROWS), jnp.int32)

    @pl.when(jnp.logical_not(has_beyond))
    def _():
        halo_buf[1] = jnp.zeros((2, ROWS, D), BF)
        halo_clause[1] = jnp.zeros((1, ROWS), jnp.int32)

    third_pair.wait_recv()
    third_out = []
    for step in range(1, ctx_count // 2):
        copy = pltpu.make_async_remote_copy(
            src_ref=s3.at[pl.ds(0, 2)],
            dst_ref=s3.at[pl.ds(ctx_count - 2 * step, 2)],
            send_sem=s3_send.at[step],
            recv_sem=s3_recv.at[step],
            device_id=(row, lax.rem(me + 2 * step, ctx_count)),
            device_id_type=mesh_id,
        )
        copy.start()
        third_out.append(copy)

    second_out.wait_recv()
    both = jnp.concatenate([s2[0], s2[1]], axis=0)
    for h in range(2):
        q, k, v, g = [both[:, (2 * i + h) * D : (2 * i + h + 1) * D] for i in range(4)]
        results = softmax_grads(nt(q, k) * scale, q, k, v, g, scale)[:4]
        for i in range(4):
            second_ref[i, :, h * D : (h + 1) * D] = results[i][:32]

    for copy in third_out:
        copy.wait_recv()
    blocks = [s3[i].astype(F32) for i in range(ctx_count)]
    upper = jnp.concatenate([block[:8] for block in blocks], axis=0).astype(BF)
    lower = jnp.concatenate([block[8:] for block in blocks], axis=0).astype(BF)
    for h in range(2):
        q, k = [upper[:, (2 * i + h) * D : (2 * i + h + 1) * D] for i in range(2)]
        v, g = [lower[:, (2 * i + h) * D : (2 * i + h + 1) * D] for i in range(2)]
        results = softmax_grads(nt(q, k) * scale, q, k, v, g, scale)[:4]
        for i in range(4):
            third_ref[i, :, h * D : (h + 1) * D] = results[i][:8]

    smalls = [
        pltpu.make_async_copy(second_ref, second_out_ref, out_sem.at[12]),
        pltpu.make_async_copy(third_ref, third_out_ref, out_sem.at[13]),
    ]
    for copy in smalls:
        copy.start()
    for copy in parts[2] + parts[0][2:]:
        copy.wait()
    own = [local[0, i] for i in range(4)]
    other = [pair_buf[0], pair_buf[1]]
    clauses = {"own": clause_ref, "other": pair_clause}
    cols = {name: clause_column(ref) for name, ref in clauses.items()}
    hots = {name: one_hot(col) for name, col in cols.items()}
    def band_block(slot, mine, near, mine_name, near_name, sign, halo_valid):
        k = jnp.concatenate([mine[0], near[0], halo_buf[slot, 0]], axis=0)
        v = jnp.concatenate([mine[1], near[1], halo_buf[slot, 1]], axis=0)
        q, g = mine[2], mine[3]
        halo_hot = one_hot(clause_column(halo_clause.at[slot]))
        key_hot = jnp.concatenate([hots[mine_name], hots[near_name], halo_hot], axis=0)
        key_row = jnp.concatenate(
            [clauses[mine_name][0:1, :], clauses[near_name][0:1, :], halo_clause[slot, 0:1, :]],
            axis=1,
        )
        query_hot = hots[mine_name]
        spread = jnp.concatenate(
            [nn(query_hot, table_high).astype(BF), nn(query_hot, table_low).astype(BF)], axis=1
        )
        band_bias[...] = nt(spread, jnp.concatenate([key_hot, key_hot], axis=1))
        band_scores[...] = nt(q, k)
        band_wg[...] = nt(g, v)
        reach = jnp.where(halo_valid, 0, ROWS)
        col = cols[mine_name]
        turn = (1 - 2 * c) * sign
        chunk = 16

        def near_clauses(start):
            return jnp.abs(col[start : start + chunk, 0:1] - key_row) < BUCKETS - 1

        def shape_scores(at, start, scores):
            close = near_clauses(start)
            scores = scores * scale + jnp.where(close, band_bias[at, :], far_bias)
            row_index = lax.broadcasted_iota(jnp.int32, (chunk, ROWS), 0) + start
            col_index = lax.broadcasted_iota(jnp.int32, (chunk, ROWS), 1)
            signed = (row_index - col_index) * turn
            return jnp.concatenate(
                [
                    scores[:, :ROWS],
                    jnp.where(signed > 0, scores[:, ROWS : 2 * ROWS], -jnp.inf),
                    jnp.where(-signed > reach, scores[:, 2 * ROWS :], -jnp.inf),
                ],
                axis=1,
            )

        def take_grads(at, logit_grads):
            high, low = halves(jnp.where(near_clauses(at.start), logit_grads, 0.0))
            band_high[at, :] = high
            band_low[at, :] = low

        softmax_rows(ROWS, chunk, band_scores, band_wg, band_w, band_sg, shape_scores, take_grads)
        weights, score_grads = band_w[...], band_sg[...]
        attended = nn(weights, v)
        grad_q = nn(score_grads, k) * scale
        grad_k = tn(score_grads, q) * scale
        grad_v = tn(weights, g)
        by_clause = nn(band_high[...], key_hot) + nn(band_low[...], key_hot)
        high, low = halves(by_clause)
        pairs = tn(query_hot, high) + tn(query_hot, low) + tn(high, query_hot) + tn(low, query_hot)
        return attended, grad_q, grad_k, grad_v, pairs

    @pl.when(has_out)
    def _():
        for copy in far_halo:
            copy.wait_recv()

    attended, grad_q, gk_a, gv_a, pairs_a = band_block(
        0, own, other, "own", "other", 1, has_out
    )
    keeps = [
        pltpu.make_async_copy(mine_send.at[i], out_ref.at[i, c], out_sem.at[i]) for i in range(4)
    ] + [
        pltpu.make_async_copy(mine_send.at[4 + 4 * h + i], out_ref.at[4 + i, h], out_sem.at[4 + 4 * h + i])
        for h in range(2)
        for i in range(4)
    ]

    def keep(i, value):
        mine_send[i] = value.astype(BF)
        keeps[i].start()

    keep(0, attended)
    keep(1, grad_q)
    grad_send[0, 0] = gk_a[2 * ROWS :].astype(BF)
    grad_send[0, 1] = gv_a[2 * ROWS :].astype(BF)
    back_out = remote(grad_send.at[0], grad_buf.at[0], 16, outward)
    back_far = remote(grad_send.at[1], grad_buf.at[1], 17, beyond)

    @pl.when(has_out)
    def _():
        back_out.start()

    ret = [remote(ret_send.at[i], out_ref.at[i, c], 4 + i, partner) for i in range(4)]
    first_out[1].start()
    band_out[1].wait_recv()
    other += [pair_buf[2], pair_buf[3]]

    @pl.when(has_beyond)
    def _():
        for copy in own_halo:
            copy.wait_recv()

    attended, grad_q, gk_b, gv_b, pairs_b = band_block(
        1, other, own, "other", "own", -1, has_beyond
    )
    ret_send[0] = attended.astype(BF)
    ret_send[1] = grad_q.astype(BF)
    grad_send[1, 0] = gk_b[2 * ROWS :].astype(BF)
    grad_send[1, 1] = gv_b[2 * ROWS :].astype(BF)

    @pl.when(has_beyond)
    def _():
        back_far.start()

    ret[0].start()
    ret[1].start()
    own_gk = gk_a[:ROWS] + gk_b[ROWS : 2 * ROWS]
    own_gv = gv_a[:ROWS] + gv_b[ROWS : 2 * ROWS]
    other_gk = gk_b[:ROWS] + gk_a[ROWS : 2 * ROWS]
    other_gv = gv_b[:ROWS] + gv_a[ROWS : 2 * ROWS]

    turned = pairs_a + pairs_b
    line = lax.broadcasted_iota(jnp.int32, (D, D), 0)
    for bit in range(7):
        shift = 1 << bit
        rolled = jnp.concatenate([turned[:, shift:], turned[:, :shift]], axis=1)
        turned = jnp.where((line & shift) > 0, rolled, turned)
    sums = jnp.sum(turned, axis=0, keepdims=True)
    lane = lax.broadcasted_iota(jnp.int32, (1, D), 1)
    sums = jnp.where(lane == 0, 0.5 * sums, sums)
    sums = jnp.where(lane < BUCKETS - 1, sums, 0.0)
    sums = jnp.where(lane == BUCKETS - 1, -jnp.sum(sums, axis=1, keepdims=True), sums)
    tile_line = lax.broadcasted_iota(jnp.int32, (8, D), 0)
    bias_ctx[me] = jnp.where(tile_line == c, sums, 0.0)
    bias_out = []
    for step in range(1, ctx_count):
        copy = pltpu.make_async_remote_copy(
            src_ref=bias_ctx.at[me],
            dst_ref=bias_ctx.at[me],
            send_sem=bc_send.at[step],
            recv_sem=bc_recv.at[step],
            device_id=(row, lax.rem(me + step, ctx_count)),
            device_id_type=mesh_id,
        )
        copy.start()
        bias_out.append(copy)

    def first_group(h):
        first_out[h].wait_recv()
        k, v, q, g = [
            jnp.concatenate([local[1 + h, i], pair_buf[4 + 4 * h + i]], axis=0) for i in range(4)
        ]
        pair_scores[...] = nt(q, k)
        pair_wg[...] = nt(g, v)
        softmax_rows(
            2 * ROWS, 16, pair_scores, pair_wg, pair_w, pair_sg,
            lambda at, start, scores: scores * scale, lambda at, logit_grads: None,
        )
        keep(4 + 4 * h, nn(pair_w[:ROWS, :], v))
        keep(5 + 4 * h, nn(pair_sg[:ROWS, :], k) * scale)
        keep(6 + 4 * h, tn(pair_sg[:, :ROWS], q) * scale)
        keep(7 + 4 * h, tn(pair_w[:, :ROWS], g))

    first_group(0)

    @pl.when(has_beyond)
    def _():
        back_out.wait_recv()

    @pl.when(has_out)
    def _():
        back_far.wait_recv()

    @pl.when(jnp.logical_not(has_beyond))
    def _():
        grad_buf[0] = jnp.zeros((2, ROWS, D), BF)

    @pl.when(jnp.logical_not(has_out))
    def _():
        grad_buf[1] = jnp.zeros((2, ROWS, D), BF)

    ret_send[2] = (other_gk + grad_buf[0, 0].astype(F32)).astype(BF)
    ret_send[3] = (other_gv + grad_buf[0, 1].astype(F32)).astype(BF)
    ret[2].start()
    ret[3].start()
    keep(2, own_gk + grad_buf[1, 0].astype(F32))
    keep(3, own_gv + grad_buf[1, 1].astype(F32))

    for copy in bias_out:
        copy.wait_recv()
    total = bias_ctx[0]
    for i in range(1, ctx_count):
        total = total + bias_ctx[i]
    bias_dp[row] = total
    docs_out = []
    for step in range(1, dp_count):
        copy = pltpu.make_async_remote_copy(
            src_ref=bias_dp.at[row],
            dst_ref=bias_dp.at[row],
            send_sem=bd_send.at[step],
            recv_sem=bd_recv.at[step],
            device_id=(lax.rem(row + step, dp_count), me),
            device_id_type=mesh_id,
        )
        copy.start()
        docs_out.append(copy)

    first_group(1)

    for copy in docs_out:
        copy.wait_recv()
    total = bias_dp[0]
    for i in range(1, dp_count):
        total = total + bias_dp[i]
    bias_ref[...] = total

    for copy in ret:
        copy.wait_recv()
    for copy in keeps + smalls:
        copy.wait()

    for copy in band_out + first_out + [clause_out, second_out, third_pair] + third_out + bias_out + docs_out + ret:
        copy.wait_send()

    @pl.when(has_out)
    def _():
        for copy in own_halo + [back_out]:
            copy.wait_send()

    @pl.when(has_beyond)
    def _():
        for copy in far_halo + [back_far]:
            copy.wait_send()


def layout_kernel(heads_ref, second_ref, third_ref, tile_ref, *outs):
    half = ROWS // 2
    outs[4][...] = tile_ref[0:2, 0:BUCKETS]
    first_row = pl.program_id(0) * half

    def spread(ref, i, h, count, step, offset):
        row = lax.broadcasted_iota(jnp.int32, (count, half), 0)
        col = lax.broadcasted_iota(jnp.int32, (count, half), 1)
        pick = (col + offset == row * step + h * step // 2).astype(BF)
        return tn(pick, ref[i, :, h * D : (h + 1) * D].astype(BF)).astype(BF)

    for i, out in enumerate(outs[:4]):
        for h in range(2):
            out[:, h * D : (h + 1) * D] = heads_ref[i, h]
            out[:, (2 + h) * D : (3 + h) * D] = heads_ref[4 + i, h]
            out[:, (4 + h) * D : (5 + h) * D] = spread(second_ref, i, h, 16, DILATION_SECOND, 0)
            out[:, (6 + h) * D : (7 + h) * D] = spread(third_ref, i, h, 8, DILATION_THIRD, first_row)


def paired(ctx_count, dp_count, query, key, value, grad_out, clause, bias_table):
    vmem = pl.BlockSpec(memory_space=pltpu.VMEM)
    far = pl.BlockSpec(memory_space=pltpu.HBM)
    dma = pltpu.SemaphoreType.DMA
    block = (ROWS, D)
    heads, second, third, bias = pl.pallas_call(
        lambda *refs: main_kernel(ctx_count, dp_count, *refs),
        out_shape=[
            jax.ShapeDtypeStruct((8, 2) + block, BF),
            jax.ShapeDtypeStruct((4, 32, 2 * D), F32),
            jax.ShapeDtypeStruct((4, 8, 2 * D), F32),
            jax.ShapeDtypeStruct((8, D), F32),
        ],
        in_specs=[far] * 6,
        out_specs=[far] * 3 + [vmem],
        scratch_shapes=[
            pltpu.VMEM((4, 32, 2 * D), F32),
            pltpu.VMEM((4, 8, 2 * D), F32),
            pltpu.SMEM((2, BUCKETS), F32),
            pltpu.VMEM((1, ROWS), jnp.int32),
            pltpu.VMEM((4, 4) + block, BF),
            pltpu.VMEM((4, ROWS, 4 * D), BF),
            pltpu.VMEM((12,) + block, BF),
            dma((22,)),
            dma((14,)),
            pltpu.VMEM((12,) + block, BF),
            pltpu.VMEM((2, 2) + block, BF),
            pltpu.VMEM((2, 1, ROWS), jnp.int32),
            pltpu.VMEM((1, ROWS), jnp.int32),
            pltpu.VMEM((2, 2) + block, BF),
            pltpu.VMEM((2, 2) + block, BF),
            pltpu.VMEM((4,) + block, BF),
            pltpu.VMEM((2, 32, 8 * D), BF),
            pltpu.VMEM((ctx_count, 16, 4 * D), BF),
            pltpu.VMEM((ctx_count, 8, D), F32),
            pltpu.VMEM((dp_count, 8, D), F32),
            pltpu.VMEM((ROWS, 3 * ROWS), F32),
            pltpu.VMEM((ROWS, 3 * ROWS), F32),
            pltpu.VMEM((ROWS, 3 * ROWS), F32),
            pltpu.VMEM((ROWS, 3 * ROWS), BF),
            pltpu.VMEM((ROWS, 3 * ROWS), BF),
            pltpu.VMEM((ROWS, 3 * ROWS), BF),
            pltpu.VMEM((ROWS, 3 * ROWS), BF),
            pltpu.VMEM((2 * ROWS, 2 * ROWS), F32),
            pltpu.VMEM((2 * ROWS, 2 * ROWS), F32),
            pltpu.VMEM((2 * ROWS, 2 * ROWS), BF),
            pltpu.VMEM((2 * ROWS, 2 * ROWS), BF),
            dma((26,)),
            dma((26,)),
            dma((ctx_count,)),
            dma((ctx_count,)),
            dma((ctx_count,)),
            dma((ctx_count,)),
            dma((dp_count,)),
            dma((dp_count,)),
        ],
        compiler_params=pltpu.CompilerParams(
            collective_id=0, has_side_effects=True, vmem_limit_bytes=64 * 1024 * 1024
        ),
        name="attend",
    )(bias_table.T, clause, query[0], key[0], value[0], grad_out[0])
    outs = pl.pallas_call(
        layout_kernel,
        out_shape=[jax.ShapeDtypeStruct((ROWS, HEADS * D), BF)] * 4
        + [jax.ShapeDtypeStruct((2, BUCKETS), F32)],
        grid=(2,),
        in_specs=[
            pl.BlockSpec((8, 2, ROWS // 2, D), lambda i: (0, 0, i, 0)),
            pl.BlockSpec((4, 16, 2 * D), lambda i: (0, i, 0)),
            pl.BlockSpec((4, 8, 2 * D), lambda i: (0, 0, 0)),
            pl.BlockSpec((8, D), lambda i: (0, 0)),
        ],
        out_specs=[pl.BlockSpec((ROWS // 2, HEADS * D), lambda i: (i, 0))] * 4
        + [pl.BlockSpec((2, BUCKETS), lambda i: (0, 0))],
        compiler_params=pltpu.CompilerParams(vmem_limit_bytes=64 * 1024 * 1024),
        name="layout",
    )(heads, second, third, bias)
    return tuple(out[None] for out in outs[:4]) + (outs[4].T,)


def solution(mesh):
    ctx_count, dp_count = mesh.shape["ctx"], mesh.shape["dp"]
    if ctx_count != 8:
        return general(mesh)
    spec = P("dp", "ctx", None)

    def body(*arrays):
        return paired(ctx_count, dp_count, *arrays)

    return jax.shard_map(
        body,
        mesh=mesh,
        in_specs=(spec, spec, spec, spec, P("dp", "ctx"), P()),
        out_specs=(spec, spec, spec, spec, P()),
        check_vma=False,
    )
```
